32 devices in a mesh: dp: 8 (over z, x), seq: 4 (over y, core).
Axes of the slice: x: 2, y: 2, z: 4, core: 2. Of those that a mesh axis runs over, the one named last changes fastest.
Arguments:
- tokens: bfloat16 [64, 1024, 512], P('dp', 'seq'), may hold values from -6 to 6
- cotangent: bfloat16 [64, 1024, 512], P('dp', 'seq'), may hold values from -6 to 6
- masked: int32 [64, 1024], P('dp', 'seq'), may hold values from 0 to 1, as said below
- omega: float32 [64, 256], replicated, may hold values from -5 to 5
- att_weights: float32 [1050624], P(('dp', 'seq'))
- att_first: float32 [1050624], P(('dp', 'seq'))
- att_second: float32 [1050624], P(('dp', 'seq')), as said below
- ffn_in: float32 [512, 2048], P('dp', 'seq'), may hold values from -0.25 to 0.25
- ffn_out: float32 [2048, 512], P('seq', 'dp'), may hold values from -0.125 to 0.125
- ffn_in_first: float32 [512, 2048], P('dp', 'seq')
- ffn_in_second: float32 [512, 2048], P('dp', 'seq'), as said below
- ffn_out_first: float32 [2048, 512], P('seq', 'dp')
- ffn_out_second: float32 [2048, 512], P('seq', 'dp'), as said below
Outputs:
- block_out: bfloat16 [64, 1024, 512], P('dp', 'seq')
- input_grad: float32 [64, 1024, 512], P('dp', 'seq')
- att_new: float32 [1050624], P(('dp', 'seq'))
- att_first_new: float32 [1050624], P(('dp', 'seq'))
- att_second_new: float32 [1050624], P(('dp', 'seq'))
- att_copy: bfloat16 [1050624], P(('dp', 'seq'))
- ffn_in_new: float32 [512, 2048], P('dp', 'seq')
- ffn_in_first_new: float32 [512, 2048], P('dp', 'seq')
- ffn_in_second_new: float32 [512, 2048], P('dp', 'seq')
- ffn_in_copy: bfloat16 [512, 2048], P('dp', 'seq')
- ffn_out_new: float32 [2048, 512], P('seq', 'dp')
- ffn_out_first_new: float32 [2048, 512], P('seq', 'dp')
- ffn_out_second_new: float32 [2048, 512], P('seq', 'dp')
- ffn_out_copy: bfloat16 [2048, 512], P('seq', 'dp')
The draws below stay inside these ranges and needn't reach their ends.
Inputs may be any that keep to these rules, and one draw needn't show every extreme that they name: `masked`: each sequence marks a number of positions, from 51 to 256, at random places; some sequence marks exactly 256; the positions of one device are not bounded by that share. `att_second`: positive. `ffn_in_second`: positive. `ffn_out_second`: positive.
All inputs are finite; a program needn't handle non-finite values.
Results may differ from the reference program's by a relative error of at most 0.015.
Values may be sent and summed in bfloat16 or wider, within the bound.
No kernel may reach another device: no remote copies, remote signals or barrier semaphores. Data moves between devices by JAX's collectives and lax.ppermute only.
A program may use at most 320 MiB of HBM per device.

```python
import math
import jax
import jax.numpy as jnp
from jax import lax

D = 512
H = 8
DH = 64
M = 256
FF = 2048
SEQ_DP = 8
CH = 256
STEP = 10
SEQS = 64
LEN = 1024


def grad_size(base):
    return base * math.sqrt(SEQS * LEN)


def att_grad_scale():
    return jnp.concatenate([jnp.full((2 * D * D,), grad_size(0.03), jnp.float32), jnp.full((D * D,), grad_size(0.1), jnp.float32), jnp.full((D * D,), grad_size(0.15), jnp.float32), jnp.full((4 * D,), grad_size(0.3), jnp.float32)])


def spread_factor(key, shape):
    return jnp.exp(jax.random.uniform(key, shape, jnp.float32, 0.0, math.log(4.0)))


def draw_att_weights(key, part):
    key = jax.random.fold_in(key, 1)
    base_key, gain_key, offset_key = jax.random.split(key, 3)
    count = 4 * D * D
    base = jax.random.normal(base_key, (count,), jnp.float32)
    scale = jnp.concatenate([jnp.full((2 * D * D,), 0.5, jnp.float32), jnp.full((D * D,), 1.0, jnp.float32), jnp.full((D * D,), 1.5, jnp.float32)]) / math.sqrt(D)
    gains = jax.random.uniform(gain_key, (2, D), jnp.float32, 0.6, 1.4)
    offsets = 0.2 * jax.random.normal(offset_key, (2, D), jnp.float32)
    norm_part = jnp.stack([gains[0], offsets[0], gains[1], offsets[1]]).reshape(-1)
    return jnp.concatenate([base * scale, norm_part])


def draw_att_first(key, part):
    key = jax.random.fold_in(key, 2)
    return 0.11 * att_grad_scale() * jax.random.normal(key, (4 * D * D + 4 * D,), jnp.float32)


def draw_att_second(key, part):
    key = jax.random.fold_in(key, 3)
    scale = att_grad_scale()
    return 0.001 * scale * scale * spread_factor(key, (4 * D * D + 4 * D,))


def draw_ffn_in_first(key, part):
    key = jax.random.fold_in(key, 4)
    return 0.11 * grad_size(0.12) * jax.random.normal(key, (D, FF), jnp.float32)


def draw_ffn_in_second(key, part):
    key = jax.random.fold_in(key, 5)
    return 0.001 * grad_size(0.12) ** 2 * spread_factor(key, (D, FF))


def draw_ffn_out_first(key, part):
    key = jax.random.fold_in(key, 6)
    return 0.11 * grad_size(0.2) * jax.random.normal(key, (FF, D), jnp.float32)


def draw_ffn_out_second(key, part):
    key = jax.random.fold_in(key, 7)
    return 0.001 * grad_size(0.2) ** 2 * spread_factor(key, (FF, D))


def draw_masked(key, part):
    key = jax.random.fold_in(key, 9)
    count_key, place_key, chosen_key = jax.random.split(key, 3)
    counts = jax.random.randint(count_key, (SEQS,), LEN // 20, LEN // 4 + 1)
    chosen = jax.random.randint(chosen_key, (), 0, SEQS)
    counts = jnp.where(jnp.arange(SEQS) == chosen, LEN // 4, counts)
    orders = jax.vmap(lambda single: jax.random.permutation(single, LEN))(jax.random.split(place_key, SEQS))
    return (orders < counts[:, None]).astype(jnp.int32)


def steps_of(own_key, extent, pieces, smallest, top_value):
    loudness = 1.0
    for axis_at, blocks in pieces:
        steps = jax.random.uniform(jax.random.fold_in(jax.random.fold_in(own_key, 6), axis_at), (blocks,), jnp.float32, smallest / len(pieces), top_value / len(pieces))
        loudness = loudness * jnp.repeat(jnp.exp(steps), extent[axis_at] // blocks).reshape((-1,) + (1,) * (len(extent) - 1 - axis_at))
    return loudness


def bell_draw(key, extent, deviation, bound, cuts=(), kind=jnp.bfloat16):
    entries = jax.random.normal(key, extent, jnp.float32) * deviation
    if len(cuts) > 0:
        entries = steps_of(key, extent, cuts, -0.22, 0.18) * entries
    return jnp.clip(entries, min=-bound, max=bound).astype(kind)


def setup_inputs(seed: int = 0) -> dict:
    arg_keys = jax.random.split(jax.random.key(seed), 14)
    tokens = bell_draw(arg_keys[0], (SEQS, LEN, D), 1.0, 6.0, ((0, 8), (1, 4)))
    cotangent = bell_draw(arg_keys[1], (SEQS, LEN, D), 1.0, 6.0, ((0, 8), (1, 4)))
    masked = draw_masked(jax.random.fold_in(arg_keys[13], 71), 0)
    omega = bell_draw(arg_keys[3], (DH, M), 1.0, 5.0, (), jnp.float32)
    att_weights = draw_att_weights(jax.random.fold_in(arg_keys[13], 71), 0)
    att_first = draw_att_first(jax.random.fold_in(arg_keys[13], 71), 0)
    att_second = draw_att_second(jax.random.fold_in(arg_keys[13], 71), 0)
    ffn_in = bell_draw(arg_keys[7], (D, FF), D ** -0.5, 0.25, ((0, 8), (1, 4)), jnp.float32)
    ffn_out = bell_draw(arg_keys[8], (FF, D), FF ** -0.5, 0.125, ((0, 4), (1, 8)), jnp.float32)
    ffn_in_first = draw_ffn_in_first(jax.random.fold_in(arg_keys[13], 71), 0)
    ffn_in_second = draw_ffn_in_second(jax.random.fold_in(arg_keys[13], 71), 0)
    ffn_out_first = draw_ffn_out_first(jax.random.fold_in(arg_keys[13], 71), 0)
    ffn_out_second = draw_ffn_out_second(jax.random.fold_in(arg_keys[13], 71), 0)
    return dict(tokens=tokens, cotangent=cotangent, masked=masked, omega=omega, att_weights=att_weights, att_first=att_first, att_second=att_second, ffn_in=ffn_in, ffn_out=ffn_out, ffn_in_first=ffn_in_first, ffn_in_second=ffn_in_second, ffn_out_first=ffn_out_first, ffn_out_second=ffn_out_second)


PRECISE = lax.Precision.HIGHEST
BETA_FIRST = 0.9
BETA_SECOND = 0.999
ADAM_EPS = 1e-08
WEIGHT_DECAY = 0.1
RATE_MATRIX = 0.02
RATE_NORM = 0.3
NORM_EPS = 1e-05

@jax.custom_vjp
def low(v):
    return lax.optimization_barrier(v.astype(jnp.bfloat16)).astype(jnp.float32)

@jax.custom_vjp
def low_back(v):
    return v

def low_keep(v):
    return (low(v), None)

def low_pass(kept, grad):
    return (grad,)

def back_keep(v):
    return (v, None)

def back_low(kept, grad):
    return (low(grad),)
low.defvjp(low_keep, low_pass)
low_back.defvjp(back_keep, back_low)

def matmul(left, right):
    return jnp.einsum('gld,de->gle', left, right, precision=PRECISE)

def norm_rows(inputs, gain, offset):
    centre = inputs - lax.optimization_barrier(jnp.mean(inputs, axis=-1, keepdims=True))
    spread = lax.optimization_barrier(jnp.mean(centre * centre, axis=-1, keepdims=True))
    return centre * lax.rsqrt(spread + NORM_EPS) * gain + offset

def feature_map(inputs, omega):
    scaled = inputs * DH ** (-0.25)
    projected = jnp.einsum('...e,em->...m', scaled, omega, precision=PRECISE)
    return jnp.exp(projected - 0.5 * lax.optimization_barrier(jnp.sum(scaled * scaled, axis=-1, keepdims=True))) * M ** (-0.5)

def attend(queries, key_rows, values, omega):
    groups, length, head_count, head_size = queries.shape
    span_count = length // CH
    values = low(values)

    def blocks(source):
        return jnp.moveaxis(source.reshape(groups, span_count, CH, head_count, head_size), 1, 0)
    lower = jnp.arange(CH)[:, None] >= jnp.arange(CH)[None, :]

    def span_step(carry, piece):
        state, total = carry
        query_block, key_block, value_block = piece
        query_feat = low(feature_map(query_block, omega))
        key_feat = low(feature_map(key_block, omega))
        scores = low(jnp.where(lower, jnp.einsum('gihm,gjhm->ghij', query_feat, key_feat, precision=PRECISE), 0.0))
        state_low = low(state)
        numerator = jnp.einsum('ghij,gjhe->gihe', scores, value_block, precision=PRECISE)
        numerator = numerator + jnp.einsum('gihm,ghme->gihe', query_feat, state_low, precision=PRECISE)
        denominator = jnp.einsum('ghij->gih', scores) + jnp.einsum('gihm,ghm->gih', query_feat, total, precision=PRECISE)
        state = state + jnp.einsum('gjhm,gjhe->ghme', key_feat, value_block, precision=PRECISE)
        total = total + lax.optimization_barrier(jnp.sum(key_feat, axis=1))
        return ((state, total), numerator / denominator[..., None])
    start = (jnp.zeros((groups, head_count, M, head_size), jnp.float32), jnp.zeros((groups, head_count, M), jnp.float32))
    _, outputs = lax.scan(jax.checkpoint(span_step), start, (blocks(queries), blocks(key_rows), blocks(values)))
    return jnp.moveaxis(outputs, 0, 1).reshape(groups, length, head_count, head_size)

def block_layer(inputs, att_weights, ffn_in, ffn_out, omega):
    groups = inputs.shape[0]
    square = D * D
    matrices = low(att_weights[:4 * square].reshape(4, D, D))
    norm_params = low(att_weights[4 * square:].reshape(4, D))
    first_weight = low(ffn_in)
    second_weight = low(ffn_out)
    normed = low(norm_rows(inputs, norm_params[0], norm_params[1]))
    head_shape = (groups, LEN, H, DH)
    queries = low_back(matmul(normed, matrices[0])).reshape(head_shape)
    key_rows = low_back(matmul(normed, matrices[1])).reshape(head_shape)
    values = low_back(matmul(normed, matrices[2])).reshape(head_shape)
    mixed = attend(queries, key_rows, values, omega).reshape(groups, LEN, D)
    middle = inputs + low_back(matmul(low(mixed), matrices[3]))
    normed_two = low(norm_rows(middle, norm_params[2], norm_params[3]))
    hidden = low_back(matmul(normed_two, first_weight))
    active = low(jax.nn.gelu(hidden))
    return middle + matmul(active, second_weight)

def adamw(weight, first, second, grad, rate, decay):
    first_new = BETA_FIRST * first + (1.0 - BETA_FIRST) * grad
    second_new = BETA_SECOND * second + (1.0 - BETA_SECOND) * grad * grad
    first_hat = first_new / (1.0 - BETA_FIRST ** STEP)
    second_hat = second_new / (1.0 - BETA_SECOND ** STEP)
    weight_new = weight - rate * (first_hat / (jnp.sqrt(second_hat) + ADAM_EPS) + decay * weight)
    return (weight_new, first_new, second_new)

def reference(tokens, cotangent, masked, omega, att_weights, att_first, att_second, ffn_in, ffn_out, ffn_in_first, ffn_in_second, ffn_out_first, ffn_out_second):
    group_count = SEQS // SEQ_DP
    inputs = tokens.astype(jnp.float32).reshape(group_count, SEQ_DP, LEN, D)
    weighting = cotangent.astype(jnp.float32) * masked.astype(jnp.float32)[:, :, None]
    weighting = weighting.reshape(group_count, SEQ_DP, LEN, D)

    def forward(tok_in, att_in, first_in, second_in):
        return block_layer(tok_in, att_in, first_in, second_in, omega)

    def group_step(running, group_in):
        group_tokens, group_grad = group_in
        result, pullback = jax.vjp(forward, group_tokens, att_weights, ffn_in, ffn_out)
        grad_tok, grad_att, grad_first, grad_second = pullback(group_grad)
        running = (running[0] + grad_att, running[1] + grad_first, running[2] + grad_second)
        return (running, (result, grad_tok))
    start = (jnp.zeros_like(att_weights), jnp.zeros_like(ffn_in), jnp.zeros_like(ffn_out))
    (att_grad, first_grad, second_grad), (results, tok_grads) = lax.scan(group_step, start, (inputs, weighting))
    block_out = results.reshape(SEQS, LEN, D).astype(jnp.bfloat16)
    input_grad = tok_grads.reshape(SEQS, LEN, D)
    position = jnp.arange(att_weights.shape[0], dtype=jnp.int32)
    is_matrix = position < 4 * D * D
    rate = jnp.where(is_matrix, RATE_MATRIX, RATE_NORM)
    decay = jnp.where(is_matrix, WEIGHT_DECAY, 0.0)
    att_new, att_first_new, att_second_new = adamw(att_weights, att_first, att_second, att_grad, rate, decay)
    ffn_in_new, ffn_in_first_new, ffn_in_second_new = adamw(ffn_in, ffn_in_first, ffn_in_second, first_grad, RATE_MATRIX, WEIGHT_DECAY)
    ffn_out_new, ffn_out_first_new, ffn_out_second_new = adamw(ffn_out, ffn_out_first, ffn_out_second, second_grad, RATE_MATRIX, WEIGHT_DECAY)
    return (block_out, input_grad, att_new, att_first_new, att_second_new, att_new.astype(jnp.bfloat16), ffn_in_new, ffn_in_first_new, ffn_in_second_new, ffn_in_new.astype(jnp.bfloat16), ffn_out_new, ffn_out_first_new, ffn_out_second_new, ffn_out_new.astype(jnp.bfloat16))
```

```python
import functools
import math

import jax
import jax.numpy as jnp
from jax import lax
from jax.experimental import pallas as pl
from jax.experimental.pallas import tpu as pltpu
from jax.sharding import PartitionSpec as P

CH = 256
STEP = 10
BETA_FIRST = 0.9
BETA_SECOND = 0.999
ADAM_EPS = 1e-08
WEIGHT_DECAY = 0.1
RATE_MATRIX = 0.02
RATE_NORM = 0.3
NORM_EPS = 1e-05
SPARE = 16
VMEM_LIMIT = 16 * 1024 * 1024
BIG = 1 << 20
LIMITS = {'keys': 14, 'queries': 16, 'mix': 12, 'ffn': 40, 'outer': 14, 'back_query': 24, 'back_key': 34}
F32 = jnp.float32
LOW = jnp.bfloat16


def dot_nn(left, right):
    return lax.dot_general(left, right, (((1,), (0,)), ((), ())), preferred_element_type=F32)


def dot_nt(left, right):
    return lax.dot_general(left, right, (((1,), (1,)), ((), ())), preferred_element_type=F32)


def dot_tn(left, right):
    return lax.dot_general(left, right, (((0,), (0,)), ((), ())), preferred_element_type=F32)


def norm_parts(inputs):
    centre = inputs - jnp.mean(inputs, axis=-1, keepdims=True)
    root = lax.rsqrt(jnp.mean(centre * centre, axis=-1, keepdims=True) + NORM_EPS)
    return centre * root, root


def norm_back(grad, gain, unit, root):
    inner = grad * gain
    mean_inner = jnp.mean(inner, axis=-1, keepdims=True)
    return root * (inner - mean_inner - unit * jnp.mean(inner * unit, axis=-1, keepdims=True))


def causal(length):
    earlier = lax.broadcasted_iota(jnp.int32, (length, length), 0)
    return earlier <= lax.broadcasted_iota(jnp.int32, (length, length), 1)


def put_states(own_out, their_out, core, heads, size, states, copies):
    half = heads // 2
    base = half * size
    first = core[0] == 0
    own_out[0, base:] = jnp.zeros((SPARE, own_out.shape[2]), LOW)
    their_out[0, base:] = jnp.zeros((SPARE, own_out.shape[2]), LOW)
    for index in range(half):
        low, high = states[index], states[index + half]
        total_low, total_high = [
            sum(s[size + i : size + i + 1] for i in range(copies)) for s in (low, high)
        ]
        at = slice(index * size, (index + 1) * size)
        own_out[0, at] = jnp.where(first, low[:size], high[:size]).astype(LOW)
        their_out[0, at] = jnp.where(first, high[:size], low[:size]).astype(LOW)
        row = slice(base + index, base + index + 1)
        own_out[0, row] = jnp.where(first, total_low, total_high).astype(LOW)
        their_out[0, row] = jnp.where(first, total_high, total_low).astype(LOW)


def get_state(core, keep, come, head, heads, size, copies):
    part, index = divmod(head, heads // 2)
    base = heads // 2 * size
    own = core[0] == part
    total = jnp.where(own, keep[0, base : base + SPARE], come[0, base : base + SPARE]).astype(F32)[index : index + 1]
    line = lax.broadcasted_iota(jnp.int32, (SPARE, total.shape[1]), 0)
    spare = jnp.where(line < copies, total, 0.0).astype(LOW)
    rows = slice(index * size, (index + 1) * size)
    return jnp.concatenate([jnp.where(own, keep[0, rows], come[0, rows]), spare], axis=0)


def split_features(rows, scale, shift, high_out, stack, half):
    size = rows.shape[0]
    scaled = rows * scale
    high = scaled.astype(LOW)
    rest = (scaled - high.astype(F32)).astype(LOW)
    high_out[...] = high
    for part, piece in enumerate((high, high, rest, rest)):
        stack[part * size : (part + 1) * size] = piece
    half[...] = 0.5 * jnp.sum(scaled * scaled, axis=0, keepdims=True) + shift


def staged(count, *stages):
    for stage in stages:
        for item in range(count):
            stage(item)


def keys_kernel(
    heads,
    size,
    tok,
    norms,
    weights,
    omega,
    core,
    turned_out,
    uk_out,
    value_out,
    pk_out,
    own_out,
    their_out,
    rows,
    stacks,
    halves,
    states,
):
    width = heads * size
    length = tok.shape[1]
    unit, _ = norm_parts(tok[0].astype(F32))
    turned_out[0] = (unit * norms[0:1] + norms[1:2]).astype(LOW).T
    rows[...] = dot_nn(weights[width:], turned_out[0])
    spare = (lax.broadcasted_iota(jnp.int32, (SPARE, length), 0) < 2).astype(F32).astype(LOW)
    shift = 0.5 * math.log(omega.shape[0])

    def split(head):
        at = slice(head * size, (head + 1) * size)
        split_features(
            rows[at], size ** (-0.25), shift, uk_out.at[0, at], stacks.at[head], halves.at[head : head + 1]
        )
        value_out[0, head, :size] = rows[width + head * size : width + (head + 1) * size].astype(LOW)
        value_out[0, head, size:] = spare

    def feature(head):
        projected = dot_nn(omega[...], stacks[head])
        pk_out[0, head] = jnp.exp(projected - halves[head : head + 1]).astype(LOW)

    def local_state(head):
        states[head] = dot_nt(value_out[0, head], pk_out[0, head])

    staged(heads, split, feature, local_state)
    put_states(own_out, their_out, core, heads, size, states, 1)


def queries_kernel(heads, size, turned, weights, omega, value, pk, uq_out, pq_out, score_out, num_out, rows, stacks, halves):
    width = heads * size
    length = turned.shape[2]
    rows[...] = dot_nn(weights[:width], turned[0])
    shift = 0.5 * math.log(omega.shape[0])
    keep = causal(length)

    def split(head):
        at = slice(head * size, (head + 1) * size)
        split_features(
            rows[at], size ** (-0.25), shift, uq_out.at[0, at], stacks.at[head], halves.at[head : head + 1]
        )

    def feature(head):
        projected = dot_nn(omega[...], stacks[head])
        pq_out[0, head] = jnp.exp(projected - halves[head : head + 1]).astype(LOW)

    def score(head):
        score_out[0, head] = jnp.where(keep, dot_tn(pk[0, head], pq_out[0, head]), 0.0).astype(LOW)

    def numerator(head):
        num_out[0, head] = dot_nn(value[0, head], score_out[0, head])

    staged(heads, split, feature, score, numerator)


def mix_kernel(heads, size, tok, norms, out_weight, num, core, keep, come, pq, mixed_out, recip_out, middle_out, normed_out):
    state = (core, keep, come)
    for head in range(heads):
        at = head * size
        total = num[0, head] + dot_nn(get_state(*state, head, heads, size, 2), pq[0, head])
        recip = 1.0 / total[size : size + 1]
        mixed_out[0, at : at + size] = (total[:size] * recip).astype(LOW)
        recip_out[0, head : head + 1] = recip
    mixed = mixed_out[0]
    middle = tok[0].astype(F32) + dot_tn(mixed, out_weight[...])
    middle_out[0] = middle
    unit, _ = norm_parts(middle)
    normed_out[0] = (unit * norms[2:3] + norms[3:4]).astype(LOW)


def gelu_pair(hidden):
    slope = math.sqrt(2.0 / math.pi)
    square = hidden * hidden
    tanh = jnp.tanh(hidden * (slope + (slope * 0.044715) * square))
    upper = 0.5 + 0.5 * tanh
    inner = (0.5 * slope) + (1.5 * slope * 0.044715) * square
    return hidden * upper, upper + hidden * (1.0 - tanh * tanh) * inner


def ffn_kernel(
    groups, normed, middle, target, norms, pair, core, out, grad_out, leave, stay, norm_grad, first_sum, second_sum
):
    step = pl.program_id(0)
    half = pair.shape[2] // 2
    own = normed[...]
    grads = target[...]
    own_turned = own.T
    grads_turned = grads.T

    @pl.when(step == 0)
    def _():
        first_sum[...] = jnp.zeros_like(first_sum)
        second_sum[...] = jnp.zeros_like(second_sum)
        norm_grad[...] = jnp.zeros_like(norm_grad)

    result = jnp.zeros(own.shape, F32)
    grad_normed = jnp.zeros(own.shape, F32)
    for group in range(groups):
        first = pair[group, :, :half]
        second = pair[group, :, half:]
        active, slope = gelu_pair(dot_nn(own, first))
        active = active.astype(LOW)
        result = result + dot_nt(active, second)
        grad_hidden = (dot_nn(grads, second) * slope).astype(LOW)
        grad_normed = grad_normed + dot_nt(grad_hidden, first)
        first_sum[group] += dot_nn(own_turned, grad_hidden)
        second_sum[group] += dot_nn(grads_turned, active)
    rows = middle[...]
    out[...] = (rows + result).astype(LOW)
    unit, root = norm_parts(rows)
    grad_out[...] = grads.astype(F32) + norm_back(grad_normed, norms[2:3], unit, root)
    norm_grad[0:1] += jnp.sum(grad_normed * unit, axis=0, keepdims=True)
    norm_grad[1:2] += jnp.sum(grad_normed, axis=0, keepdims=True)

    @pl.when(step == pl.num_programs(0) - 1)
    def _():
        mine = core[0]
        for chip in range(groups // 2):
            at = 2 * half * chip
            for side, target_ref in ((mine, stay), (1 - mine, leave)):
                target_ref[:, at : at + half] = first_sum[2 * chip + side].astype(LOW)
                target_ref[:, at + half : at + 2 * half] = second_sum[2 * chip + side].astype(LOW)


def through_omega(flow, scaled, omega_low, size):
    back = dot_nn(omega_low, flow)
    return ((back[:size] - scaled.astype(F32) * back[size : size + 1]) * size ** (-0.25))


def outer_kernel(
    heads, size, grad_middle, out_weight, mixed, recip, pq, core, outer_out, own_out, their_out, out_proj, grad_mixed, states
):
    length = grad_middle.shape[1]

    @pl.when(pl.program_id(0) == 0)
    def _():
        out_proj[...] = jnp.zeros_like(out_proj)

    grad_low = grad_middle[0].astype(LOW)
    grad_mixed[...] = dot_nt(out_weight[...], grad_low)
    out_proj[...] += dot_nn(mixed[0], grad_low)
    line = lax.broadcasted_iota(jnp.int32, (SPARE, length), 0)

    def scale(head):
        at = head * size
        outer = grad_mixed[at : at + size] * recip[0, head : head + 1]
        centre = -jnp.sum(outer * mixed[0, at : at + size].astype(F32), axis=0, keepdims=True)
        rest = centre - centre.astype(LOW).astype(F32)
        outer_out[0, head, :size] = outer.astype(LOW)
        outer_out[0, head, size:] = jnp.where(line == 0, centre, jnp.where(line == 1, rest, 0.0)).astype(LOW)

    def local_state(head):
        states[head] = dot_nt(outer_out[0, head], pq[0, head])

    staged(heads, scale, local_state)
    put_states(own_out, their_out, core, heads, size, states, 2)


def back_query_kernel(
    heads,
    size,
    turned,
    omega_low,
    outers,
    value,
    pq,
    pk,
    scores,
    core,
    keep_state,
    come_state,
    uq,
    uk,
    query_out,
    key_out,
    value_out,
    query_weight,
    befores,
    grad_scores,
    flows,
    key_flows,
):
    @pl.when(pl.program_id(0) == 0)
    def _():
        query_weight[...] = jnp.zeros_like(query_weight)

    keep = causal(turned.shape[2])

    def score(head):
        befores[head] = get_state(core, keep_state, come_state, head, heads, size, 2)
        grad_scores[head] = jnp.where(keep, dot_tn(value[0, head], outers[0, head]), 0.0).astype(LOW)

    def feature(head):
        at = head * size
        grad_feat = dot_nn(pk[0, head], grad_scores[head]) + dot_tn(befores[head], outers[0, head])
        flows[head] = (grad_feat * pq[0, head].astype(F32)).astype(LOW)
        grad_key_feat = dot_nt(pq[0, head], grad_scores[head])
        key_flows[head] = (grad_key_feat * pk[0, head].astype(F32)).astype(LOW)
        value_out[0, at : at + size] = dot_nt(outers[0, head], scores[0, head])[:size].astype(LOW)

    def query(head):
        at = head * size
        query_out[0, at : at + size] = through_omega(flows[head], uq[0, at : at + size], omega_low[...], size).astype(
            LOW
        )
        key_out[0, at : at + size] = through_omega(key_flows[head], uk[0, at : at + size], omega_low[...], size).astype(LOW)

    staged(heads, score, feature, query)
    query_weight[...] += dot_nt(turned[0], query_out[0])


def back_key_kernel(
    heads,
    size,
    layout,
    tok,
    norms,
    grad_middle,
    weights,
    omega_low,
    value,
    pk,
    core,
    keep_state,
    come_state,
    uk,
    query_grad,
    key_part,
    value_part,
    query_weight,
    out_proj,
    norm_two,
    turned,
    input_grad,
    leave,
    stay,
    flat,
    laters,
    flows,
    pair_weight,
    norm_grad,
    whole,
):
    width = heads * size

    @pl.when(pl.program_id(0) == 0)
    def _():
        pair_weight[...] = jnp.zeros_like(pair_weight)
        norm_grad[...] = jnp.zeros_like(norm_grad)

    unit, root = norm_parts(tok[0].astype(F32))
    flat[:width] = query_grad[0]

    def later(head):
        laters[head] = get_state(core, keep_state, come_state, head, heads, size, 1)

    def feature(head):
        at = 2 * width + head * size
        grad_feat = dot_tn(laters[head], value[0, head])
        flows[head] = (grad_feat * pk[0, head].astype(F32)).astype(LOW)
        extra = dot_nn(laters[head], pk[0, head])[:size]
        flat[at : at + size] = (
            value_part[0, head * size : (head + 1) * size].astype(F32) + extra
        ).astype(LOW)

    def key(head):
        at = width + head * size
        part = slice(head * size, (head + 1) * size)
        total = key_part[0, part].astype(F32) + through_omega(flows[head], uk[0, part], omega_low[...], size)
        flat[at : at + size] = total.astype(LOW)

    staged(heads, later, feature, key)
    pair_weight[...] += dot_nt(turned[0], flat[width:])
    grad_normed = dot_tn(flat[...], weights[...])
    input_grad[0] = grad_middle[0] + norm_back(grad_normed, norms[0:1], unit, root)
    norm_grad[0:1] += jnp.sum(grad_normed * unit, axis=0, keepdims=True)
    norm_grad[1:2] += jnp.sum(grad_normed, axis=0, keepdims=True)

    @pl.when(pl.program_id(0) == pl.num_programs(0) - 1)
    def _():
        whole[:width] = query_weight[...]
        whole[width : 2 * width] = pair_weight[:, :width]
        whole[2 * width : 3 * width] = pair_weight[:, width:]
        whole[3 * width : 4 * width] = out_proj[...]
        whole[4 * width : 4 * width + 2] = norm_grad[...]
        whole[4 * width + 2 : 4 * width + 4] = norm_two[...]
        starts, rows, owners = layout
        half = width // 2
        first = core[0] == 0
        leave[...] = jnp.zeros_like(leave)
        stay[...] = jnp.zeros_like(stay)
        for part in range(2):
            count = leave.shape[1]
            columns = slice(part * half, (part + 1) * half)
            for spot in range(count):
                low = starts[owners[part][spot]]
                high = starts[owners[part][spot + count]]
                low = whole[low : low + rows, columns]
                high = whole[high : high + rows, columns]
                stay[part, spot, :rows] = jnp.where(first, low, high)
                leave[part, spot, :rows] = jnp.where(first, high, low).astype(LOW)


def per_seq(shape, offset=0):
    rest = tuple(shape[1:])
    return pl.BlockSpec((1,) + rest, lambda i: (i + offset,) + (0,) * len(rest))


def fixed(shape):
    return pl.BlockSpec(tuple(shape), lambda i: (0,) * len(shape))


def call(kernel, steps, args, in_specs, outs, out_specs, name, flops, scratch=(), aliases=None, after=(), chip=None):
    if chip is not None:
        args = tuple(
            on_chip(a) if i in chip else off_chip(a) if math.prod(a.shape) >= BIG else a for i, a in enumerate(args)
        )
    if after:
        count, body = len(args), kernel
        args = tuple(args) + tuple(after)
        in_specs = list(in_specs) + [pl.BlockSpec(memory_space=pl.ANY)] * len(after)

        def kernel(*refs):
            body(*refs[:count], *refs[count + len(after) :])

    moved = sum(math.prod(a.shape) * jnp.dtype(a.dtype).itemsize for a in list(args) + list(outs))
    return pl.pallas_call(
        kernel,
        grid=(steps,),
        in_specs=in_specs,
        out_specs=out_specs,
        out_shape=outs,
        scratch_shapes=list(scratch),
        name=name,
        input_output_aliases=aliases or {},
        compiler_params=pltpu.CompilerParams(
            dimension_semantics=("arbitrary",), vmem_limit_bytes=LIMITS[name] * 1024 * 1024
        ),
        cost_estimate=pl.CostEstimate(
            flops=flops, bytes_accessed=moved if flops > 1 else 1, transcendentals=0
        ),
    )(*args)


def on_chip(value):
    return pltpu.with_memory_space_constraint(value, pltpu.VMEM)


def off_chip(value):
    return pltpu.with_memory_space_constraint(value, pltpu.HBM)


def array(shape, dtype):
    return pltpu.HBM(tuple(shape), dtype)


def flip(value, axis, bit):
    return lax.ppermute(value, axis, [(i, i ^ (1 << bit)) for i in range(lax.axis_size(axis))])


def bit_of(axis, bit):
    return (lax.axis_index(axis) >> bit) & 1


def send_half(own, their, forward):
    count = lax.axis_size("seq")
    beside = flip(their, "seq", 0)
    mine = (own.astype(F32) + beside.astype(F32)).astype(LOW)
    far = None
    for step in range(1, count // 2):
        hop = 2 * step if forward else -2 * step
        pairs = [(i, i + hop) for i in range(count) if 0 <= i + hop < count]
        come = lax.ppermute(mine, "seq", pairs)
        far = come if far is None else far + come
    return beside, far, mine


def receive_half(own, beside, far, forward):
    core = bit_of("seq", 0)
    giver = (core == 0) if forward else (core == 1)
    give = (far.astype(F32) + jnp.where(giver, own.astype(F32), 0.0)).astype(LOW)
    keep = (far.astype(F32) + jnp.where(giver, 0.0, beside.astype(F32))).astype(LOW)
    return keep, flip(give, "seq", 0)


def axis_bits(axis):
    return lax.axis_size(axis).bit_length() - 1


def gather_orders():
    high = [("dp", bit) for bit in range(1, axis_bits("dp"))]
    seq_high = [("seq", bit) for bit in range(1, axis_bits("seq"))]
    near = [("dp", 0)]
    return [high + near + seq_high + [("seq", 0)], seq_high + high + near + [("seq", 0)]]


def scatter_orders():
    high = [("dp", bit) for bit in range(axis_bits("dp") - 1, 0, -1)]
    seq_high = [("seq", bit) for bit in range(axis_bits("seq") - 1, 0, -1)]
    near = [("dp", 0)]
    return [[("seq", 0)] + seq_high + near + high, [("seq", 0)] + near + high + seq_high]


def place_in(order, index):
    seq_bits = axis_bits("seq")
    spot = 0
    for axis, bit in order:
        shift = bit if axis == "seq" else bit + seq_bits
        spot = 2 * spot + ((index >> shift) & 1)
    return spot


def gather_doubling(value, order, early):
    value = value[None]
    for axis, bit in order:
        come = flip(value, axis, bit)
        early.append(come)
        low = bit_of(axis, bit) == 0
        value = jnp.concatenate([jnp.where(low, value, come), jnp.where(low, come, value)], axis=0)
    return value


def total_of(terms):
    return sum(term.astype(F32) for term in terms)


def scatter_step(terms, axis, bit, leave=None):
    mine = bit_of(axis, bit)
    if leave is None:
        leave = total_of([lax.dynamic_index_in_dim(term, 1 - mine, 0, keepdims=False) for term in terms]).astype(LOW)
    come = flip(leave, axis, bit)
    stay = total_of([lax.dynamic_index_in_dim(term, mine, 0, keepdims=False) for term in terms])
    return [stay, come]


def split_rows(terms, axis, bits, low):
    ways = 1 << len(bits)
    terms = [t.reshape(-1, ways, low, t.shape[1]) for t in terms]
    shift = min(bits)
    mine = (lax.axis_index(axis) >> shift) & (ways - 1)

    def part(which):
        total = total_of([lax.dynamic_index_in_dim(t, which, 1, keepdims=False) for t in terms]).astype(LOW)
        return total.reshape(-1, total.shape[-1])

    leaving = [part(mine ^ other) for other in range(1, ways)]
    size = lax.axis_size(axis)
    come = [
        lax.ppermute(leave, axis, [(i, i ^ (other << shift)) for i in range(size)])
        for other, leave in enumerate(leaving, 1)
    ]
    return leaving, [part(mine)] + come


def scatter_halving(terms, order):
    for axis, bit in order:
        terms = scatter_step([t.reshape((2, t.shape[0] // 2) + t.shape[1:]) for t in terms], axis, bit)
    return total_of(terms)[0]


def adamw(weight, first, second, grad, rate, decay):
    first_new = BETA_FIRST * first + (1.0 - BETA_FIRST) * grad
    second_new = BETA_SECOND * second + (1.0 - BETA_SECOND) * grad * grad
    first_hat = first_new / (1.0 - BETA_FIRST**STEP)
    second_hat = second_new / (1.0 - BETA_SECOND**STEP)
    weight_new = weight - rate * (first_hat / (jnp.sqrt(second_hat) + ADAM_EPS) + decay * weight)
    return (weight_new, first_new, second_new)


def unpack_kernel(starts, spots, rows, left, right, wide_out, out_weight, norms, whole):
    whole[...] = jnp.zeros_like(whole)
    half = left.shape[2]
    for index, start in enumerate(starts):
        whole[start : start + rows, :half] += left[spots[0][index], :rows].astype(F32)
        whole[start : start + rows, half:] += right[spots[1][index], :rows].astype(F32)
    width = out_weight.shape[0]
    for part in range(3):
        wide_out[part * width : (part + 1) * width] = whole[part * width : (part + 1) * width].astype(LOW).T
    out_weight[...] = whole[3 * width : 4 * width].astype(LOW)
    norms[...] = whole[4 * width : 4 * width + 4]


def shards(
    tokens,
    cotangent,
    masked,
    omega,
    att_weights,
    att_first,
    att_second,
    ffn_in,
    ffn_out,
    ffn_in_first,
    ffn_in_second,
    ffn_out_first,
    ffn_out_second,
):
    seqs, length, width = tokens.shape
    size, count = omega.shape
    heads = width // size
    square = width * width
    groups = lax.axis_size("seq")
    devices = lax.axis_size("dp") * groups
    shard_len = att_weights.shape[0]
    place = lax.axis_index(("dp", "seq"))
    starts = [(i * shard_len) // width for i in range(devices)]
    offsets = [(i * shard_len) % width for i in range(devices)]
    rows = -(-(max(offsets) + shard_len) // width)
    held_rows = -(-rows // 8) * 8
    offset = (place * shard_len) % width

    framed = lax.dynamic_update_slice(
        jnp.zeros((held_rows * width,), LOW), att_weights.astype(LOW), (offset,)
    ).reshape(held_rows, width)
    early = []
    halves = [framed[:, : width // 2], framed[:, width // 2 :]]
    gathered = [gather_doubling(half, order, early) for half, order in zip(halves, gather_orders())]
    spots = [[place_in(order[::-1], i) for i in range(devices)] for order in gather_orders()]
    whole_rows = -(-(starts[-1] + rows) // 8) * 8
    group_width = ffn_in.shape[1]
    pair = jnp.concatenate([ffn_in.astype(LOW), ffn_out.astype(LOW).T], axis=1)
    pair, early[0] = lax.optimization_barrier((pair, early[0]))
    pair = lax.all_gather(pair, ("seq", "dp"), axis=0, tiled=True)
    pair = pair.reshape(groups, width, 2 * group_width)

    weights, out_weight, norms = pl.pallas_call(
        functools.partial(unpack_kernel, starts, spots, rows),
        out_shape=[array((3 * width, width), LOW), array((width, width), LOW), array((4, width), F32)],
        scratch_shapes=[pltpu.VMEM((whole_rows, width), F32)],
        name="unpack",
        compiler_params=pltpu.CompilerParams(vmem_limit_bytes=VMEM_LIMIT),
    )(*gathered)

    first_shape = (width, groups * group_width)
    target = (cotangent.astype(F32) * masked.astype(F32)[:, :, None]).astype(LOW)
    omega_high = lax.reduce_precision(omega, 8, 7)
    omega_rest = omega - omega_high
    omega_parts = jnp.concatenate([omega_high, omega_rest, omega_high, omega_rest], axis=0).T.astype(LOW)
    omega_low = jnp.concatenate(
        [omega, jnp.ones((1, count), F32), jnp.zeros((SPARE - 1, count), F32)], axis=0
    ).astype(LOW)

    ext = size + SPARE
    unit = 2 * heads * length * length * length * seqs
    flat = (seqs, width, length)
    feat = (seqs, heads, count, length)
    held = (seqs, heads, ext, length)
    score_shape = (seqs, heads, length, length)
    recip_shape = (seqs, heads, length)
    state_rows = heads // 2 * size + SPARE
    state_shape = (seqs, state_rows, count)
    core = bit_of("seq", 0).astype(jnp.int32).reshape(1)
    in_smem = pl.BlockSpec(memory_space=pltpu.SMEM)

    def spec(value):
        return per_seq(value.shape) if value.shape[0] == seqs else fixed(value.shape)

    def scratch_rows(parts):
        return [
            pltpu.VMEM((parts * width, length), F32),
            pltpu.VMEM((heads, 4 * size, length), LOW),
            pltpu.VMEM((heads, length), F32),
        ]

    tokens, target, omega_low = lax.optimization_barrier((tokens, target, omega_low))
    args = (tokens, norms, weights, omega_parts)
    outs = [array(flat, LOW)] * 2 + [array(held, LOW), pltpu.VMEM(feat, LOW)] + [array(state_shape, LOW)] * 2
    turned, uk, value, pk, own, their = call(
        functools.partial(keys_kernel, heads, size),
        seqs,
        args + (core,),
        [spec(a) for a in args] + [in_smem],
        outs,
        [spec(a) for a in outs],
        "keys",
        1,
        chip=(),
        scratch=scratch_rows(2) + [pltpu.VMEM((heads, ext, count), F32)],
    )
    beside, far, mine = send_half(own, their, True)
    args = (turned, weights, omega_parts, value, pk)
    outs = [array(flat, LOW), pltpu.VMEM(feat, LOW), array(score_shape, LOW), pltpu.VMEM(held, F32)]
    uq, pq, score, num = call(
        functools.partial(queries_kernel, heads, size),
        seqs,
        args,
        [spec(a) for a in args],
        outs,
        [spec(a) for a in outs],
        "queries",
        1,
        scratch_rows(1),
        chip=(4,),
        after=(mine,),
    )
    far, uq = lax.optimization_barrier((far, uq))
    keep, come = receive_half(own, beside, far, True)
    states = [per_seq(keep.shape)] * 2
    outs = [array(flat, LOW), array(recip_shape, F32), array(tokens.shape, F32), array(tokens.shape, LOW)]
    mixed, recip, middle, normed_two = call(
        functools.partial(mix_kernel, heads, size),
        seqs,
        (tokens, norms, out_weight, num, core, keep, come, pq),
        [spec(tokens), spec(norms), spec(out_weight), spec(num), in_smem, *states, spec(pq)],
        outs,
        [spec(a) for a in outs],
        "mix",
        1,
        chip=(3, 7),
    )

    total_rows = seqs * length
    block = 2 * length
    by_block = pl.BlockSpec((block, width), lambda i: (i, 0))
    rows_shape = (total_rows, width)
    block_out, grad_middle, leave, stay, norm_two_grad = call(
        functools.partial(ffn_kernel, groups),
        total_rows // block,
        (*[a.reshape(rows_shape) for a in (normed_two, middle, target)], norms, pair, core),
        [by_block, by_block, by_block, fixed(norms.shape), fixed(pair.shape), in_smem],
        [array(rows_shape, LOW), array(rows_shape, F32)] + [array(first_shape, LOW)] * 2 + [array((2, width), F32)],
        [by_block, by_block, fixed(first_shape), fixed(first_shape), fixed((2, width))],
        "ffn",
        20 * unit,
        chip=(),
        scratch=[pltpu.VMEM((groups, width, group_width), F32)] * 2,
    )
    block_out = block_out.reshape(tokens.shape)
    grad_middle = grad_middle.reshape(tokens.shape)
    come_pair = flip(leave, "seq", 0)

    args = (grad_middle, out_weight, mixed, recip, pq)
    outs = [array(held, LOW)] + [array(state_shape, LOW)] * 2
    outs = outs + [array((width, width), F32)]
    outers, own, their, out_proj = call(
        functools.partial(outer_kernel, heads, size),
        seqs,
        args + (core,),
        [spec(a) for a in args] + [in_smem],
        outs,
        [spec(a) for a in outs],
        "outer",
        1,
        chip=(),
        scratch=[pltpu.VMEM((width, length), F32), pltpu.VMEM((heads, ext, count), F32)],
    )
    their, come_pair = lax.optimization_barrier((their, come_pair))
    dp_rows = width // lax.axis_size("dp")
    near_sent, terms = split_rows([stay, come_pair], "dp", [0], dp_rows)
    beside, far, mine = send_half(own, their, False)
    args = (turned, omega_low, outers, value, pq, pk, score, core, keep, come, uq, uk)
    outs = [array(flat, LOW)] * 3
    query_grad, key_part, value_part, query_weight = call(
        functools.partial(back_query_kernel, heads, size),
        seqs,
        args,
        [spec(a) for a in args[:7]] + [in_smem, *states, spec(uq), spec(uk)],
        outs + [array((width, width), F32)],
        [spec(a) for a in outs] + [fixed((width, width))],
        "back_query",
        1,
        chip=(),
        scratch=[
            pltpu.VMEM((heads, ext, count), LOW),
            pltpu.VMEM(score_shape[1:], LOW),
            pltpu.VMEM(feat[1:], LOW),
            pltpu.VMEM(feat[1:], LOW),
        ],
        after=(mine, *near_sent),
    )
    far, query_grad = lax.optimization_barrier((far, query_grad))
    keep, come = receive_half(own, beside, far, False)
    high = list(range(axis_bits("dp") - 1, 0, -1))
    near_sent, terms = split_rows(terms, "dp", high[:2], dp_rows << max(len(high) - 2, 0))
    orders = scatter_orders()
    owners = [sorted(range(devices), key=lambda i: place_in(order, i)) for order in orders]
    piece_shape = (2, devices // 2, held_rows, width // 2)
    args = (tokens, norms, grad_middle, weights, omega_low, value, pk, core, keep, come)
    more = (uk, query_grad, key_part, value_part, query_weight, out_proj, norm_two_grad, turned)
    input_grad, leave, stay = call(
        functools.partial(back_key_kernel, heads, size, (starts, rows, owners)),
        seqs,
        args + more,
        [spec(a) for a in args[:7]] + [in_smem, *states] + [spec(a) for a in more],
        [array(tokens.shape, F32), array(piece_shape, LOW), array(piece_shape, F32)],
        [per_seq(tokens.shape), fixed(piece_shape), fixed(piece_shape)],
        "back_key",
        7 * unit,
        chip=(),
        scratch=[
            pltpu.VMEM((3 * width, length), LOW),
            pltpu.VMEM((heads, ext, count), LOW),
            pltpu.VMEM(feat[1:], LOW),
            pltpu.VMEM((width, 2 * width), F32),
            pltpu.VMEM((2, width), F32),
            pltpu.VMEM((whole_rows, width), F32),
        ],
        after=tuple(near_sent),
    )
    leave, terms = lax.optimization_barrier((leave, terms))
    come_pieces = flip(leave, "seq", 0)
    for step, bit in enumerate(high[2:]):
        _, terms = split_rows(terms, "dp", [bit], dp_rows << (len(high) - 3 - step))
    terms, come_pieces = lax.optimization_barrier(([total_of(terms)], come_pieces))
    for bit in range(axis_bits("seq") - 1, 0, -1):
        terms = [t.reshape(t.shape[0], 2, -1) for t in terms]
        side = bit_of("seq", bit)
        sent = total_of([lax.dynamic_index_in_dim(t, 1 - side, 1, keepdims=False) for t in terms]).astype(LOW)
        kept = total_of([lax.dynamic_index_in_dim(t, side, 1, keepdims=False) for t in terms])
        terms = [kept, flip(sent, "seq", bit)]
    sums = []
    for index, order in enumerate(orders):
        sums.append(scatter_halving([stay[index], come_pieces[index]], order[1:]))
    own_pair = total_of(terms)
    grad_first = own_pair[:, :group_width]
    grad_second = own_pair[:, group_width:].T
    att_grad = jnp.concatenate(sums, axis=1)
    att_grad = lax.dynamic_slice(att_grad.reshape(-1), (offset,), (shard_len,)).astype(F32)

    position = place * shard_len + jnp.arange(shard_len, dtype=jnp.int32)
    is_matrix = position < 4 * square
    rate = jnp.where(is_matrix, RATE_MATRIX, RATE_NORM)
    decay = jnp.where(is_matrix, WEIGHT_DECAY, 0.0)
    att_new, att_first_new, att_second_new = adamw(
        att_weights, att_first, att_second, att_grad, rate, decay
    )
    ffn_in_new, ffn_in_first_new, ffn_in_second_new = adamw(
        ffn_in, ffn_in_first, ffn_in_second, grad_first, RATE_MATRIX, WEIGHT_DECAY
    )
    ffn_out_new, ffn_out_first_new, ffn_out_second_new = adamw(
        ffn_out, ffn_out_first, ffn_out_second, grad_second, RATE_MATRIX, WEIGHT_DECAY
    )
    return (
        block_out,
        input_grad,
        att_new,
        att_first_new,
        att_second_new,
        att_new.astype(jnp.bfloat16),
        ffn_in_new,
        ffn_in_first_new,
        ffn_in_second_new,
        ffn_in_new.astype(jnp.bfloat16),
        ffn_out_new,
        ffn_out_first_new,
        ffn_out_second_new,
        ffn_out_new.astype(jnp.bfloat16),
    )


def solution(mesh):
    in_specs = (
        P("dp", "seq", None),
        P("dp", "seq", None),
        P("dp", "seq"),
        P(),
        P(("dp", "seq")),
        P(("dp", "seq")),
        P(("dp", "seq")),
        P("dp", "seq"),
        P("seq", "dp"),
        P("dp", "seq"),
        P("dp", "seq"),
        P("seq", "dp"),
        P("seq", "dp"),
    )
    out_specs = (
        P("dp", "seq", None),
        P("dp", "seq", None),
        P(("dp", "seq")),
        P(("dp", "seq")),
        P(("dp", "seq")),
        P(("dp", "seq")),
        P("dp", "seq"),
        P("dp", "seq"),
        P("dp", "seq"),
        P("dp", "seq"),
        P("seq", "dp"),
        P("seq", "dp"),
        P("seq", "dp"),
        P("seq", "dp"),
    )
    return jax.shard_map(shards, mesh=mesh, in_specs=in_specs, out_specs=out_specs, check_vma=False)
```

```python
import functools
import math

import jax
import jax.numpy as jnp
from jax import lax
from jax.experimental import pallas as pl
from jax.experimental.pallas import tpu as pltpu
from jax.sharding import PartitionSpec as P

CH = 256
STEP = 10
BETA_FIRST = 0.9
BETA_SECOND = 0.999
ADAM_EPS = 1e-08
WEIGHT_DECAY = 0.1
RATE_MATRIX = 0.02
RATE_NORM = 0.3
NORM_EPS = 1e-05
SPARE = 16
VMEM_LIMIT = 16 * 1024 * 1024
BIG = 1 << 20
LIMITS = {'keys': 14, 'queries': 16, 'mix': 12, 'ffn': 40, 'outer': 14, 'back_query': 24, 'back_key': 34}
F32 = jnp.float32
LOW = jnp.bfloat16


def dot_nn(left, right):
    return lax.dot_general(left, right, (((1,), (0,)), ((), ())), preferred_element_type=F32)


def dot_nt(left, right):
    return lax.dot_general(left, right, (((1,), (1,)), ((), ())), preferred_element_type=F32)


def dot_tn(left, right):
    return lax.dot_general(left, right, (((0,), (0,)), ((), ())), preferred_element_type=F32)


def norm_parts(inputs):
    centre = inputs - jnp.mean(inputs, axis=-1, keepdims=True)
    root = lax.rsqrt(jnp.mean(centre * centre, axis=-1, keepdims=True) + NORM_EPS)
    return centre * root, root


def norm_back(grad, gain, unit, root):
    inner = grad * gain
    mean_inner = jnp.mean(inner, axis=-1, keepdims=True)
    return root * (inner - mean_inner - unit * jnp.mean(inner * unit, axis=-1, keepdims=True))


def causal(length):
    earlier = lax.broadcasted_iota(jnp.int32, (length, length), 0)
    return earlier <= lax.broadcasted_iota(jnp.int32, (length, length), 1)


def put_states(own_out, their_out, core, heads, size, states, copies):
    half = heads // 2
    base = half * size
    first = core[0] == 0
    own_out[0, base:] = jnp.zeros((SPARE, own_out.shape[2]), LOW)
    their_out[0, base:] = jnp.zeros((SPARE, own_out.shape[2]), LOW)
    for index in range(half):
        low, high = states[index], states[index + half]
        total_low, total_high = [
            sum(s[size + i : size + i + 1] for i in range(copies)) for s in (low, high)
        ]
        at = slice(index * size, (index + 1) * size)
        own_out[0, at] = jnp.where(first, low[:size], high[:size]).astype(LOW)
        their_out[0, at] = jnp.where(first, high[:size], low[:size]).astype(LOW)
        row = slice(base + index, base + index + 1)
        own_out[0, row] = jnp.where(first, total_low, total_high).astype(LOW)
        their_out[0, row] = jnp.where(first, total_high, total_low).astype(LOW)


def get_state(core, keep, come, head, heads, size, copies):
    part, index = divmod(head, heads // 2)
    base = heads // 2 * size
    own = core[0] == part
    total = jnp.where(own, keep[0, base : base + SPARE], come[0, base : base + SPARE]).astype(F32)[index : index + 1]
    line = lax.broadcasted_iota(jnp.int32, (SPARE, total.shape[1]), 0)
    spare = jnp.where(line < copies, total, 0.0).astype(LOW)
    rows = slice(index * size, (index + 1) * size)
    return jnp.concatenate([jnp.where(own, keep[0, rows], come[0, rows]), spare], axis=0)


def split_features(rows, scale, shift, high_out, stack, half):
    size = rows.shape[0]
    scaled = rows * scale
    high = scaled.astype(LOW)
    rest = (scaled - high.astype(F32)).astype(LOW)
    high_out[...] = high
    for part, piece in enumerate((high, high, rest, rest)):
        stack[part * size : (part + 1) * size] = piece
    half[...] = 0.5 * jnp.sum(scaled * scaled, axis=0, keepdims=True) + shift


def staged(count, *stages):
    for stage in stages:
        for item in range(count):
            stage(item)


def keys_kernel(
    heads,
    size,
    tok,
    norms,
    weights,
    omega,
    core,
    turned_out,
    uk_out,
    value_out,
    pk_out,
    own_out,
    their_out,
    rows,
    stacks,
    halves,
    states,
):
    width = heads * size
    length = tok.shape[1]
    unit, _ = norm_parts(tok[0].astype(F32))
    turned_out[0] = (unit * norms[0:1] + norms[1:2]).astype(LOW).T
    rows[...] = dot_nn(weights[width:], turned_out[0])
    spare = (lax.broadcasted_iota(jnp.int32, (SPARE, length), 0) < 2).astype(F32).astype(LOW)
    shift = 0.5 * math.log(omega.shape[0])

    def split(head):
        at = slice(head * size, (head + 1) * size)
        split_features(
            rows[at], size ** (-0.25), shift, uk_out.at[0, at], stacks.at[head], halves.at[head : head + 1]
        )
        value_out[0, head, :size] = rows[width + head * size : width + (head + 1) * size].astype(LOW)
        value_out[0, head, size:] = spare

    def feature(head):
        projected = dot_nn(omega[...], stacks[head])
        pk_out[0, head] = jnp.exp(projected - halves[head : head + 1]).astype(LOW)

    def local_state(head):
        states[head] = dot_nt(value_out[0, head], pk_out[0, head])

    staged(heads, split, feature, local_state)
    put_states(own_out, their_out, core, heads, size, states, 1)


def queries_kernel(heads, size, turned, weights, omega, value, pk, uq_out, pq_out, pq_copy, score_out, num_out, rows, stacks, halves):
    width = heads * size
    length = turned.shape[2]
    rows[...] = dot_nn(weights[:width], turned[0])
    shift = 0.5 * math.log(omega.shape[0])
    keep = causal(length)

    def split(head):
        at = slice(head * size, (head + 1) * size)
        split_features(
            rows[at], size ** (-0.25), shift, uq_out.at[0, at], stacks.at[head], halves.at[head : head + 1]
        )

    def feature(head):
        projected = dot_nn(omega[...], stacks[head])
        feat = jnp.exp(projected - halves[head : head + 1]).astype(LOW)
        pq_out[0, head] = feat
        pq_copy[0, head] = feat

    def score(head):
        score_out[0, head] = jnp.where(keep, dot_tn(pk[0, head], pq_out[0, head]), 0.0).astype(LOW)

    def numerator(head):
        num_out[0, head] = dot_nn(value[0, head], score_out[0, head])

    staged(heads, split, feature, score, numerator)


def mix_kernel(heads, size, tok, norms, out_weight, num, core, keep, come, pq, mixed_out, recip_out, middle_out, normed_out):
    state = (core, keep, come)
    for head in range(heads):
        at = head * size
        total = num[0, head] + dot_nn(get_state(*state, head, heads, size, 2), pq[0, head])
        recip = 1.0 / total[size : size + 1]
        mixed_out[0, at : at + size] = (total[:size] * recip).astype(LOW)
        recip_out[0, head : head + 1] = recip
    mixed = mixed_out[0]
    middle = tok[0].astype(F32) + dot_tn(mixed, out_weight[...])
    middle_out[0] = middle
    unit, _ = norm_parts(middle)
    normed_out[0] = (unit * norms[2:3] + norms[3:4]).astype(LOW)


def gelu_pair(hidden):
    slope = math.sqrt(2.0 / math.pi)
    square = hidden * hidden
    tanh = jnp.tanh(hidden * (slope + (slope * 0.044715) * square))
    upper = 0.5 + 0.5 * tanh
    inner = (0.5 * slope) + (1.5 * slope * 0.044715) * square
    return hidden * upper, upper + hidden * (1.0 - tanh * tanh) * inner


def ffn_kernel(
    groups, devices, normed, middle, target, norms, pair, core, out, grad_out, leave, stay, norm_grad, first_sum, second_sum
):
    step = pl.program_id(0)
    half = pair.shape[2] // 2
    own = normed[...]
    grads = target[...]
    own_turned = own.T
    grads_turned = grads.T

    @pl.when(step == 0)
    def _():
        first_sum[...] = jnp.zeros_like(first_sum)
        second_sum[...] = jnp.zeros_like(second_sum)
        norm_grad[...] = jnp.zeros_like(norm_grad)

    result = jnp.zeros(own.shape, F32)
    grad_normed = jnp.zeros(own.shape, F32)
    for group in range(groups):
        first = pair[group, :, :half]
        second = pair[group, :, half:]
        active, slope = gelu_pair(dot_nn(own, first))
        active = active.astype(LOW)
        result = result + dot_nt(active, second)
        grad_hidden = (dot_nn(grads, second) * slope).astype(LOW)
        grad_normed = grad_normed + dot_nt(grad_hidden, first)
        first_sum[group] += dot_nn(own_turned, grad_hidden)
        second_sum[group] += dot_nn(grads_turned, active)
    rows = middle[...]
    out[...] = (rows + result).astype(LOW)
    unit, root = norm_parts(rows)
    grad_out[...] = grads.astype(F32) + norm_back(grad_normed, norms[2:3], unit, root)
    norm_grad[0:1] += jnp.sum(grad_normed * unit, axis=0, keepdims=True)
    norm_grad[1:2] += jnp.sum(grad_normed, axis=0, keepdims=True)

    @pl.when(step == pl.num_programs(0) - 1)
    def _():
        mine = core[0]
        count = normed.shape[1] // devices
        for chip in range(groups // 2):
            at = 2 * half * chip
            for side, target_ref in ((mine, stay), (1 - mine, leave)):
                for place in range(devices):
                    spot = place // 2 + (place % 2) * (devices // 2)
                    rows_in = slice(place * count, (place + 1) * count)
                    rows_out = slice(spot * count, (spot + 1) * count)
                    target_ref[rows_out, at : at + half] = first_sum[2 * chip + side, rows_in].astype(LOW)
                    target_ref[rows_out, at + half : at + 2 * half] = second_sum[2 * chip + side, rows_in].astype(LOW)


def through_omega(flow, scaled, omega_low, size):
    back = dot_nn(omega_low, flow)
    return ((back[:size] - scaled.astype(F32) * back[size : size + 1]) * size ** (-0.25))


def outer_kernel(
    heads, size, grad_middle, out_weight, mixed, recip, pq, core, outer_out, own_out, their_out, out_proj, grad_mixed, states
):
    length = grad_middle.shape[1]

    @pl.when(pl.program_id(0) == 0)
    def _():
        out_proj[...] = jnp.zeros_like(out_proj)

    grad_low = grad_middle[0].astype(LOW)
    grad_mixed[...] = dot_nt(out_weight[...], grad_low)
    out_proj[...] += dot_nn(mixed[0], grad_low)
    line = lax.broadcasted_iota(jnp.int32, (SPARE, length), 0)

    def scale(head):
        at = head * size
        outer = grad_mixed[at : at + size] * recip[0, head : head + 1]
        centre = -jnp.sum(outer * mixed[0, at : at + size].astype(F32), axis=0, keepdims=True)
        rest = centre - centre.astype(LOW).astype(F32)
        outer_out[0, head, :size] = outer.astype(LOW)
        outer_out[0, head, size:] = jnp.where(line == 0, centre, jnp.where(line == 1, rest, 0.0)).astype(LOW)

    def local_state(head):
        states[head] = dot_nt(outer_out[0, head], pq[0, head])

    staged(heads, scale, local_state)
    put_states(own_out, their_out, core, heads, size, states, 2)


def back_query_kernel(
    heads,
    size,
    turned,
    omega_low,
    outers,
    value,
    pq,
    pk,
    scores,
    core,
    keep_state,
    come_state,
    uq,
    uk,
    query_out,
    key_out,
    value_out,
    query_weight,
    befores,
    grad_scores,
    flows,
    key_flows,
):
    @pl.when(pl.program_id(0) == 0)
    def _():
        query_weight[...] = jnp.zeros_like(query_weight)

    keep = causal(turned.shape[2])

    def score(head):
        befores[head] = get_state(core, keep_state, come_state, head, heads, size, 2)
        grad_scores[head] = jnp.where(keep, dot_tn(value[0, head], outers[0, head]), 0.0).astype(LOW)

    def feature(head):
        at = head * size
        grad_feat = dot_nn(pk[0, head], grad_scores[head]) + dot_tn(befores[head], outers[0, head])
        flows[head] = (grad_feat * pq[0, head].astype(F32)).astype(LOW)
        grad_key_feat = dot_nt(pq[0, head], grad_scores[head])
        key_flows[head] = (grad_key_feat * pk[0, head].astype(F32)).astype(LOW)
        value_out[0, at : at + size] = dot_nt(outers[0, head], scores[0, head])[:size].astype(LOW)

    def query(head):
        at = head * size
        query_out[0, at : at + size] = through_omega(flows[head], uq[0, at : at + size], omega_low[...], size).astype(
            LOW
        )
        key_out[0, at : at + size] = through_omega(key_flows[head], uk[0, at : at + size], omega_low[...], size).astype(LOW)

    staged(heads, score, feature, query)
    query_weight[...] += dot_nt(turned[0], query_out[0])


def back_key_kernel(
    heads,
    size,
    layout,
    tok,
    norms,
    grad_middle,
    weights,
    omega_low,
    value,
    pk,
    core,
    keep_state,
    come_state,
    uk,
    query_grad,
    key_part,
    value_part,
    query_weight,
    out_proj,
    norm_two,
    turned,
    input_grad,
    leave,
    stay,
    flat,
    laters,
    flows,
    pair_weight,
    norm_grad,
    whole,
):
    width = heads * size

    @pl.when(pl.program_id(0) == 0)
    def _():
        pair_weight[...] = jnp.zeros_like(pair_weight)
        norm_grad[...] = jnp.zeros_like(norm_grad)

    unit, root = norm_parts(tok[0].astype(F32))
    flat[:width] = query_grad[0]

    def later(head):
        laters[head] = get_state(core, keep_state, come_state, head, heads, size, 1)

    def feature(head):
        at = 2 * width + head * size
        grad_feat = dot_tn(laters[head], value[0, head])
        flows[head] = (grad_feat * pk[0, head].astype(F32)).astype(LOW)
        extra = dot_nn(laters[head], pk[0, head])[:size]
        flat[at : at + size] = (
            value_part[0, head * size : (head + 1) * size].astype(F32) + extra
        ).astype(LOW)

    def key(head):
        at = width + head * size
        part = slice(head * size, (head + 1) * size)
        total = key_part[0, part].astype(F32) + through_omega(flows[head], uk[0, part], omega_low[...], size)
        flat[at : at + size] = total.astype(LOW)

    staged(heads, later, feature, key)
    pair_weight[...] += dot_nt(turned[0], flat[width:])
    grad_normed = dot_tn(flat[...], weights[...])
    input_grad[0] = grad_middle[0] + norm_back(grad_normed, norms[0:1], unit, root)
    norm_grad[0:1] += jnp.sum(grad_normed * unit, axis=0, keepdims=True)
    norm_grad[1:2] += jnp.sum(grad_normed, axis=0, keepdims=True)

    @pl.when(pl.program_id(0) == pl.num_programs(0) - 1)
    def _():
        whole[:width] = query_weight[...]
        whole[width : 2 * width] = pair_weight[:, :width]
        whole[2 * width : 3 * width] = pair_weight[:, width:]
        whole[3 * width : 4 * width] = out_proj[...]
        whole[4 * width : 4 * width + 2] = norm_grad[...]
        whole[4 * width + 2 : 4 * width + 4] = norm_two[...]
        starts, rows, owners = layout
        half = width // 2
        first = core[0] == 0
        leave[...] = jnp.zeros_like(leave)
        stay[...] = jnp.zeros_like(stay)
        for part in range(2):
            count = leave.shape[1]
            columns = slice(part * half, (part + 1) * half)
            for spot in range(count):
                low = starts[owners[part][spot]]
                high = starts[owners[part][spot + count]]
                low = whole[low : low + rows, columns]
                high = whole[high : high + rows, columns]
                stay[part, spot, :rows] = jnp.where(first, low, high)
                leave[part, spot, :rows] = jnp.where(first, high, low).astype(LOW)


def per_seq(shape, offset=0):
    rest = tuple(shape[1:])
    return pl.BlockSpec((1,) + rest, lambda i: (i + offset,) + (0,) * len(rest))


def fixed(shape):
    return pl.BlockSpec(tuple(shape), lambda i: (0,) * len(shape))


def call(kernel, steps, args, in_specs, outs, out_specs, name, flops, scratch=(), aliases=None, after=(), chip=None):
    if chip is not None:
        args = tuple(
            on_chip(a) if i in chip else off_chip(a) if math.prod(a.shape) >= BIG else a for i, a in enumerate(args)
        )
    if after:
        count, body = len(args), kernel
        args = tuple(args) + tuple(after)
        in_specs = list(in_specs) + [pl.BlockSpec(memory_space=pl.ANY)] * len(after)

        def kernel(*refs):
            body(*refs[:count], *refs[count + len(after) :])

    moved = sum(math.prod(a.shape) * jnp.dtype(a.dtype).itemsize for a in list(args) + list(outs))
    return pl.pallas_call(
        kernel,
        grid=(steps,),
        in_specs=in_specs,
        out_specs=out_specs,
        out_shape=outs,
        scratch_shapes=list(scratch),
        name=name,
        input_output_aliases=aliases or {},
        compiler_params=pltpu.CompilerParams(
            dimension_semantics=("arbitrary",), vmem_limit_bytes=LIMITS[name] * 1024 * 1024
        ),
        cost_estimate=pl.CostEstimate(
            flops=flops, bytes_accessed=moved if flops > 1 else 1, transcendentals=0
        ),
    )(*args)


def on_chip(value):
    return pltpu.with_memory_space_constraint(value, pltpu.VMEM)


def off_chip(value):
    return pltpu.with_memory_space_constraint(value, pltpu.HBM)


def array(shape, dtype):
    return pltpu.HBM(tuple(shape), dtype)


def flip(value, axis, bit):
    return lax.ppermute(value, axis, [(i, i ^ (1 << bit)) for i in range(lax.axis_size(axis))])


def bit_of(axis, bit):
    return (lax.axis_index(axis) >> bit) & 1


def send_half(own, their, forward, tie):
    count = lax.axis_size("seq")
    beside = flip(their, "seq", 0)
    mine = (own.astype(F32) + beside.astype(F32)).astype(LOW)
    mine, tie = lax.optimization_barrier((mine, tie))
    far = None
    for step in range(1, count // 2):
        hop = 2 * step if forward else -2 * step
        pairs = [(i, i + hop) for i in range(count) if 0 <= i + hop < count]
        come = lax.ppermute(mine, "seq", pairs)
        far = come if far is None else far + come
    return beside, far, tie


def receive_half(own, beside, far, forward):
    core = bit_of("seq", 0)
    giver = (core == 0) if forward else (core == 1)
    give = (far.astype(F32) + jnp.where(giver, own.astype(F32), 0.0)).astype(LOW)
    keep = (far.astype(F32) + jnp.where(giver, 0.0, beside.astype(F32))).astype(LOW)
    return keep, flip(give, "seq", 0)


def axis_bits(axis):
    return lax.axis_size(axis).bit_length() - 1


def gather_orders():
    high = [("dp", bit) for bit in range(1, axis_bits("dp"))]
    seq_high = [("seq", bit) for bit in range(1, axis_bits("seq"))]
    near = [("dp", 0)]
    return [high + near + seq_high + [("seq", 0)], seq_high + high + near + [("seq", 0)]]


def scatter_orders():
    high = [("dp", bit) for bit in range(axis_bits("dp") - 1, 0, -1)]
    seq_high = [("seq", bit) for bit in range(axis_bits("seq") - 1, 0, -1)]
    near = [("dp", 0)]
    return [[("seq", 0)] + seq_high + near + high, [("seq", 0)] + near + high + seq_high]


def place_in(order, index):
    seq_bits = axis_bits("seq")
    spot = 0
    for axis, bit in order:
        shift = bit if axis == "seq" else bit + seq_bits
        spot = 2 * spot + ((index >> shift) & 1)
    return spot


def gather_doubling(value, order, early):
    value = value[None]
    for axis, bit in order:
        come = flip(value, axis, bit)
        early.append(come)
        low = bit_of(axis, bit) == 0
        value = jnp.concatenate([jnp.where(low, value, come), jnp.where(low, come, value)], axis=0)
    return value


def total_of(terms):
    return sum(term.astype(F32) for term in terms)


def scatter_step(terms, axis, bit, leave=None):
    mine = bit_of(axis, bit)
    if leave is None:
        leave = total_of([lax.dynamic_index_in_dim(term, 1 - mine, 0, keepdims=False) for term in terms]).astype(LOW)
    come = flip(leave, axis, bit)
    stay = total_of([lax.dynamic_index_in_dim(term, mine, 0, keepdims=False) for term in terms])
    return [stay, come]


def split_rows(terms, axis, bits, low, tie):
    ways = 1 << len(bits)
    terms = [t.reshape(-1, ways, low, t.shape[1]) for t in terms]
    shift = min(bits)
    mine = (lax.axis_index(axis) >> shift) & (ways - 1)

    def part(which):
        total = total_of([lax.dynamic_index_in_dim(t, which, 1, keepdims=False) for t in terms]).astype(LOW)
        return total.reshape(-1, total.shape[-1])

    leaving = [part(mine ^ other) for other in range(1, ways)]
    leaving, tie = lax.optimization_barrier((leaving, tie))
    size = lax.axis_size(axis)
    come = [
        lax.ppermute(leave, axis, [(i, i ^ (other << shift)) for i in range(size)])
        for other, leave in enumerate(leaving, 1)
    ]
    return tie, [part(mine)] + come


def scatter_halving(terms, order):
    for axis, bit in order:
        terms = scatter_step([t.reshape((2, t.shape[0] // 2) + t.shape[1:]) for t in terms], axis, bit)
    return total_of(terms)[0]


def adamw(weight, first, second, grad, rate, decay):
    first_new = BETA_FIRST * first + (1.0 - BETA_FIRST) * grad
    second_new = BETA_SECOND * second + (1.0 - BETA_SECOND) * grad * grad
    first_hat = first_new / (1.0 - BETA_FIRST**STEP)
    second_hat = second_new / (1.0 - BETA_SECOND**STEP)
    weight_new = weight - rate * (first_hat / (jnp.sqrt(second_hat) + ADAM_EPS) + decay * weight)
    return (weight_new, first_new, second_new)


def unpack_kernel(starts, spots, rows, left, right, wide_out, out_weight, norms, whole):
    whole[...] = jnp.zeros_like(whole)
    half = left.shape[2]
    for index, start in enumerate(starts):
        whole[start : start + rows, :half] += left[spots[0][index], :rows].astype(F32)
        whole[start : start + rows, half:] += right[spots[1][index], :rows].astype(F32)
    width = out_weight.shape[0]
    for part in range(3):
        wide_out[part * width : (part + 1) * width] = whole[part * width : (part + 1) * width].astype(LOW).T
    out_weight[...] = whole[3 * width : 4 * width].astype(LOW)
    norms[...] = whole[4 * width : 4 * width + 4]


def shards(
    tokens,
    cotangent,
    masked,
    omega,
    att_weights,
    att_first,
    att_second,
    ffn_in,
    ffn_out,
    ffn_in_first,
    ffn_in_second,
    ffn_out_first,
    ffn_out_second,
):
    seqs, length, width = tokens.shape
    size, count = omega.shape
    heads = width // size
    square = width * width
    groups = lax.axis_size("seq")
    devices = lax.axis_size("dp") * groups
    shard_len = att_weights.shape[0]
    place = lax.axis_index(("dp", "seq"))
    starts = [(i * shard_len) // width for i in range(devices)]
    offsets = [(i * shard_len) % width for i in range(devices)]
    rows = -(-(max(offsets) + shard_len) // width)
    held_rows = -(-rows // 8) * 8
    offset = (place * shard_len) % width

    framed = lax.dynamic_update_slice(
        jnp.zeros((held_rows * width,), LOW), att_weights.astype(LOW), (offset,)
    ).reshape(held_rows, width)
    early = []
    halves = [framed[:, : width // 2], framed[:, width // 2 :]]
    gathered = [gather_doubling(half, order, early) for half, order in zip(halves, gather_orders())]
    spots = [[place_in(order[::-1], i) for i in range(devices)] for order in gather_orders()]
    whole_rows = -(-(starts[-1] + rows) // 8) * 8
    group_width = ffn_in.shape[1]
    pair = jnp.concatenate([ffn_in.astype(LOW), ffn_out.astype(LOW).T], axis=1)
    pair, early[0] = lax.optimization_barrier((pair, early[0]))
    pair = lax.all_gather(pair, ("seq", "dp"), axis=0, tiled=True)
    pair = pair.reshape(groups, width, 2 * group_width)

    weights, out_weight, norms = pl.pallas_call(
        functools.partial(unpack_kernel, starts, spots, rows),
        out_shape=[pltpu.VMEM((3 * width, width), LOW), pltpu.VMEM((width, width), LOW), array((4, width), F32)],
        scratch_shapes=[pltpu.VMEM((whole_rows, width), F32)],
        name="unpack",
        compiler_params=pltpu.CompilerParams(vmem_limit_bytes=VMEM_LIMIT),
    )(*gathered)

    first_shape = (width, groups * group_width)
    target = (cotangent.astype(F32) * masked.astype(F32)[:, :, None]).astype(LOW)
    omega_high = lax.reduce_precision(omega, 8, 7)
    omega_rest = omega - omega_high
    omega_parts = jnp.concatenate([omega_high, omega_rest, omega_high, omega_rest], axis=0).T.astype(LOW)
    omega_low = jnp.concatenate(
        [omega, jnp.ones((1, count), F32), jnp.zeros((SPARE - 1, count), F32)], axis=0
    ).astype(LOW)

    ext = size + SPARE
    unit = 2 * heads * length * length * length * seqs
    flat = (seqs, width, length)
    feat = (seqs, heads, count, length)
    held = (seqs, heads, ext, length)
    score_shape = (seqs, heads, length, length)
    recip_shape = (seqs, heads, length)
    state_rows = heads // 2 * size + SPARE
    state_shape = (seqs, state_rows, count)
    core = bit_of("seq", 0).astype(jnp.int32).reshape(1)
    in_smem = pl.BlockSpec(memory_space=pltpu.SMEM)

    def spec(value):
        return per_seq(value.shape) if value.shape[0] == seqs else fixed(value.shape)

    def scratch_rows(parts):
        return [
            pltpu.VMEM((parts * width, length), F32),
            pltpu.VMEM((heads, 4 * size, length), LOW),
            pltpu.VMEM((heads, length), F32),
        ]

    args = (tokens, norms, weights, omega_parts)
    outs = [array(flat, LOW)] * 2 + [array(held, LOW), pltpu.VMEM(feat, LOW)] + [array(state_shape, LOW)] * 2
    turned, uk, value, pk, own, their = call(
        functools.partial(keys_kernel, heads, size),
        seqs,
        args + (core,),
        [spec(a) for a in args] + [in_smem],
        outs,
        [spec(a) for a in outs],
        "keys",
        1,
        chip=(),
        scratch=scratch_rows(2) + [pltpu.VMEM((heads, ext, count), F32)],
    )
    beside, far, omega_tied = send_half(own, their, True, omega_parts)
    args = (turned, weights, omega_tied, value, pk)
    outs = [array(flat, LOW), pltpu.VMEM(feat, LOW), array(feat, LOW), array(score_shape, LOW), pltpu.VMEM(held, F32)]
    uq, pq_near, pq, score, num = call(
        functools.partial(queries_kernel, heads, size),
        seqs,
        args,
        [spec(a) for a in args],
        outs,
        [spec(a) for a in outs],
        "queries",
        1,
        scratch_rows(1),
        chip=(4,),
    )
    far, uq, target = lax.optimization_barrier((far, uq, target))
    keep, come = receive_half(own, beside, far, True)
    states = [per_seq(keep.shape)] * 2
    outs = [array(flat, LOW), array(recip_shape, F32), array(tokens.shape, F32), array(tokens.shape, LOW)]
    mixed, recip, middle, normed_two = call(
        functools.partial(mix_kernel, heads, size),
        seqs,
        (tokens, norms, out_weight, num, core, keep, come, pq_near),
        [spec(tokens), spec(norms), spec(out_weight), spec(num), in_smem, *states, spec(pq_near)],
        outs,
        [spec(a) for a in outs],
        "mix",
        1,
        chip=(3, 7),
    )

    total_rows = seqs * length
    block = 2 * length
    by_block = pl.BlockSpec((block, width), lambda i: (i, 0))
    rows_shape = (total_rows, width)
    block_out, grad_middle, leave, stay, norm_two_grad = call(
        functools.partial(ffn_kernel, groups, lax.axis_size("dp")),
        total_rows // block,
        (*[a.reshape(rows_shape) for a in (normed_two, middle, target)], norms, pair, core),
        [by_block, by_block, by_block, fixed(norms.shape), fixed(pair.shape), in_smem],
        [array(rows_shape, LOW), array(rows_shape, F32)] + [array(first_shape, LOW)] * 2 + [array((2, width), F32)],
        [by_block, by_block, fixed(first_shape), fixed(first_shape), fixed((2, width))],
        "ffn",
        20 * unit,
        chip=(),
        scratch=[pltpu.VMEM((groups, width, group_width), F32)] * 2,
    )
    block_out = block_out.reshape(tokens.shape)
    grad_middle = grad_middle.reshape(tokens.shape)
    come_pair = flip(leave, "seq", 0)

    args = (grad_middle, out_weight, mixed, recip, pq)
    outs = [array(held, LOW)] + [array(state_shape, LOW)] * 2
    outs = outs + [array((width, width), F32)]
    outers, own, their, out_proj = call(
        functools.partial(outer_kernel, heads, size),
        seqs,
        args + (core,),
        [spec(a) for a in args] + [in_smem],
        outs,
        [spec(a) for a in outs],
        "outer",
        1,
        chip=(),
        scratch=[pltpu.VMEM((width, length), F32), pltpu.VMEM((heads, ext, count), F32)],
    )
    their, come_pair = lax.optimization_barrier((their, come_pair))
    dp_rows = width // lax.axis_size("dp")
    omega_low, terms = split_rows([stay, come_pair], "dp", [0], width // 2, omega_low)
    beside, far, omega_low = send_half(own, their, False, omega_low)
    args = (turned, omega_low, outers, value, pq, pk, score, core, keep, come, uq, uk)
    outs = [array(flat, LOW)] * 3
    query_grad, key_part, value_part, query_weight = call(
        functools.partial(back_query_kernel, heads, size),
        seqs,
        args,
        [spec(a) for a in args[:7]] + [in_smem, *states, spec(uq), spec(uk)],
        outs + [array((width, width), F32)],
        [spec(a) for a in outs] + [fixed((width, width))],
        "back_query",
        1,
        chip=(),
        scratch=[
            pltpu.VMEM((heads, ext, count), LOW),
            pltpu.VMEM(score_shape[1:], LOW),
            pltpu.VMEM(feat[1:], LOW),
            pltpu.VMEM(feat[1:], LOW),
        ],
    )
    far, query_grad = lax.optimization_barrier((far, query_grad))
    keep, come = receive_half(own, beside, far, False)
    high = list(range(axis_bits("dp") - 1, 0, -1))
    omega_low, terms = split_rows(terms, "dp", high[:2], dp_rows << max(len(high) - 2, 0), omega_low)
    orders = scatter_orders()
    owners = [sorted(range(devices), key=lambda i: place_in(order, i)) for order in orders]
    piece_shape = (2, devices // 2, held_rows, width // 2)
    args = (tokens, norms, grad_middle, weights, omega_low, value, pk, core, keep, come)
    more = (uk, query_grad, key_part, value_part, query_weight, out_proj, norm_two_grad, turned)
    input_grad, leave, stay = call(
        functools.partial(back_key_kernel, heads, size, (starts, rows, owners)),
        seqs,
        args + more,
        [spec(a) for a in args[:7]] + [in_smem, *states] + [spec(a) for a in more],
        [array(tokens.shape, F32), array(piece_shape, LOW), array(piece_shape, F32)],
        [per_seq(tokens.shape), fixed(piece_shape), fixed(piece_shape)],
        "back_key",
        7 * unit,
        chip=(),
        scratch=[
            pltpu.VMEM((3 * width, length), LOW),
            pltpu.VMEM((heads, ext, count), LOW),
            pltpu.VMEM(feat[1:], LOW),
            pltpu.VMEM((width, 2 * width), F32),
            pltpu.VMEM((2, width), F32),
            pltpu.VMEM((whole_rows, width), F32),
        ],
    )
    leave, terms = lax.optimization_barrier((leave, terms))
    come_pieces = flip(leave, "seq", 0)
    for step, bit in enumerate(high[2:]):
        omega_low, terms = split_rows(terms, "dp", [bit], dp_rows << (len(high) - 3 - step), omega_low)
    terms, come_pieces = lax.optimization_barrier(([total_of(terms)], come_pieces))
    for bit in range(axis_bits("seq") - 1, 0, -1):
        terms = [t.reshape(t.shape[0], 2, -1) for t in terms]
        side = bit_of("seq", bit)
        sent = total_of([lax.dynamic_index_in_dim(t, 1 - side, 1, keepdims=False) for t in terms]).astype(LOW)
        kept = total_of([lax.dynamic_index_in_dim(t, side, 1, keepdims=False) for t in terms])
        terms = [kept, flip(sent, "seq", bit)]
    sums = []
    for index, order in enumerate(orders):
        sums.append(scatter_halving([stay[index], come_pieces[index]], order[1:]))
    own_pair = total_of(terms)
    grad_first = own_pair[:, :group_width]
    grad_second = own_pair[:, group_width:].T
    att_grad = jnp.concatenate(sums, axis=1)
    att_grad = lax.dynamic_slice(att_grad.reshape(-1), (offset,), (shard_len,)).astype(F32)

    position = place * shard_len + jnp.arange(shard_len, dtype=jnp.int32)
    is_matrix = position < 4 * square
    rate = jnp.where(is_matrix, RATE_MATRIX, RATE_NORM)
    decay = jnp.where(is_matrix, WEIGHT_DECAY, 0.0)
    att_new, att_first_new, att_second_new = adamw(
        att_weights, att_first, att_second, att_grad, rate, decay
    )
    ffn_in_new, ffn_in_first_new, ffn_in_second_new = adamw(
        ffn_in, ffn_in_first, ffn_in_second, grad_first, RATE_MATRIX, WEIGHT_DECAY
    )
    ffn_out_new, ffn_out_first_new, ffn_out_second_new = adamw(
        ffn_out, ffn_out_first, ffn_out_second, grad_second, RATE_MATRIX, WEIGHT_DECAY
    )
    return (
        block_out,
        input_grad,
        att_new,
        att_first_new,
        att_second_new,
        att_new.astype(jnp.bfloat16),
        ffn_in_new,
        ffn_in_first_new,
        ffn_in_second_new,
        ffn_in_new.astype(jnp.bfloat16),
        ffn_out_new,
        ffn_out_first_new,
        ffn_out_second_new,
        ffn_out_new.astype(jnp.bfloat16),
    )


def solution(mesh):
    in_specs = (
        P("dp", "seq", None),
        P("dp", "seq", None),
        P("dp", "seq"),
        P(),
        P(("dp", "seq")),
        P(("dp", "seq")),
        P(("dp", "seq")),
        P("dp", "seq"),
        P("seq", "dp"),
        P("dp", "seq"),
        P("dp", "seq"),
        P("seq", "dp"),
        P("seq", "dp"),
    )
    out_specs = (
        P("dp", "seq", None),
        P("dp", "seq", None),
        P(("dp", "seq")),
        P(("dp", "seq")),
        P(("dp", "seq")),
        P(("dp", "seq")),
        P("dp", "seq"),
        P("dp", "seq"),
        P("dp", "seq"),
        P("dp", "seq"),
        P("seq", "dp"),
        P("seq", "dp"),
        P("seq", "dp"),
        P("seq", "dp"),
    )
    return jax.shard_map(shards, mesh=mesh, in_specs=in_specs, out_specs=out_specs, check_vma=False)
```

```python
import functools
import math

import jax
import jax.numpy as jnp
from jax import lax
from jax.experimental import pallas as pl
from jax.experimental.pallas import tpu as pltpu
from jax.sharding import PartitionSpec as P

CH = 256
STEP = 10
BETA_FIRST = 0.9
BETA_SECOND = 0.999
ADAM_EPS = 1e-08
WEIGHT_DECAY = 0.1
RATE_MATRIX = 0.02
RATE_NORM = 0.3
NORM_EPS = 1e-05
SPARE = 16
VMEM_LIMIT = 16 * 1024 * 1024
BIG = 1 << 20
LIMITS = {'keys': 14, 'queries': 16, 'mix': 12, 'ffn': 40, 'outer': 14, 'back_query': 24, 'back_key': 34}
F32 = jnp.float32
LOW = jnp.bfloat16


def dot_nn(left, right):
    return lax.dot_general(left, right, (((1,), (0,)), ((), ())), preferred_element_type=F32)


def dot_nt(left, right):
    return lax.dot_general(left, right, (((1,), (1,)), ((), ())), preferred_element_type=F32)


def dot_tn(left, right):
    return lax.dot_general(left, right, (((0,), (0,)), ((), ())), preferred_element_type=F32)


def norm_parts(inputs):
    centre = inputs - jnp.mean(inputs, axis=-1, keepdims=True)
    root = lax.rsqrt(jnp.mean(centre * centre, axis=-1, keepdims=True) + NORM_EPS)
    return centre * root, root


def norm_back(grad, gain, unit, root):
    inner = grad * gain
    mean_inner = jnp.mean(inner, axis=-1, keepdims=True)
    return root * (inner - mean_inner - unit * jnp.mean(inner * unit, axis=-1, keepdims=True))


def causal(length):
    earlier = lax.broadcasted_iota(jnp.int32, (length, length), 0)
    return earlier <= lax.broadcasted_iota(jnp.int32, (length, length), 1)


def put_states(own_out, their_out, core, heads, size, states, copies):
    half = heads // 2
    base = half * size
    first = core[0] == 0
    own_out[0, base:] = jnp.zeros((SPARE, own_out.shape[2]), LOW)
    their_out[0, base:] = jnp.zeros((SPARE, own_out.shape[2]), LOW)
    for index in range(half):
        low, high = states[index], states[index + half]
        total_low, total_high = [
            sum(s[size + i : size + i + 1] for i in range(copies)) for s in (low, high)
        ]
        at = slice(index * size, (index + 1) * size)
        own_out[0, at] = jnp.where(first, low[:size], high[:size]).astype(LOW)
        their_out[0, at] = jnp.where(first, high[:size], low[:size]).astype(LOW)
        row = slice(base + index, base + index + 1)
        own_out[0, row] = jnp.where(first, total_low, total_high).astype(LOW)
        their_out[0, row] = jnp.where(first, total_high, total_low).astype(LOW)


def get_state(core, keep, come, head, heads, size, copies):
    part, index = divmod(head, heads // 2)
    base = heads // 2 * size
    own = core[0] == part
    total = jnp.where(own, keep[0, base : base + SPARE], come[0, base : base + SPARE]).astype(F32)[index : index + 1]
    line = lax.broadcasted_iota(jnp.int32, (SPARE, total.shape[1]), 0)
    spare = jnp.where(line < copies, total, 0.0).astype(LOW)
    rows = slice(index * size, (index + 1) * size)
    return jnp.concatenate([jnp.where(own, keep[0, rows], come[0, rows]), spare], axis=0)


def split_features(rows, scale, shift, high_out, stack, half):
    size = rows.shape[0]
    scaled = rows * scale
    high = scaled.astype(LOW)
    rest = (scaled - high.astype(F32)).astype(LOW)
    high_out[...] = high
    for part, piece in enumerate((high, high, rest, rest)):
        stack[part * size : (part + 1) * size] = piece
    half[...] = 0.5 * jnp.sum(scaled * scaled, axis=0, keepdims=True) + shift


def staged(count, *stages):
    for stage in stages:
        for item in range(count):
            stage(item)


def keys_kernel(
    heads,
    size,
    tok,
    norms,
    weights,
    omega,
    core,
    turned_out,
    uk_out,
    value_out,
    pk_out,
    own_out,
    their_out,
    rows,
    stacks,
    halves,
    states,
):
    width = heads * size
    length = tok.shape[1]
    unit, _ = norm_parts(tok[0].astype(F32))
    turned_out[0] = (unit * norms[0:1] + norms[1:2]).astype(LOW).T
    rows[...] = dot_nn(weights[width:], turned_out[0])
    spare = (lax.broadcasted_iota(jnp.int32, (SPARE, length), 0) < 2).astype(F32).astype(LOW)
    shift = 0.5 * math.log(omega.shape[0])

    def split(head):
        at = slice(head * size, (head + 1) * size)
        split_features(
            rows[at], size ** (-0.25), shift, uk_out.at[0, at], stacks.at[head], halves.at[head : head + 1]
        )
        value_out[0, head, :size] = rows[width + head * size : width + (head + 1) * size].astype(LOW)
        value_out[0, head, size:] = spare

    def feature(head):
        projected = dot_nn(omega[...], stacks[head])
        pk_out[0, head] = jnp.exp(projected - halves[head : head + 1]).astype(LOW)

    def local_state(head):
        states[head] = dot_nt(value_out[0, head], pk_out[0, head])

    staged(heads, split, feature, local_state)
    put_states(own_out, their_out, core, heads, size, states, 1)


def queries_kernel(heads, size, turned, weights, omega, value, pk, uq_out, pq_out, pq_copy, score_out, num_out, rows, stacks, halves):
    width = heads * size
    length = turned.shape[2]
    rows[...] = dot_nn(weights[:width], turned[0])
    shift = 0.5 * math.log(omega.shape[0])
    keep = causal(length)

    def split(head):
        at = slice(head * size, (head + 1) * size)
        split_features(
            rows[at], size ** (-0.25), shift, uq_out.at[0, at], stacks.at[head], halves.at[head : head + 1]
        )

    def feature(head):
        projected = dot_nn(omega[...], stacks[head])
        feat = jnp.exp(projected - halves[head : head + 1]).astype(LOW)
        pq_out[0, head] = feat
        pq_copy[0, head] = feat

    def score(head):
        score_out[0, head] = jnp.where(keep, dot_tn(pk[0, head], pq_out[0, head]), 0.0).astype(LOW)

    def numerator(head):
        num_out[0, head] = dot_nn(value[0, head], score_out[0, head])

    staged(heads, split, feature, score, numerator)


def mix_kernel(heads, size, tok, norms, out_weight, num, core, keep, come, pq, mixed_out, recip_out, middle_out, normed_out):
    state = (core, keep, come)
    for head in range(heads):
        at = head * size
        total = num[0, head] + dot_nn(get_state(*state, head, heads, size, 2), pq[0, head])
        recip = 1.0 / total[size : size + 1]
        mixed_out[0, at : at + size] = (total[:size] * recip).astype(LOW)
        recip_out[0, head : head + 1] = recip
    mixed = mixed_out[0]
    middle = tok[0].astype(F32) + dot_tn(mixed, out_weight[...])
    middle_out[0] = middle
    unit, _ = norm_parts(middle)
    normed_out[0] = (unit * norms[2:3] + norms[3:4]).astype(LOW)


def gelu_pair(hidden):
    slope = math.sqrt(2.0 / math.pi)
    square = hidden * hidden
    tanh = jnp.tanh(hidden * (slope + (slope * 0.044715) * square))
    upper = 0.5 + 0.5 * tanh
    inner = (0.5 * slope) + (1.5 * slope * 0.044715) * square
    return hidden * upper, upper + hidden * (1.0 - tanh * tanh) * inner


def ffn_kernel(
    groups, devices, normed, middle, target, norms, pair, core, out, grad_out, leave, stay, norm_grad, first_sum, second_sum
):
    step = pl.program_id(0)
    half = pair.shape[2] // 2
    own = normed[...]
    grads = target[...]
    own_turned = own.T
    grads_turned = grads.T

    @pl.when(step == 0)
    def _():
        first_sum[...] = jnp.zeros_like(first_sum)
        second_sum[...] = jnp.zeros_like(second_sum)
        norm_grad[...] = jnp.zeros_like(norm_grad)

    result = jnp.zeros(own.shape, F32)
    grad_normed = jnp.zeros(own.shape, F32)
    for group in range(groups):
        first = pair[group, :, :half]
        second = pair[group, :, half:]
        active, slope = gelu_pair(dot_nn(own, first))
        active = active.astype(LOW)
        result = result + dot_nt(active, second)
        grad_hidden = (dot_nn(grads, second) * slope).astype(LOW)
        grad_normed = grad_normed + dot_nt(grad_hidden, first)
        first_sum[group] += dot_nn(own_turned, grad_hidden)
        second_sum[group] += dot_nn(grads_turned, active)
    rows = middle[...]
    out[...] = (rows + result).astype(LOW)
    unit, root = norm_parts(rows)
    grad_out[...] = grads.astype(F32) + norm_back(grad_normed, norms[2:3], unit, root)
    norm_grad[0:1] += jnp.sum(grad_normed * unit, axis=0, keepdims=True)
    norm_grad[1:2] += jnp.sum(grad_normed, axis=0, keepdims=True)

    @pl.when(step == pl.num_programs(0) - 1)
    def _():
        mine = core[0]
        count = normed.shape[1] // devices
        for chip in range(groups // 2):
            at = 2 * half * chip
            for side, target_ref in ((mine, stay), (1 - mine, leave)):
                for place in range(devices):
                    spot = place // 2 + (place % 2) * (devices // 2)
                    rows_in = slice(place * count, (place + 1) * count)
                    rows_out = slice(spot * count, (spot + 1) * count)
                    target_ref[rows_out, at : at + half] = first_sum[2 * chip + side, rows_in].astype(LOW)
                    target_ref[rows_out, at + half : at + 2 * half] = second_sum[2 * chip + side, rows_in].astype(LOW)


def through_omega(flow, scaled, omega_low, size):
    back = dot_nn(omega_low, flow)
    return ((back[:size] - scaled.astype(F32) * back[size : size + 1]) * size ** (-0.25))


def outer_kernel(
    heads, size, grad_middle, out_weight, mixed, recip, pq, core, outer_out, own_out, their_out, out_proj, grad_mixed, states
):
    length = grad_middle.shape[1]

    @pl.when(pl.program_id(0) == 0)
    def _():
        out_proj[...] = jnp.zeros_like(out_proj)

    grad_low = grad_middle[0].astype(LOW)
    grad_mixed[...] = dot_nt(out_weight[...], grad_low)
    out_proj[...] += dot_nn(mixed[0], grad_low)
    line = lax.broadcasted_iota(jnp.int32, (SPARE, length), 0)

    def scale(head):
        at = head * size
        outer = grad_mixed[at : at + size] * recip[0, head : head + 1]
        centre = -jnp.sum(outer * mixed[0, at : at + size].astype(F32), axis=0, keepdims=True)
        rest = centre - centre.astype(LOW).astype(F32)
        outer_out[0, head, :size] = outer.astype(LOW)
        outer_out[0, head, size:] = jnp.where(line == 0, centre, jnp.where(line == 1, rest, 0.0)).astype(LOW)

    def local_state(head):
        states[head] = dot_nt(outer_out[0, head], pq[0, head])

    staged(heads, scale, local_state)
    put_states(own_out, their_out, core, heads, size, states, 2)


def back_query_kernel(
    heads,
    size,
    turned,
    omega_low,
    outers,
    value,
    pq,
    pk,
    scores,
    core,
    keep_state,
    come_state,
    uq,
    uk,
    query_out,
    key_out,
    value_out,
    query_weight,
    befores,
    grad_scores,
    flows,
    key_flows,
):
    @pl.when(pl.program_id(0) == 0)
    def _():
        query_weight[...] = jnp.zeros_like(query_weight)

    keep = causal(turned.shape[2])

    def score(head):
        befores[head] = get_state(core, keep_state, come_state, head, heads, size, 2)
        grad_scores[head] = jnp.where(keep, dot_tn(value[0, head], outers[0, head]), 0.0).astype(LOW)

    def feature(head):
        at = head * size
        grad_feat = dot_nn(pk[0, head], grad_scores[head]) + dot_tn(befores[head], outers[0, head])
        flows[head] = (grad_feat * pq[0, head].astype(F32)).astype(LOW)
        grad_key_feat = dot_nt(pq[0, head], grad_scores[head])
        key_flows[head] = (grad_key_feat * pk[0, head].astype(F32)).astype(LOW)
        value_out[0, at : at + size] = dot_nt(outers[0, head], scores[0, head])[:size].astype(LOW)

    def query(head):
        at = head * size
        query_out[0, at : at + size] = through_omega(flows[head], uq[0, at : at + size], omega_low[...], size).astype(
            LOW
        )
        key_out[0, at : at + size] = through_omega(key_flows[head], uk[0, at : at + size], omega_low[...], size).astype(LOW)

    staged(heads, score, feature, query)
    query_weight[...] += dot_nt(turned[0], query_out[0])


def back_key_kernel(
    heads,
    size,
    layout,
    tok,
    norms,
    grad_middle,
    weights,
    omega_low,
    value,
    pk,
    core,
    keep_state,
    come_state,
    uk,
    query_grad,
    key_part,
    value_part,
    query_weight,
    out_proj,
    norm_two,
    turned,
    input_grad,
    leave,
    stay_left,
    stay_right,
    flat,
    laters,
    flows,
    pair_weight,
    norm_grad,
    whole,
):
    width = heads * size

    @pl.when(pl.program_id(0) == 0)
    def _():
        pair_weight[...] = jnp.zeros_like(pair_weight)
        norm_grad[...] = jnp.zeros_like(norm_grad)

    unit, root = norm_parts(tok[0].astype(F32))
    flat[:width] = query_grad[0]

    def later(head):
        laters[head] = get_state(core, keep_state, come_state, head, heads, size, 1)

    def feature(head):
        at = 2 * width + head * size
        grad_feat = dot_tn(laters[head], value[0, head])
        flows[head] = (grad_feat * pk[0, head].astype(F32)).astype(LOW)
        extra = dot_nn(laters[head], pk[0, head])[:size]
        flat[at : at + size] = (
            value_part[0, head * size : (head + 1) * size].astype(F32) + extra
        ).astype(LOW)

    def key(head):
        at = width + head * size
        part = slice(head * size, (head + 1) * size)
        total = key_part[0, part].astype(F32) + through_omega(flows[head], uk[0, part], omega_low[...], size)
        flat[at : at + size] = total.astype(LOW)

    staged(heads, later, feature, key)
    pair_weight[...] += dot_nt(turned[0], flat[width:])
    grad_normed = dot_tn(flat[...], weights[...])
    input_grad[0] = grad_middle[0] + norm_back(grad_normed, norms[0:1], unit, root)
    norm_grad[0:1] += jnp.sum(grad_normed * unit, axis=0, keepdims=True)
    norm_grad[1:2] += jnp.sum(grad_normed, axis=0, keepdims=True)

    @pl.when(pl.program_id(0) == pl.num_programs(0) - 1)
    def _():
        whole[:width] = query_weight[...]
        whole[width : 2 * width] = pair_weight[:, :width]
        whole[2 * width : 3 * width] = pair_weight[:, width:]
        whole[3 * width : 4 * width] = out_proj[...]
        whole[4 * width : 4 * width + 2] = norm_grad[...]
        whole[4 * width + 2 : 4 * width + 4] = norm_two[...]
        starts, rows, owners = layout
        half = width // 2
        first = core[0] == 0
        leave[...] = jnp.zeros_like(leave)
        for part, stay in enumerate((stay_left, stay_right)):
            count = leave.shape[1]
            stay[...] = jnp.zeros_like(stay)
            columns = slice(part * half, (part + 1) * half)
            for spot in range(count):
                low = starts[owners[part][spot]]
                high = starts[owners[part][spot + count]]
                low = whole[low : low + rows, columns]
                high = whole[high : high + rows, columns]
                stay[spot, :rows] = jnp.where(first, low, high)
                leave[part, spot, :rows] = jnp.where(first, high, low).astype(LOW)


def per_seq(shape, offset=0):
    rest = tuple(shape[1:])
    return pl.BlockSpec((1,) + rest, lambda i: (i + offset,) + (0,) * len(rest))


def fixed(shape):
    return pl.BlockSpec(tuple(shape), lambda i: (0,) * len(shape))


def call(kernel, steps, args, in_specs, outs, out_specs, name, flops, scratch=(), aliases=None, after=(), chip=None):
    if chip is not None:
        args = tuple(
            on_chip(a) if i in chip else off_chip(a) if math.prod(a.shape) >= BIG else a for i, a in enumerate(args)
        )
    if after:
        count, body = len(args), kernel
        args = tuple(args) + tuple(after)
        in_specs = list(in_specs) + [pl.BlockSpec(memory_space=pl.ANY)] * len(after)

        def kernel(*refs):
            body(*refs[:count], *refs[count + len(after) :])

    moved = sum(math.prod(a.shape) * jnp.dtype(a.dtype).itemsize for a in list(args) + list(outs))
    return pl.pallas_call(
        kernel,
        grid=(steps,),
        in_specs=in_specs,
        out_specs=out_specs,
        out_shape=outs,
        scratch_shapes=list(scratch),
        name=name,
        input_output_aliases=aliases or {},
        compiler_params=pltpu.CompilerParams(
            dimension_semantics=("arbitrary",), vmem_limit_bytes=LIMITS[name] * 1024 * 1024
        ),
        cost_estimate=pl.CostEstimate(
            flops=flops, bytes_accessed=moved if flops > 1 else 1, transcendentals=0
        ),
    )(*args)


def on_chip(value):
    return pltpu.with_memory_space_constraint(value, pltpu.VMEM)


def off_chip(value):
    return pltpu.with_memory_space_constraint(value, pltpu.HBM)


def array(shape, dtype):
    return pltpu.HBM(tuple(shape), dtype)


def flip(value, axis, bit):
    return lax.ppermute(value, axis, [(i, i ^ (1 << bit)) for i in range(lax.axis_size(axis))])


def bit_of(axis, bit):
    return (lax.axis_index(axis) >> bit) & 1


def send_half(own, their, forward, tie):
    count = lax.axis_size("seq")
    beside = flip(their, "seq", 0)
    mine = (own.astype(F32) + beside.astype(F32)).astype(LOW)
    mine, tie = lax.optimization_barrier((mine, tie))
    far = None
    for step in range(1, count // 2):
        hop = 2 * step if forward else -2 * step
        pairs = [(i, i + hop) for i in range(count) if 0 <= i + hop < count]
        come = lax.ppermute(mine, "seq", pairs)
        far = come if far is None else far + come
    return beside, far, tie


def receive_half(own, beside, far, forward):
    core = bit_of("seq", 0)
    giver = (core == 0) if forward else (core == 1)
    give = (far.astype(F32) + jnp.where(giver, own.astype(F32), 0.0)).astype(LOW)
    keep = (far.astype(F32) + jnp.where(giver, 0.0, beside.astype(F32))).astype(LOW)
    return keep, flip(give, "seq", 0)


def axis_bits(axis):
    return lax.axis_size(axis).bit_length() - 1


def gather_orders():
    high = [("dp", bit) for bit in range(1, axis_bits("dp"))]
    seq_high = [("seq", bit) for bit in range(1, axis_bits("seq"))]
    near = [("dp", 0)]
    return [high + near + seq_high + [("seq", 0)], seq_high + high + near + [("seq", 0)]]


def scatter_orders():
    high = [("dp", bit) for bit in range(axis_bits("dp") - 1, 0, -1)]
    seq_high = [("seq", bit) for bit in range(axis_bits("seq") - 1, 0, -1)]
    near = [("dp", 0)]
    return [[("seq", 0)] + seq_high + near + high, [("seq", 0)] + near + high + seq_high]


def place_in(order, index):
    seq_bits = axis_bits("seq")
    spot = 0
    for axis, bit in order:
        shift = bit if axis == "seq" else bit + seq_bits
        spot = 2 * spot + ((index >> shift) & 1)
    return spot


def gather_doubling(value, order, late):
    value = value[None]
    for step, (axis, bit) in enumerate(order):
        come = flip(value, axis, bit)
        if step == 0:
            come, late = lax.optimization_barrier((come, late))
        low = bit_of(axis, bit) == 0
        value = jnp.concatenate([jnp.where(low, value, come), jnp.where(low, come, value)], axis=0)
    return value, late


def total_of(terms):
    return sum(term.astype(F32) for term in terms)


def scatter_step(terms, axis, bit, late=None):
    mine = bit_of(axis, bit)
    leave = total_of([lax.dynamic_index_in_dim(term, 1 - mine, 0, keepdims=False) for term in terms]).astype(LOW)
    if late is not None:
        leave, late = lax.optimization_barrier((leave, late))
    come = flip(leave, axis, bit)
    stay = total_of([lax.dynamic_index_in_dim(term, mine, 0, keepdims=False) for term in terms])
    return [stay, come], late


def split_rows(terms, axis, bits, low, tie):
    ways = 1 << len(bits)
    terms = [t.reshape(-1, ways, low, t.shape[1]) for t in terms]
    shift = min(bits)
    mine = (lax.axis_index(axis) >> shift) & (ways - 1)

    def part(which):
        total = total_of([lax.dynamic_index_in_dim(t, which, 1, keepdims=False) for t in terms]).astype(LOW)
        return total.reshape(-1, total.shape[-1])

    leaving = [part(mine ^ other) for other in range(1, ways)]
    leaving, tie = lax.optimization_barrier((leaving, tie))
    size = lax.axis_size(axis)
    come = [
        lax.ppermute(leave, axis, [(i, i ^ (other << shift)) for i in range(size)])
        for other, leave in enumerate(leaving, 1)
    ]
    return tie, [part(mine)] + come


def adamw(weight, first, second, grad, rate, decay):
    first_new = BETA_FIRST * first + (1.0 - BETA_FIRST) * grad
    second_new = BETA_SECOND * second + (1.0 - BETA_SECOND) * grad * grad
    first_hat = first_new / (1.0 - BETA_FIRST**STEP)
    second_hat = second_new / (1.0 - BETA_SECOND**STEP)
    weight_new = weight - rate * (first_hat / (jnp.sqrt(second_hat) + ADAM_EPS) + decay * weight)
    return (weight_new, first_new, second_new)


def unpack_kernel(starts, spots, rows, left, right, wide_out, out_weight, norms, whole):
    whole[...] = jnp.zeros_like(whole)
    half = left.shape[2]
    for index, start in enumerate(starts):
        whole[start : start + rows, :half] += left[spots[0][index], :rows].astype(F32)
        whole[start : start + rows, half:] += right[spots[1][index], :rows].astype(F32)
    width = out_weight.shape[0]
    for part in range(3):
        wide_out[part * width : (part + 1) * width] = whole[part * width : (part + 1) * width].astype(LOW).T
    out_weight[...] = whole[3 * width : 4 * width].astype(LOW)
    norms[...] = whole[4 * width : 4 * width + 4]


def shards(
    tokens,
    cotangent,
    masked,
    omega,
    att_weights,
    att_first,
    att_second,
    ffn_in,
    ffn_out,
    ffn_in_first,
    ffn_in_second,
    ffn_out_first,
    ffn_out_second,
):
    seqs, length, width = tokens.shape
    size, count = omega.shape
    heads = width // size
    square = width * width
    groups = lax.axis_size("seq")
    devices = lax.axis_size("dp") * groups
    shard_len = att_weights.shape[0]
    place = lax.axis_index(("dp", "seq"))
    starts = [(i * shard_len) // width for i in range(devices)]
    offsets = [(i * shard_len) % width for i in range(devices)]
    rows = -(-(max(offsets) + shard_len) // width)
    held_rows = -(-rows // 8) * 8
    offset = (place * shard_len) % width

    framed = lax.dynamic_update_slice(
        jnp.zeros((held_rows * width,), LOW), att_weights.astype(LOW), (offset,)
    ).reshape(held_rows, width)
    group_width = ffn_in.shape[1]
    ffn_pair = (ffn_in, ffn_out)
    halves = [framed[:, : width // 2], framed[:, width // 2 :]]
    gathered = []
    for half, order in zip(halves, gather_orders()):
        whole, ffn_pair = gather_doubling(half, order, ffn_pair)
        gathered.append(whole)
    spots = [[place_in(order[::-1], i) for i in range(devices)] for order in gather_orders()]
    whole_rows = -(-(starts[-1] + rows) // 8) * 8
    group_width = ffn_in.shape[1]
    pair = jnp.concatenate([ffn_pair[0].astype(LOW), ffn_pair[1].astype(LOW).T], axis=1)
    pair = lax.all_gather(pair, ("seq", "dp"), axis=0, tiled=True)
    pair = pair.reshape(groups, width, 2 * group_width)

    weights, out_weight, norms = pl.pallas_call(
        functools.partial(unpack_kernel, starts, spots, rows),
        out_shape=[pltpu.VMEM((3 * width, width), LOW), pltpu.VMEM((width, width), LOW), pltpu.VMEM((4, width), F32)],
        scratch_shapes=[pltpu.VMEM((whole_rows, width), F32)],
        name="unpack",
        compiler_params=pltpu.CompilerParams(vmem_limit_bytes=VMEM_LIMIT),
    )(*gathered)

    first_shape = (width, groups * group_width)
    target = (cotangent.astype(F32) * masked.astype(F32)[:, :, None]).astype(LOW)
    omega_high = lax.reduce_precision(omega, 8, 7)
    omega_rest = omega - omega_high
    omega_parts = jnp.concatenate([omega_high, omega_rest, omega_high, omega_rest], axis=0).T.astype(LOW)
    omega_low = jnp.concatenate(
        [omega, jnp.ones((1, count), F32), jnp.zeros((SPARE - 1, count), F32)], axis=0
    ).astype(LOW)

    ext = size + SPARE
    unit = 2 * heads * length * length * length * seqs
    flat = (seqs, width, length)
    feat = (seqs, heads, count, length)
    held = (seqs, heads, ext, length)
    score_shape = (seqs, heads, length, length)
    recip_shape = (seqs, heads, length)
    state_rows = heads // 2 * size + SPARE
    state_shape = (seqs, state_rows, count)
    core = bit_of("seq", 0).astype(jnp.int32).reshape(1)
    in_smem = pl.BlockSpec(memory_space=pltpu.SMEM)

    def spec(value):
        return per_seq(value.shape) if value.shape[0] == seqs else fixed(value.shape)

    def scratch_rows(parts):
        return [
            pltpu.VMEM((parts * width, length), F32),
            pltpu.VMEM((heads, 4 * size, length), LOW),
            pltpu.VMEM((heads, length), F32),
        ]

    args = (tokens, norms, weights, omega_parts)
    outs = [array(flat, LOW)] * 2 + [array(held, LOW), pltpu.VMEM(feat, LOW)] + [pltpu.VMEM(state_shape, LOW)] * 2
    turned, uk, value, pk, own, their = call(
        functools.partial(keys_kernel, heads, size),
        seqs,
        args + (core,),
        [spec(a) for a in args] + [in_smem],
        outs,
        [spec(a) for a in outs],
        "keys",
        1,
        chip=(),
        scratch=scratch_rows(2) + [pltpu.VMEM((heads, ext, count), F32)],
    )
    beside, far, omega_tied = send_half(own, their, True, omega_parts)
    args = (turned, weights, omega_tied, value, pk)
    outs = [array(flat, LOW), pltpu.VMEM(feat, LOW), array(feat, LOW), array(score_shape, LOW), pltpu.VMEM(held, F32)]
    uq, pq_near, pq, score, num = call(
        functools.partial(queries_kernel, heads, size),
        seqs,
        args,
        [spec(a) for a in args],
        outs,
        [spec(a) for a in outs],
        "queries",
        1,
        scratch_rows(1),
        chip=(4,),
    )
    far, uq, target = lax.optimization_barrier((far, uq, target))
    keep, come = receive_half(own, beside, far, True)
    states = [per_seq(keep.shape)] * 2
    outs = [array(flat, LOW), array(recip_shape, F32), array(tokens.shape, F32), array(tokens.shape, LOW)]
    mixed, recip, middle, normed_two = call(
        functools.partial(mix_kernel, heads, size),
        seqs,
        (tokens, norms, out_weight, num, core, keep, come, pq_near),
        [spec(tokens), spec(norms), spec(out_weight), spec(num), in_smem, *states, spec(pq_near)],
        outs,
        [spec(a) for a in outs],
        "mix",
        1,
        chip=(3, 7),
    )

    total_rows = seqs * length
    block = 2 * length
    by_block = pl.BlockSpec((block, width), lambda i: (i, 0))
    rows_shape = (total_rows, width)
    block_out, grad_middle, leave, stay, norm_two_grad = call(
        functools.partial(ffn_kernel, groups, lax.axis_size("dp")),
        total_rows // block,
        (*[a.reshape(rows_shape) for a in (normed_two, middle, target)], norms, pair, core),
        [by_block, by_block, by_block, fixed(norms.shape), fixed(pair.shape), in_smem],
        [array(rows_shape, LOW), array(rows_shape, F32)] + [array(first_shape, LOW)] * 2 + [array((2, width), F32)],
        [by_block, by_block, fixed(first_shape), fixed(first_shape), fixed((2, width))],
        "ffn",
        20 * unit,
        chip=(),
        scratch=[pltpu.VMEM((groups, width, group_width), F32)] * 2,
    )
    block_out = block_out.reshape(tokens.shape)
    grad_middle = grad_middle.reshape(tokens.shape)
    come_pair = flip(leave, "seq", 0)

    args = (grad_middle, out_weight, mixed, recip, pq)
    outs = [array(held, LOW)] + [pltpu.VMEM(state_shape, LOW)] * 2
    outs = outs + [array((width, width), F32)]
    outers, own, their, out_proj = call(
        functools.partial(outer_kernel, heads, size),
        seqs,
        args + (core,),
        [spec(a) for a in args] + [in_smem],
        outs,
        [spec(a) for a in outs],
        "outer",
        1,
        chip=(),
        scratch=[pltpu.VMEM((width, length), F32), pltpu.VMEM((heads, ext, count), F32)],
    )
    their, come_pair = lax.optimization_barrier((their, come_pair))
    dp_rows = width // lax.axis_size("dp")
    columns = stay.shape[1]
    near = bit_of("dp", 0)
    sent = total_of(
        [lax.dynamic_index_in_dim(t.reshape(2, width // 2, columns), 1 - near, 0, keepdims=False) for t in (stay, come_pair)]
    ).astype(LOW)
    sent, omega_low = lax.optimization_barrier((sent, omega_low))
    come_near = flip(sent, "dp", 0)
    beside, far, omega_low = send_half(own, their, False, omega_low)
    args = (turned, omega_low, outers, value, pq, pk, score, core, keep, come, uq, uk)
    outs = [array(flat, LOW)] * 3
    query_grad, key_part, value_part, query_weight = call(
        functools.partial(back_query_kernel, heads, size),
        seqs,
        args,
        [spec(a) for a in args[:7]] + [in_smem, *states, spec(uq), spec(uk)],
        outs + [array((width, width), F32)],
        [spec(a) for a in outs] + [fixed((width, width))],
        "back_query",
        1,
        chip=(),
        scratch=[
            pltpu.VMEM((heads, ext, count), LOW),
            pltpu.VMEM(score_shape[1:], LOW),
            pltpu.VMEM(feat[1:], LOW),
            pltpu.VMEM(feat[1:], LOW),
        ],
    )
    far, query_grad = lax.optimization_barrier((far, query_grad))
    keep, come = receive_half(own, beside, far, False)
    high = list(range(axis_bits("dp") - 1, 0, -1))
    ways = 1 << len(high[:2])
    low = width // 2 // ways
    chosen = (lax.axis_index("dp") >> (high[0] + 1 - len(high[:2]))) & (ways - 1)

    def part(which):
        pieces = [
            lax.dynamic_slice(t.reshape(2, ways, low, columns), (near, which, 0, 0), (1, 1, low, columns))
            for t in (stay, come_pair)
        ]
        pieces.append(lax.dynamic_index_in_dim(come_near.reshape(ways, low, columns), which, 0))
        return total_of([p.reshape(low, columns) for p in pieces]).astype(LOW)

    leaving = [part(chosen ^ other) for other in range(1, ways)]
    leaving, omega_low = lax.optimization_barrier((leaving, omega_low))
    terms = [part(chosen)]
    for other, leave_part in enumerate(leaving, 1):
        jump = other << (high[0] + 1 - len(high[:2]))
        terms.append(lax.ppermute(leave_part, "dp", [(i, i ^ jump) for i in range(lax.axis_size("dp"))]))
    orders = scatter_orders()
    owners = [sorted(range(devices), key=lambda i: place_in(order, i)) for order in orders]
    piece_shape = (2, devices // 2, held_rows, width // 2)
    args = (tokens, norms, grad_middle, weights, omega_low, value, pk, core, keep, come)
    more = (uk, query_grad, key_part, value_part, query_weight, out_proj, norm_two_grad, turned)
    input_grad, leave, *stays = call(
        functools.partial(back_key_kernel, heads, size, (starts, rows, owners)),
        seqs,
        args + more,
        [spec(a) for a in args[:7]] + [in_smem, *states] + [spec(a) for a in more],
        [array(tokens.shape, F32), array(piece_shape, LOW)] + [array(piece_shape[1:], F32)] * 2,
        [per_seq(tokens.shape), fixed(piece_shape)] + [fixed(piece_shape[1:])] * 2,
        "back_key",
        7 * unit,
        chip=(),
        scratch=[
            pltpu.VMEM((3 * width, length), LOW),
            pltpu.VMEM((heads, ext, count), LOW),
            pltpu.VMEM(feat[1:], LOW),
            pltpu.VMEM((width, 2 * width), F32),
            pltpu.VMEM((2, width), F32),
            pltpu.VMEM((whole_rows, width), F32),
        ],
    )
    leave, terms = lax.optimization_barrier((leave, terms))
    come_pieces = flip(leave, "seq", 0)
    for step, bit in enumerate(high[2:]):
        omega_low, terms = split_rows(terms, "dp", [bit], dp_rows << (len(high) - 3 - step), omega_low)
    sums = []
    for index, (stay, order) in enumerate(zip(stays, orders)):
        part = [stay, come_pieces[index]]
        for step, (axis, bit) in enumerate(order[1:]):
            part = [t.reshape((2, t.shape[0] // 2) + t.shape[1:]) for t in part]
            if index == 0 and step == 1:
                part, terms = scatter_step(part, axis, bit, terms)
            else:
                part, _ = scatter_step(part, axis, bit)
        sums.append(total_of(part)[0])
    terms = [total_of(terms)]
    for bit in range(axis_bits("seq") - 1, 0, -1):
        terms = [t.reshape(t.shape[0], 2, -1) for t in terms]
        side = bit_of("seq", bit)
        sent = total_of([lax.dynamic_index_in_dim(t, 1 - side, 1, keepdims=False) for t in terms]).astype(LOW)
        kept = total_of([lax.dynamic_index_in_dim(t, side, 1, keepdims=False) for t in terms])
        terms = [kept, flip(sent, "seq", bit)]
    own_pair = total_of(terms)
    grad_first = own_pair[:, :group_width]
    grad_second = own_pair[:, group_width:].T
    att_grad = jnp.concatenate(sums, axis=1)
    att_grad = lax.dynamic_slice(att_grad.reshape(-1), (offset,), (shard_len,)).astype(F32)

    position = place * shard_len + jnp.arange(shard_len, dtype=jnp.int32)
    is_matrix = position < 4 * square
    rate = jnp.where(is_matrix, RATE_MATRIX, RATE_NORM)
    decay = jnp.where(is_matrix, WEIGHT_DECAY, 0.0)
    att_new, att_first_new, att_second_new = adamw(
        att_weights, att_first, att_second, att_grad, rate, decay
    )
    ffn_in_new, ffn_in_first_new, ffn_in_second_new = adamw(
        ffn_in, ffn_in_first, ffn_in_second, grad_first, RATE_MATRIX, WEIGHT_DECAY
    )
    ffn_out_new, ffn_out_first_new, ffn_out_second_new = adamw(
        ffn_out, ffn_out_first, ffn_out_second, grad_second, RATE_MATRIX, WEIGHT_DECAY
    )
    return (
        block_out,
        input_grad,
        att_new,
        att_first_new,
        att_second_new,
        att_new.astype(jnp.bfloat16),
        ffn_in_new,
        ffn_in_first_new,
        ffn_in_second_new,
        ffn_in_new.astype(jnp.bfloat16),
        ffn_out_new,
        ffn_out_first_new,
        ffn_out_second_new,
        ffn_out_new.astype(jnp.bfloat16),
    )


def solution(mesh):
    in_specs = (
        P("dp", "seq", None),
        P("dp", "seq", None),
        P("dp", "seq"),
        P(),
        P(("dp", "seq")),
        P(("dp", "seq")),
        P(("dp", "seq")),
        P("dp", "seq"),
        P("seq", "dp"),
        P("dp", "seq"),
        P("dp", "seq"),
        P("seq", "dp"),
        P("seq", "dp"),
    )
    out_specs = (
        P("dp", "seq", None),
        P("dp", "seq", None),
        P(("dp", "seq")),
        P(("dp", "seq")),
        P(("dp", "seq")),
        P(("dp", "seq")),
        P("dp", "seq"),
        P("dp", "seq"),
        P("dp", "seq"),
        P("dp", "seq"),
        P("seq", "dp"),
        P("seq", "dp"),
        P("seq", "dp"),
        P("seq", "dp"),
    )
    return jax.shard_map(shards, mesh=mesh, in_specs=in_specs, out_specs=out_specs, check_vma=False)
```

```python
import functools
import math

import jax
import jax.numpy as jnp
from jax import lax
from jax.experimental import pallas as pl
from jax.experimental.pallas import tpu as pltpu
from jax.sharding import PartitionSpec as P

CH = 256
STEP = 10
BETA_FIRST = 0.9
BETA_SECOND = 0.999
ADAM_EPS = 1e-08
WEIGHT_DECAY = 0.1
RATE_MATRIX = 0.02
RATE_NORM = 0.3
NORM_EPS = 1e-05
SPARE = 16
VMEM_LIMIT = 16 * 1024 * 1024
BIG = 1 << 20
LIMITS = {'keys': 14, 'queries': 16, 'mix': 12, 'ffn': 44, 'outer': 14, 'back_query': 24, 'back_key': 34}
F32 = jnp.float32
LOW = jnp.bfloat16


def dot_nn(left, right):
    return lax.dot_general(left, right, (((1,), (0,)), ((), ())), preferred_element_type=F32)


def dot_nt(left, right):
    return lax.dot_general(left, right, (((1,), (1,)), ((), ())), preferred_element_type=F32)


def dot_tn(left, right):
    return lax.dot_general(left, right, (((0,), (0,)), ((), ())), preferred_element_type=F32)


def norm_parts(inputs):
    centre = inputs - jnp.mean(inputs, axis=-1, keepdims=True)
    root = lax.rsqrt(jnp.mean(centre * centre, axis=-1, keepdims=True) + NORM_EPS)
    return centre * root, root


def norm_back(grad, gain, unit, root):
    inner = grad * gain
    mean_inner = jnp.mean(inner, axis=-1, keepdims=True)
    return root * (inner - mean_inner - unit * jnp.mean(inner * unit, axis=-1, keepdims=True))


def causal(length):
    earlier = lax.broadcasted_iota(jnp.int32, (length, length), 0)
    return earlier <= lax.broadcasted_iota(jnp.int32, (length, length), 1)


def put_states(own_out, their_out, core, heads, size, states, copies):
    half = heads // 2
    base = half * size
    first = core[0] == 0
    own_out[0, base:] = jnp.zeros((SPARE, own_out.shape[2]), LOW)
    their_out[0, base:] = jnp.zeros((SPARE, own_out.shape[2]), LOW)
    for index in range(half):
        low, high = states[index], states[index + half]
        total_low, total_high = [
            sum(s[size + i : size + i + 1] for i in range(copies)) for s in (low, high)
        ]
        at = slice(index * size, (index + 1) * size)
        own_out[0, at] = jnp.where(first, low[:size], high[:size]).astype(LOW)
        their_out[0, at] = jnp.where(first, high[:size], low[:size]).astype(LOW)
        row = slice(base + index, base + index + 1)
        own_out[0, row] = jnp.where(first, total_low, total_high).astype(LOW)
        their_out[0, row] = jnp.where(first, total_high, total_low).astype(LOW)


def get_state(core, keep, come, head, heads, size, copies):
    part, index = divmod(head, heads // 2)
    base = heads // 2 * size
    own = core[0] == part
    total = jnp.where(own, keep[0, base : base + SPARE], come[0, base : base + SPARE]).astype(F32)[index : index + 1]
    line = lax.broadcasted_iota(jnp.int32, (SPARE, total.shape[1]), 0)
    spare = jnp.where(line < copies, total, 0.0).astype(LOW)
    rows = slice(index * size, (index + 1) * size)
    return jnp.concatenate([jnp.where(own, keep[0, rows], come[0, rows]), spare], axis=0)


def split_features(rows, scale, shift, high_out, stack, half):
    size = rows.shape[0]
    scaled = rows * scale
    high = scaled.astype(LOW)
    rest = (scaled - high.astype(F32)).astype(LOW)
    high_out[...] = high
    for part, piece in enumerate((high, high, rest, rest)):
        stack[part * size : (part + 1) * size] = piece
    half[...] = 0.5 * jnp.sum(scaled * scaled, axis=0, keepdims=True) + shift


def staged(count, *stages):
    for stage in stages:
        for item in range(count):
            stage(item)


def keys_kernel(
    heads,
    size,
    tok,
    norms,
    weights,
    omega,
    core,
    turned_out,
    uk_out,
    value_out,
    pk_out,
    own_out,
    their_out,
    rows,
    stacks,
    halves,
    states,
):
    width = heads * size
    length = tok.shape[1]
    unit, _ = norm_parts(tok[0].astype(F32))
    turned_out[0] = (unit * norms[0:1] + norms[1:2]).astype(LOW).T
    rows[...] = dot_nn(weights[width:], turned_out[0])
    spare = (lax.broadcasted_iota(jnp.int32, (SPARE, length), 0) < 2).astype(F32).astype(LOW)
    shift = 0.5 * math.log(omega.shape[0])

    def split(head):
        at = slice(head * size, (head + 1) * size)
        split_features(
            rows[at], size ** (-0.25), shift, uk_out.at[0, at], stacks.at[head], halves.at[head : head + 1]
        )
        value_out[0, head, :size] = rows[width + head * size : width + (head + 1) * size].astype(LOW)
        value_out[0, head, size:] = spare

    def feature(head):
        projected = dot_nn(omega[...], stacks[head])
        pk_out[0, head] = jnp.exp(projected - halves[head : head + 1]).astype(LOW)

    def local_state(head):
        states[head] = dot_nt(value_out[0, head], pk_out[0, head])

    staged(heads, split, feature, local_state)
    put_states(own_out, their_out, core, heads, size, states, 1)


def queries_kernel(heads, size, turned, weights, omega, value, pk, uq_out, pq_out, pq_copy, score_out, num_out, rows, stacks, halves):
    width = heads * size
    length = turned.shape[2]
    rows[...] = dot_nn(weights[:width], turned[0])
    shift = 0.5 * math.log(omega.shape[0])
    keep = causal(length)

    def split(head):
        at = slice(head * size, (head + 1) * size)
        split_features(
            rows[at], size ** (-0.25), shift, uq_out.at[0, at], stacks.at[head], halves.at[head : head + 1]
        )

    def feature(head):
        projected = dot_nn(omega[...], stacks[head])
        feat = jnp.exp(projected - halves[head : head + 1]).astype(LOW)
        pq_out[0, head] = feat
        pq_copy[0, head] = feat

    def score(head):
        score_out[0, head] = jnp.where(keep, dot_tn(pk[0, head], pq_out[0, head]), 0.0).astype(LOW)

    def numerator(head):
        num_out[0, head] = dot_nn(value[0, head], score_out[0, head])

    staged(heads, split, feature, score, numerator)


def mix_kernel(heads, size, tok, norms, out_weight, num, core, keep, come, pq, mixed_out, recip_out, middle_out, normed_out):
    state = (core, keep, come)
    for head in range(heads):
        at = head * size
        total = num[0, head] + dot_nn(get_state(*state, head, heads, size, 2), pq[0, head])
        recip = 1.0 / total[size : size + 1]
        mixed_out[0, at : at + size] = (total[:size] * recip).astype(LOW)
        recip_out[0, head : head + 1] = recip
    mixed = mixed_out[0]
    middle = tok[0].astype(F32) + dot_tn(mixed, out_weight[...])
    middle_out[0] = middle
    unit, _ = norm_parts(middle)
    normed_out[0] = (unit * norms[2:3] + norms[3:4]).astype(LOW)


def gelu_pair(hidden):
    slope = math.sqrt(2.0 / math.pi)
    square = hidden * hidden
    tanh = jnp.tanh(hidden * (slope + (slope * 0.044715) * square))
    upper = 0.5 + 0.5 * tanh
    inner = (0.5 * slope) + (1.5 * slope * 0.044715) * square
    return hidden * upper, upper + hidden * (1.0 - tanh * tanh) * inner


def ffn_kernel(
    groups,
    devices,
    found,
    normed,
    middle,
    target,
    norms,
    own_pair,
    their_pair,
    core,
    place,
    out,
    grad_out,
    leave,
    stay,
    norm_grad,
    first_sum,
    second_sum,
    pair,
):
    step = pl.program_id(0)
    half = pair.shape[3] // 2
    width = normed.shape[1]

    @pl.when(step == 0)
    def _():
        for index, (seq_jump, dp_jump) in enumerate(found):
            pair[place[0] ^ seq_jump, place[1] ^ dp_jump] = own_pair[index]
            pair[place[0] ^ (seq_jump ^ 1), place[1] ^ dp_jump] = their_pair[index]

    own = normed[...]
    grads = target[...]
    own_turned = own.T
    grads_turned = grads.T

    @pl.when(step == 0)
    def _():
        first_sum[...] = jnp.zeros_like(first_sum)
        second_sum[...] = jnp.zeros_like(second_sum)
        norm_grad[...] = jnp.zeros_like(norm_grad)

    result = jnp.zeros(own.shape, F32)
    grad_normed = jnp.zeros(own.shape, F32)
    for group in range(groups):
        first = pair[group, :, :, :half].reshape(width, half)
        second = pair[group, :, :, half:].reshape(width, half)
        active, slope = gelu_pair(dot_nn(own, first))
        active = active.astype(LOW)
        result = result + dot_nt(active, second)
        grad_hidden = (dot_nn(grads, second) * slope).astype(LOW)
        grad_normed = grad_normed + dot_nt(grad_hidden, first)
        first_sum[group] += dot_nn(own_turned, grad_hidden)
        second_sum[group] += dot_nn(grads_turned, active)
    rows = middle[...]
    out[...] = (rows + result).astype(LOW)
    unit, root = norm_parts(rows)
    grad_out[...] = grads.astype(F32) + norm_back(grad_normed, norms[2:3], unit, root)
    norm_grad[0:1] += jnp.sum(grad_normed * unit, axis=0, keepdims=True)
    norm_grad[1:2] += jnp.sum(grad_normed, axis=0, keepdims=True)

    @pl.when(step == pl.num_programs(0) - 1)
    def _():
        mine = core[0]
        count = normed.shape[1] // devices
        for chip in range(groups // 2):
            at = 2 * half * chip
            for side, target_ref in ((mine, stay), (1 - mine, leave)):
                for place in range(devices):
                    spot = place // 2 + (place % 2) * (devices // 2)
                    rows_in = slice(place * count, (place + 1) * count)
                    rows_out = slice(spot * count, (spot + 1) * count)
                    target_ref[rows_out, at : at + half] = first_sum[2 * chip + side, rows_in].astype(LOW)
                    target_ref[rows_out, at + half : at + 2 * half] = second_sum[2 * chip + side, rows_in].astype(LOW)


def through_omega(flow, scaled, omega_low, size):
    back = dot_nn(omega_low, flow)
    return ((back[:size] - scaled.astype(F32) * back[size : size + 1]) * size ** (-0.25))


def outer_kernel(
    heads, size, grad_middle, out_weight, mixed, recip, pq, core, outer_out, own_out, their_out, out_proj, grad_mixed, states
):
    length = grad_middle.shape[1]

    @pl.when(pl.program_id(0) == 0)
    def _():
        out_proj[...] = jnp.zeros_like(out_proj)

    grad_low = grad_middle[0].astype(LOW)
    grad_mixed[...] = dot_nt(out_weight[...], grad_low)
    out_proj[...] += dot_nn(mixed[0], grad_low)
    line = lax.broadcasted_iota(jnp.int32, (SPARE, length), 0)

    def scale(head):
        at = head * size
        outer = grad_mixed[at : at + size] * recip[0, head : head + 1]
        centre = -jnp.sum(outer * mixed[0, at : at + size].astype(F32), axis=0, keepdims=True)
        rest = centre - centre.astype(LOW).astype(F32)
        outer_out[0, head, :size] = outer.astype(LOW)
        outer_out[0, head, size:] = jnp.where(line == 0, centre, jnp.where(line == 1, rest, 0.0)).astype(LOW)

    def local_state(head):
        states[head] = dot_nt(outer_out[0, head], pq[0, head])

    staged(heads, scale, local_state)
    put_states(own_out, their_out, core, heads, size, states, 2)


def back_query_kernel(
    heads,
    size,
    turned,
    omega_low,
    outers,
    value,
    pq,
    pk,
    scores,
    core,
    keep_state,
    come_state,
    uq,
    uk,
    query_out,
    key_out,
    value_out,
    query_weight,
    befores,
    grad_scores,
    flows,
    key_flows,
):
    @pl.when(pl.program_id(0) == 0)
    def _():
        query_weight[...] = jnp.zeros_like(query_weight)

    keep = causal(turned.shape[2])

    def score(head):
        befores[head] = get_state(core, keep_state, come_state, head, heads, size, 2)
        grad_scores[head] = jnp.where(keep, dot_tn(value[0, head], outers[0, head]), 0.0).astype(LOW)

    def feature(head):
        at = head * size
        grad_feat = dot_nn(pk[0, head], grad_scores[head]) + dot_tn(befores[head], outers[0, head])
        flows[head] = (grad_feat * pq[0, head].astype(F32)).astype(LOW)
        grad_key_feat = dot_nt(pq[0, head], grad_scores[head])
        key_flows[head] = (grad_key_feat * pk[0, head].astype(F32)).astype(LOW)
        value_out[0, at : at + size] = dot_nt(outers[0, head], scores[0, head])[:size].astype(LOW)

    def query(head):
        at = head * size
        query_out[0, at : at + size] = through_omega(flows[head], uq[0, at : at + size], omega_low[...], size).astype(
            LOW
        )
        key_out[0, at : at + size] = through_omega(key_flows[head], uk[0, at : at + size], omega_low[...], size).astype(LOW)

    staged(heads, score, feature, query)
    query_weight[...] += dot_nt(turned[0], query_out[0])


def back_key_kernel(
    heads,
    size,
    layout,
    tok,
    norms,
    grad_middle,
    weights,
    omega_low,
    value,
    pk,
    core,
    keep_state,
    come_state,
    uk,
    query_grad,
    key_part,
    value_part,
    query_weight,
    out_proj,
    norm_two,
    turned,
    input_grad,
    leave,
    stay_left,
    stay_right,
    flat,
    laters,
    flows,
    pair_weight,
    norm_grad,
    whole,
):
    width = heads * size

    @pl.when(pl.program_id(0) == 0)
    def _():
        pair_weight[...] = jnp.zeros_like(pair_weight)
        norm_grad[...] = jnp.zeros_like(norm_grad)

    unit, root = norm_parts(tok[0].astype(F32))
    flat[:width] = query_grad[0]

    def later(head):
        laters[head] = get_state(core, keep_state, come_state, head, heads, size, 1)

    def feature(head):
        at = 2 * width + head * size
        grad_feat = dot_tn(laters[head], value[0, head])
        flows[head] = (grad_feat * pk[0, head].astype(F32)).astype(LOW)
        extra = dot_nn(laters[head], pk[0, head])[:size]
        flat[at : at + size] = (
            value_part[0, head * size : (head + 1) * size].astype(F32) + extra
        ).astype(LOW)

    def key(head):
        at = width + head * size
        part = slice(head * size, (head + 1) * size)
        total = key_part[0, part].astype(F32) + through_omega(flows[head], uk[0, part], omega_low[...], size)
        flat[at : at + size] = total.astype(LOW)

    staged(heads, later, feature, key)
    pair_weight[...] += dot_nt(turned[0], flat[width:])
    grad_normed = dot_tn(flat[...], weights[...])
    input_grad[0] = grad_middle[0] + norm_back(grad_normed, norms[0:1], unit, root)
    norm_grad[0:1] += jnp.sum(grad_normed * unit, axis=0, keepdims=True)
    norm_grad[1:2] += jnp.sum(grad_normed, axis=0, keepdims=True)

    @pl.when(pl.program_id(0) == pl.num_programs(0) - 1)
    def _():
        whole[:width] = query_weight[...]
        whole[width : 2 * width] = pair_weight[:, :width]
        whole[2 * width : 3 * width] = pair_weight[:, width:]
        whole[3 * width : 4 * width] = out_proj[...]
        whole[4 * width : 4 * width + 2] = norm_grad[...]
        whole[4 * width + 2 : 4 * width + 4] = norm_two[...]
        starts, rows, owners = layout
        half = width // 2
        first = core[0] == 0
        leave[...] = jnp.zeros_like(leave)
        for part, stay in enumerate((stay_left, stay_right)):
            count = leave.shape[1]
            stay[...] = jnp.zeros_like(stay)
            columns = slice(part * half, (part + 1) * half)
            for spot in range(count):
                low = starts[owners[part][spot]]
                high = starts[owners[part][spot + count]]
                low = whole[low : low + rows, columns]
                high = whole[high : high + rows, columns]
                stay[spot, :rows] = jnp.where(first, low, high)
                leave[part, spot, :rows] = jnp.where(first, high, low).astype(LOW)


def per_seq(shape, offset=0):
    rest = tuple(shape[1:])
    return pl.BlockSpec((1,) + rest, lambda i: (i + offset,) + (0,) * len(rest))


def fixed(shape):
    return pl.BlockSpec(tuple(shape), lambda i: (0,) * len(shape))


def call(kernel, steps, args, in_specs, outs, out_specs, name, flops, scratch=(), aliases=None, after=(), chip=None):
    if chip is not None:
        args = tuple(
            on_chip(a) if i in chip else off_chip(a) if math.prod(a.shape) >= BIG else a for i, a in enumerate(args)
        )
    if after:
        count, body = len(args), kernel
        args = tuple(args) + tuple(after)
        in_specs = list(in_specs) + [pl.BlockSpec(memory_space=pl.ANY)] * len(after)

        def kernel(*refs):
            body(*refs[:count], *refs[count + len(after) :])

    moved = sum(math.prod(a.shape) * jnp.dtype(a.dtype).itemsize for a in list(args) + list(outs))
    return pl.pallas_call(
        kernel,
        grid=(steps,),
        in_specs=in_specs,
        out_specs=out_specs,
        out_shape=outs,
        scratch_shapes=list(scratch),
        name=name,
        input_output_aliases=aliases or {},
        compiler_params=pltpu.CompilerParams(
            dimension_semantics=("arbitrary",), vmem_limit_bytes=LIMITS[name] * 1024 * 1024
        ),
        cost_estimate=pl.CostEstimate(
            flops=flops, bytes_accessed=moved if flops > 1 else 1, transcendentals=0
        ),
    )(*args)


def on_chip(value):
    return pltpu.with_memory_space_constraint(value, pltpu.VMEM)


def off_chip(value):
    return pltpu.with_memory_space_constraint(value, pltpu.HBM)


def array(shape, dtype):
    return pltpu.HBM(tuple(shape), dtype)


def flip(value, axis, bit):
    return lax.ppermute(value, axis, [(i, i ^ (1 << bit)) for i in range(lax.axis_size(axis))])


def bit_of(axis, bit):
    return (lax.axis_index(axis) >> bit) & 1


def send_half(own, their, forward, tie):
    count = lax.axis_size("seq")
    beside = flip(their, "seq", 0)
    mine = (own.astype(F32) + beside.astype(F32)).astype(LOW)
    mine, tie = lax.optimization_barrier((mine, tie))
    far = None
    for step in range(1, count // 2):
        hop = 2 * step if forward else -2 * step
        pairs = [(i, i + hop) for i in range(count) if 0 <= i + hop < count]
        come = lax.ppermute(mine, "seq", pairs)
        far = come if far is None else far + come
    return beside, far, tie


def receive_half(own, beside, far, forward):
    core = bit_of("seq", 0)
    giver = (core == 0) if forward else (core == 1)
    give = (far.astype(F32) + jnp.where(giver, own.astype(F32), 0.0)).astype(LOW)
    keep = (far.astype(F32) + jnp.where(giver, 0.0, beside.astype(F32))).astype(LOW)
    return keep, flip(give, "seq", 0)


def axis_bits(axis):
    return lax.axis_size(axis).bit_length() - 1


def gather_orders():
    high = [("dp", bit) for bit in range(1, axis_bits("dp"))]
    seq_high = [("seq", bit) for bit in range(1, axis_bits("seq"))]
    near = [("dp", 0)]
    return [high + near + seq_high + [("seq", 0)], seq_high + high + near + [("seq", 0)]]


def scatter_orders():
    high = [("dp", bit) for bit in range(axis_bits("dp") - 1, 0, -1)]
    seq_high = [("seq", bit) for bit in range(axis_bits("seq") - 1, 0, -1)]
    near = [("dp", 0)]
    return [[("seq", 0)] + seq_high + near + high, [("seq", 0)] + near + high + seq_high]


def place_in(order, index):
    seq_bits = axis_bits("seq")
    spot = 0
    for axis, bit in order:
        shift = bit if axis == "seq" else bit + seq_bits
        spot = 2 * spot + ((index >> shift) & 1)
    return spot


def gather_more(value, found, axis, jumps):
    size = lax.axis_size(axis)
    come = [lax.ppermute(value, axis, [(i, i ^ jump) for i in range(size)]) for jump in jumps]
    more = list(found)
    for jump in jumps:
        more += [(a ^ jump, b) if axis == "seq" else (a, b ^ jump) for a, b in found]
    return jnp.concatenate([value] + come, axis=0), more


def gather_doubling(value, order, late):
    value = value[None]
    for step, (axis, bit) in enumerate(order):
        come = flip(value, axis, bit)
        if step == 0:
            come, late = lax.optimization_barrier((come, late))
        low = bit_of(axis, bit) == 0
        value = jnp.concatenate([jnp.where(low, value, come), jnp.where(low, come, value)], axis=0)
    return value, late


def total_of(terms):
    return sum(term.astype(F32) for term in terms)


def scatter_step(terms, axis, bit, late=None):
    mine = bit_of(axis, bit)
    leave = total_of([lax.dynamic_index_in_dim(term, 1 - mine, 0, keepdims=False) for term in terms]).astype(LOW)
    if late is not None:
        leave, late = lax.optimization_barrier((leave, late))
    come = flip(leave, axis, bit)
    stay = total_of([lax.dynamic_index_in_dim(term, mine, 0, keepdims=False) for term in terms])
    return [stay, come], late


def split_rows(terms, axis, bits, low, tie):
    ways = 1 << len(bits)
    terms = [t.reshape(-1, ways, low, t.shape[1]) for t in terms]
    shift = min(bits)
    mine = (lax.axis_index(axis) >> shift) & (ways - 1)

    def part(which):
        total = total_of([lax.dynamic_index_in_dim(t, which, 1, keepdims=False) for t in terms]).astype(LOW)
        return total.reshape(-1, total.shape[-1])

    leaving = [part(mine ^ other) for other in range(1, ways)]
    leaving, tie = lax.optimization_barrier((leaving, tie))
    size = lax.axis_size(axis)
    come = [
        lax.ppermute(leave, axis, [(i, i ^ (other << shift)) for i in range(size)])
        for other, leave in enumerate(leaving, 1)
    ]
    return tie, [part(mine)] + come


def adamw(weight, first, second, grad, rate, decay):
    first_new = BETA_FIRST * first + (1.0 - BETA_FIRST) * grad
    second_new = BETA_SECOND * second + (1.0 - BETA_SECOND) * grad * grad
    first_hat = first_new / (1.0 - BETA_FIRST**STEP)
    second_hat = second_new / (1.0 - BETA_SECOND**STEP)
    weight_new = weight - rate * (first_hat / (jnp.sqrt(second_hat) + ADAM_EPS) + decay * weight)
    return (weight_new, first_new, second_new)


def unpack_kernel(starts, spots, rows, left, right, wide_out, out_weight, norms, whole):
    whole[...] = jnp.zeros_like(whole)
    half = left.shape[2]
    for index, start in enumerate(starts):
        whole[start : start + rows, :half] += left[spots[0][index], :rows].astype(F32)
        whole[start : start + rows, half:] += right[spots[1][index], :rows].astype(F32)
    width = out_weight.shape[0]
    for part in range(3):
        wide_out[part * width : (part + 1) * width] = whole[part * width : (part + 1) * width].astype(LOW).T
    out_weight[...] = whole[3 * width : 4 * width].astype(LOW)
    norms[...] = whole[4 * width : 4 * width + 4]


def shards(
    tokens,
    cotangent,
    masked,
    omega,
    att_weights,
    att_first,
    att_second,
    ffn_in,
    ffn_out,
    ffn_in_first,
    ffn_in_second,
    ffn_out_first,
    ffn_out_second,
):
    seqs, length, width = tokens.shape
    size, count = omega.shape
    heads = width // size
    square = width * width
    groups = lax.axis_size("seq")
    devices = lax.axis_size("dp") * groups
    shard_len = att_weights.shape[0]
    place = lax.axis_index(("dp", "seq"))
    starts = [(i * shard_len) // width for i in range(devices)]
    offsets = [(i * shard_len) % width for i in range(devices)]
    rows = -(-(max(offsets) + shard_len) // width)
    held_rows = -(-rows // 8) * 8
    offset = (place * shard_len) % width

    framed = lax.dynamic_update_slice(
        jnp.zeros((held_rows * width,), LOW), att_weights.astype(LOW), (offset,)
    ).reshape(held_rows, width)
    group_width = ffn_in.shape[1]
    ffn_pair = (ffn_in, ffn_out)
    halves = [framed[:, : width // 2], framed[:, width // 2 :]]
    gathered = []
    for half, order in zip(halves, gather_orders()):
        whole, ffn_pair = gather_doubling(half, order, ffn_pair)
        gathered.append(whole)
    spots = [[place_in(order[::-1], i) for i in range(devices)] for order in gather_orders()]
    whole_rows = -(-(starts[-1] + rows) // 8) * 8
    group_width = ffn_in.shape[1]
    pair = jnp.concatenate([ffn_pair[0].astype(LOW), ffn_pair[1].astype(LOW).T], axis=1)[None]
    top = lax.axis_size("dp") // 4
    pair, found = gather_more(pair, [(0, 0)], "dp", [top, 2 * top, 3 * top])
    for bit in range(axis_bits("dp") - 3, 0, -1):
        pair, found = gather_more(pair, found, "dp", [1 << bit])
    pair, gathered = lax.optimization_barrier((pair, gathered))


    weights, out_weight, norms = pl.pallas_call(
        functools.partial(unpack_kernel, starts, spots, rows),
        out_shape=[pltpu.VMEM((3 * width, width), LOW), pltpu.VMEM((width, width), LOW), pltpu.VMEM((4, width), F32)],
        scratch_shapes=[pltpu.VMEM((whole_rows, width), F32)],
        name="unpack",
        compiler_params=pltpu.CompilerParams(vmem_limit_bytes=VMEM_LIMIT),
    )(*gathered)

    first_shape = (width, groups * group_width)
    target = (cotangent.astype(F32) * masked.astype(F32)[:, :, None]).astype(LOW)
    omega_high = lax.reduce_precision(omega, 8, 7)
    omega_rest = omega - omega_high
    omega_parts = jnp.concatenate([omega_high, omega_rest, omega_high, omega_rest], axis=0).T.astype(LOW)
    omega_low = jnp.concatenate(
        [omega, jnp.ones((1, count), F32), jnp.zeros((SPARE - 1, count), F32)], axis=0
    ).astype(LOW)

    ext = size + SPARE
    unit = 2 * heads * length * length * length * seqs
    flat = (seqs, width, length)
    feat = (seqs, heads, count, length)
    held = (seqs, heads, ext, length)
    score_shape = (seqs, heads, length, length)
    recip_shape = (seqs, heads, length)
    state_rows = heads // 2 * size + SPARE
    state_shape = (seqs, state_rows, count)
    core = bit_of("seq", 0).astype(jnp.int32).reshape(1)
    place_both = jnp.stack([lax.axis_index("seq"), lax.axis_index("dp")]).astype(jnp.int32)
    in_smem = pl.BlockSpec(memory_space=pltpu.SMEM)

    def spec(value):
        return per_seq(value.shape) if value.shape[0] == seqs else fixed(value.shape)

    def scratch_rows(parts):
        return [
            pltpu.VMEM((parts * width, length), F32),
            pltpu.VMEM((heads, 4 * size, length), LOW),
            pltpu.VMEM((heads, length), F32),
        ]

    pair, omega_parts = lax.optimization_barrier((pair, omega_parts))
    for bit in range(1, axis_bits("seq")):
        pair, found = gather_more(pair, found, "seq", [1 << bit])
    args = (tokens, norms, weights, omega_parts)
    outs = [array(flat, LOW)] * 2 + [array(held, LOW), pltpu.VMEM(feat, LOW)] + [pltpu.VMEM(state_shape, LOW)] * 2
    turned, uk, value, pk, own, their = call(
        functools.partial(keys_kernel, heads, size),
        seqs,
        args + (core,),
        [spec(a) for a in args] + [in_smem],
        outs,
        [spec(a) for a in outs],
        "keys",
        1,
        chip=(),
        scratch=scratch_rows(2) + [pltpu.VMEM((heads, ext, count), F32)],
    )
    their, pair = lax.optimization_barrier((their, pair))
    beside, far, omega_tied = send_half(own, their, True, omega_parts)
    pair, omega_tied, pk = lax.optimization_barrier((pair, omega_tied, pk))
    pair, found = gather_more(pair, found, "dp", [1])
    args = (turned, weights, omega_tied, value, pk)
    outs = [array(flat, LOW), pltpu.VMEM(feat, LOW), array(feat, LOW), array(score_shape, LOW), pltpu.VMEM(held, F32)]
    uq, pq_near, pq, score, num = call(
        functools.partial(queries_kernel, heads, size),
        seqs,
        args,
        [spec(a) for a in args],
        outs,
        [spec(a) for a in outs],
        "queries",
        1,
        scratch_rows(1),
        chip=(4,),
    )
    far, uq, target, pair = lax.optimization_barrier((far, uq, target, pair))
    pair, mix_norms = lax.optimization_barrier((pair, norms))
    pair_beside = flip(pair, "seq", 0)
    keep, come = receive_half(own, beside, far, True)
    states = [per_seq(keep.shape)] * 2
    outs = [array(flat, LOW), array(recip_shape, F32), array(tokens.shape, F32), array(tokens.shape, LOW)]
    mixed, recip, middle, normed_two = call(
        functools.partial(mix_kernel, heads, size),
        seqs,
        (tokens, mix_norms, out_weight, num, core, keep, come, pq_near),
        [spec(tokens), spec(norms), spec(out_weight), spec(num), in_smem, *states, spec(pq_near)],
        outs,
        [spec(a) for a in outs],
        "mix",
        1,
        chip=(3, 7),
    )

    total_rows = seqs * length
    block = 2 * length
    by_block = pl.BlockSpec((block, width), lambda i: (i, 0))
    rows_shape = (total_rows, width)
    block_out, grad_middle, leave, stay, norm_two_grad = call(
        functools.partial(ffn_kernel, groups, lax.axis_size("dp"), found),
        total_rows // block,
        (*[a.reshape(rows_shape) for a in (normed_two, middle, target)], norms, pair, pair_beside, core, place_both),
        [by_block, by_block, by_block, fixed(norms.shape), fixed(pair.shape), fixed(pair.shape), in_smem, in_smem],
        [array(rows_shape, LOW), array(rows_shape, F32)] + [array(first_shape, LOW)] * 2 + [array((2, width), F32)],
        [by_block, by_block, fixed(first_shape), fixed(first_shape), fixed((2, width))],
        "ffn",
        20 * unit,
        chip=(),
        scratch=[pltpu.VMEM((groups, width, group_width), F32)] * 2
        + [pltpu.VMEM((groups, lax.axis_size("dp"), width // lax.axis_size("dp"), 2 * group_width), LOW)],
    )
    block_out = block_out.reshape(tokens.shape)
    grad_middle = grad_middle.reshape(tokens.shape)
    come_pair = flip(leave, "seq", 0)

    args = (grad_middle, out_weight, mixed, recip, pq)
    outs = [array(held, LOW)] + [pltpu.VMEM(state_shape, LOW)] * 2
    outs = outs + [array((width, width), F32)]
    outers, own, their, out_proj = call(
        functools.partial(outer_kernel, heads, size),
        seqs,
        args + (core,),
        [spec(a) for a in args] + [in_smem],
        outs,
        [spec(a) for a in outs],
        "outer",
        1,
        chip=(),
        scratch=[pltpu.VMEM((width, length), F32), pltpu.VMEM((heads, ext, count), F32)],
    )
    their, come_pair = lax.optimization_barrier((their, come_pair))
    dp_rows = width // lax.axis_size("dp")
    columns = stay.shape[1]
    near = bit_of("dp", 0)
    sent = total_of(
        [lax.dynamic_index_in_dim(t.reshape(2, width // 2, columns), 1 - near, 0, keepdims=False) for t in (stay, come_pair)]
    ).astype(LOW)
    sent, omega_low = lax.optimization_barrier((sent, omega_low))
    come_near = flip(sent, "dp", 0)
    beside, far, omega_low = send_half(own, their, False, omega_low)
    args = (turned, omega_low, outers, value, pq, pk, score, core, keep, come, uq, uk)
    outs = [array(flat, LOW)] * 3
    query_grad, key_part, value_part, query_weight = call(
        functools.partial(back_query_kernel, heads, size),
        seqs,
        args,
        [spec(a) for a in args[:7]] + [in_smem, *states, spec(uq), spec(uk)],
        outs + [array((width, width), F32)],
        [spec(a) for a in outs] + [fixed((width, width))],
        "back_query",
        1,
        chip=(),
        scratch=[
            pltpu.VMEM((heads, ext, count), LOW),
            pltpu.VMEM(score_shape[1:], LOW),
            pltpu.VMEM(feat[1:], LOW),
            pltpu.VMEM(feat[1:], LOW),
        ],
    )
    far, query_grad = lax.optimization_barrier((far, query_grad))
    keep, come = receive_half(own, beside, far, False)
    high = list(range(axis_bits("dp") - 1, 0, -1))
    ways = 1 << len(high[:2])
    low = width // 2 // ways
    chosen = (lax.axis_index("dp") >> (high[0] + 1 - len(high[:2]))) & (ways - 1)

    def part(which):
        pieces = [
            lax.dynamic_slice(t.reshape(2, ways, low, columns), (near, which, 0, 0), (1, 1, low, columns))
            for t in (stay, come_pair)
        ]
        pieces.append(lax.dynamic_index_in_dim(come_near.reshape(ways, low, columns), which, 0))
        return total_of([p.reshape(low, columns) for p in pieces]).astype(LOW)

    leaving = [part(chosen ^ other) for other in range(1, ways)]
    leaving, omega_low = lax.optimization_barrier((leaving, omega_low))
    terms = [part(chosen)]
    for other, leave_part in enumerate(leaving, 1):
        jump = other << (high[0] + 1 - len(high[:2]))
        terms.append(lax.ppermute(leave_part, "dp", [(i, i ^ jump) for i in range(lax.axis_size("dp"))]))
    orders = scatter_orders()
    owners = [sorted(range(devices), key=lambda i: place_in(order, i)) for order in orders]
    piece_shape = (2, devices // 2, held_rows, width // 2)
    args = (tokens, norms, grad_middle, weights, omega_low, value, pk, core, keep, come)
    more = (uk, query_grad, key_part, value_part, query_weight, out_proj, norm_two_grad, turned)
    input_grad, leave, *stays = call(
        functools.partial(back_key_kernel, heads, size, (starts, rows, owners)),
        seqs,
        args + more,
        [spec(a) for a in args[:7]] + [in_smem, *states] + [spec(a) for a in more],
        [array(tokens.shape, F32), array(piece_shape, LOW)] + [array(piece_shape[1:], F32)] * 2,
        [per_seq(tokens.shape), fixed(piece_shape)] + [fixed(piece_shape[1:])] * 2,
        "back_key",
        7 * unit,
        chip=(),
        scratch=[
            pltpu.VMEM((3 * width, length), LOW),
            pltpu.VMEM((heads, ext, count), LOW),
            pltpu.VMEM(feat[1:], LOW),
            pltpu.VMEM((width, 2 * width), F32),
            pltpu.VMEM((2, width), F32),
            pltpu.VMEM((whole_rows, width), F32),
        ],
    )
    leave, terms = lax.optimization_barrier((leave, terms))
    come_pieces = flip(leave, "seq", 0)
    for step, bit in enumerate(high[2:]):
        omega_low, terms = split_rows(terms, "dp", [bit], dp_rows << (len(high) - 3 - step), omega_low)
    sums = []
    for index, (stay, order) in enumerate(zip(stays, orders)):
        part = [stay, come_pieces[index]]
        for step, (axis, bit) in enumerate(order[1:]):
            part = [t.reshape((2, t.shape[0] // 2) + t.shape[1:]) for t in part]
            if index == 0 and step == 1:
                part, terms = scatter_step(part, axis, bit, terms)
            else:
                part, _ = scatter_step(part, axis, bit)
        sums.append(total_of(part)[0])
    terms = [total_of(terms)]
    for bit in range(axis_bits("seq") - 1, 0, -1):
        terms = [t.reshape(t.shape[0], 2, -1) for t in terms]
        side = bit_of("seq", bit)
        sent = total_of([lax.dynamic_index_in_dim(t, 1 - side, 1, keepdims=False) for t in terms]).astype(LOW)
        kept = total_of([lax.dynamic_index_in_dim(t, side, 1, keepdims=False) for t in terms])
        terms = [kept, flip(sent, "seq", bit)]
    own_pair = total_of(terms)
    grad_first = own_pair[:, :group_width]
    grad_second = own_pair[:, group_width:].T
    att_grad = jnp.concatenate(sums, axis=1)
    att_grad = lax.dynamic_slice(att_grad.reshape(-1), (offset,), (shard_len,)).astype(F32)

    position = place * shard_len + jnp.arange(shard_len, dtype=jnp.int32)
    is_matrix = position < 4 * square
    rate = jnp.where(is_matrix, RATE_MATRIX, RATE_NORM)
    decay = jnp.where(is_matrix, WEIGHT_DECAY, 0.0)
    att_new, att_first_new, att_second_new = adamw(
        att_weights, att_first, att_second, att_grad, rate, decay
    )
    ffn_in_new, ffn_in_first_new, ffn_in_second_new = adamw(
        ffn_in, ffn_in_first, ffn_in_second, grad_first, RATE_MATRIX, WEIGHT_DECAY
    )
    ffn_out_new, ffn_out_first_new, ffn_out_second_new = adamw(
        ffn_out, ffn_out_first, ffn_out_second, grad_second, RATE_MATRIX, WEIGHT_DECAY
    )
    return (
        block_out,
        input_grad,
        att_new,
        att_first_new,
        att_second_new,
        att_new.astype(jnp.bfloat16),
        ffn_in_new,
        ffn_in_first_new,
        ffn_in_second_new,
        ffn_in_new.astype(jnp.bfloat16),
        ffn_out_new,
        ffn_out_first_new,
        ffn_out_second_new,
        ffn_out_new.astype(jnp.bfloat16),
    )


def solution(mesh):
    in_specs = (
        P("dp", "seq", None),
        P("dp", "seq", None),
        P("dp", "seq"),
        P(),
        P(("dp", "seq")),
        P(("dp", "seq")),
        P(("dp", "seq")),
        P("dp", "seq"),
        P("seq", "dp"),
        P("dp", "seq"),
        P("dp", "seq"),
        P("seq", "dp"),
        P("seq", "dp"),
    )
    out_specs = (
        P("dp", "seq", None),
        P("dp", "seq", None),
        P(("dp", "seq")),
        P(("dp", "seq")),
        P(("dp", "seq")),
        P(("dp", "seq")),
        P("dp", "seq"),
        P("dp", "seq"),
        P("dp", "seq"),
        P("dp", "seq"),
        P("seq", "dp"),
        P("seq", "dp"),
        P("seq", "dp"),
        P("seq", "dp"),
    )
    return jax.shard_map(shards, mesh=mesh, in_specs=in_specs, out_specs=out_specs, check_vma=False)
```

```python
import functools
import math

import jax
import jax.numpy as jnp
from jax import lax
from jax.experimental import pallas as pl
from jax.experimental.pallas import tpu as pltpu
from jax.sharding import PartitionSpec as P

CH = 256
STEP = 10
BETA_FIRST = 0.9
BETA_SECOND = 0.999
ADAM_EPS = 1e-08
WEIGHT_DECAY = 0.1
RATE_MATRIX = 0.02
RATE_NORM = 0.3
NORM_EPS = 1e-05
SPARE = 16
VMEM_LIMIT = 16 * 1024 * 1024
BIG = 1 << 20
LIMITS = {'keys': 14, 'queries': 16, 'mix': 12, 'ffn': 44, 'outer': 14, 'back_query': 18, 'back_key': 26}
F32 = jnp.float32
LOW = jnp.bfloat16


def dot_nn(left, right):
    return lax.dot_general(left, right, (((1,), (0,)), ((), ())), preferred_element_type=F32)


def dot_nt(left, right):
    return lax.dot_general(left, right, (((1,), (1,)), ((), ())), preferred_element_type=F32)


def dot_tn(left, right):
    return lax.dot_general(left, right, (((0,), (0,)), ((), ())), preferred_element_type=F32)


def norm_parts(inputs):
    centre = inputs - jnp.mean(inputs, axis=-1, keepdims=True)
    root = lax.rsqrt(jnp.mean(centre * centre, axis=-1, keepdims=True) + NORM_EPS)
    return centre * root, root


def norm_back(grad, gain, unit, root):
    inner = grad * gain
    mean_inner = jnp.mean(inner, axis=-1, keepdims=True)
    return root * (inner - mean_inner - unit * jnp.mean(inner * unit, axis=-1, keepdims=True))


def causal(length):
    earlier = lax.broadcasted_iota(jnp.int32, (length, length), 0)
    return earlier <= lax.broadcasted_iota(jnp.int32, (length, length), 1)


def put_states(own_out, their_out, core, heads, size, states, copies):
    half = heads // 2
    base = half * size
    first = core[0] == 0
    own_out[0, base:] = jnp.zeros((SPARE, own_out.shape[2]), LOW)
    their_out[0, base:] = jnp.zeros((SPARE, own_out.shape[2]), LOW)
    for index in range(half):
        low, high = states[index], states[index + half]
        total_low, total_high = [
            sum(s[size + i : size + i + 1] for i in range(copies)) for s in (low, high)
        ]
        at = slice(index * size, (index + 1) * size)
        own_out[0, at] = jnp.where(first, low[:size], high[:size]).astype(LOW)
        their_out[0, at] = jnp.where(first, high[:size], low[:size]).astype(LOW)
        row = slice(base + index, base + index + 1)
        own_out[0, row] = jnp.where(first, total_low, total_high).astype(LOW)
        their_out[0, row] = jnp.where(first, total_high, total_low).astype(LOW)


def get_state(core, keep, come, head, heads, size, copies):
    part, index = divmod(head, heads // 2)
    base = heads // 2 * size
    own = core[0] == part
    total = jnp.where(own, keep[0, base : base + SPARE], come[0, base : base + SPARE]).astype(F32)[index : index + 1]
    line = lax.broadcasted_iota(jnp.int32, (SPARE, total.shape[1]), 0)
    spare = jnp.where(line < copies, total, 0.0).astype(LOW)
    rows = slice(index * size, (index + 1) * size)
    return jnp.concatenate([jnp.where(own, keep[0, rows], come[0, rows]), spare], axis=0)


def split_features(rows, scale, shift, high_out, stack, half):
    size = rows.shape[0]
    scaled = rows * scale
    high = scaled.astype(LOW)
    rest = (scaled - high.astype(F32)).astype(LOW)
    high_out[...] = high
    for part, piece in enumerate((high, high, rest, rest)):
        stack[part * size : (part + 1) * size] = piece
    half[...] = 0.5 * jnp.sum(scaled * scaled, axis=0, keepdims=True) + shift


def staged(count, *stages):
    for stage in stages:
        for item in range(count):
            stage(item)


def keys_kernel(
    heads,
    size,
    tok,
    norms,
    weights,
    omega,
    core,
    turned_out,
    uk_out,
    value_out,
    pk_out,
    own_out,
    their_out,
    rows,
    stacks,
    halves,
    states,
):
    width = heads * size
    length = tok.shape[1]
    unit, _ = norm_parts(tok[0].astype(F32))
    turned_out[0] = (unit * norms[0:1] + norms[1:2]).astype(LOW).T
    rows[...] = dot_nn(weights[width:], turned_out[0])
    spare = (lax.broadcasted_iota(jnp.int32, (SPARE, length), 0) < 2).astype(F32).astype(LOW)
    shift = 0.5 * math.log(omega.shape[0])

    def split(head):
        at = slice(head * size, (head + 1) * size)
        split_features(
            rows[at], size ** (-0.25), shift, uk_out.at[0, at], stacks.at[head], halves.at[head : head + 1]
        )
        value_out[0, head, :size] = rows[width + head * size : width + (head + 1) * size].astype(LOW)
        value_out[0, head, size:] = spare

    def feature(head):
        projected = dot_nn(omega[...], stacks[head])
        pk_out[0, head] = jnp.exp(projected - halves[head : head + 1]).astype(LOW)

    def local_state(head):
        states[head] = dot_nt(value_out[0, head], pk_out[0, head])

    staged(heads, split, feature, local_state)
    put_states(own_out, their_out, core, heads, size, states, 1)


def queries_kernel(heads, size, turned, weights, omega, value, pk, uq_out, pq_out, pq_copy, score_out, num_out, rows, stacks, halves):
    width = heads * size
    length = turned.shape[2]
    rows[...] = dot_nn(weights[:width], turned[0])
    shift = 0.5 * math.log(omega.shape[0])
    keep = causal(length)

    def split(head):
        at = slice(head * size, (head + 1) * size)
        split_features(
            rows[at], size ** (-0.25), shift, uq_out.at[0, at], stacks.at[head], halves.at[head : head + 1]
        )

    def feature(head):
        projected = dot_nn(omega[...], stacks[head])
        feat = jnp.exp(projected - halves[head : head + 1]).astype(LOW)
        pq_out[0, head] = feat
        pq_copy[0, head] = feat

    def score(head):
        score_out[0, head] = jnp.where(keep, dot_tn(pk[0, head], pq_out[0, head]), 0.0).astype(LOW)

    def numerator(head):
        num_out[0, head] = dot_nn(value[0, head], score_out[0, head])

    staged(heads, split, feature, score, numerator)


def mix_kernel(heads, size, tok, norms, out_weight, num, core, keep, come, pq, mixed_out, recip_out, middle_out, normed_out):
    state = (core, keep, come)
    for head in range(heads):
        at = head * size
        total = num[0, head] + dot_nn(get_state(*state, head, heads, size, 2), pq[0, head])
        recip = 1.0 / total[size : size + 1]
        mixed_out[0, at : at + size] = (total[:size] * recip).astype(LOW)
        recip_out[0, head : head + 1] = recip
    mixed = mixed_out[0]
    middle = tok[0].astype(F32) + dot_tn(mixed, out_weight[...])
    middle_out[0] = middle
    unit, _ = norm_parts(middle)
    normed_out[0] = (unit * norms[2:3] + norms[3:4]).astype(LOW)


def gelu_pair(hidden):
    slope = math.sqrt(2.0 / math.pi)
    square = hidden * hidden
    tanh = jnp.tanh(hidden * (slope + (slope * 0.044715) * square))
    upper = 0.5 + 0.5 * tanh
    inner = (0.5 * slope) + (1.5 * slope * 0.044715) * square
    return hidden * upper, upper + hidden * (1.0 - tanh * tanh) * inner


def ffn_kernel(
    groups,
    devices,
    found,
    normed,
    middle,
    target,
    norms,
    own_pair,
    their_pair,
    core,
    place,
    out,
    grad_out,
    leave,
    stay,
    norm_grad,
    first_sum,
    second_sum,
    pair,
):
    step = pl.program_id(0)
    half = pair.shape[3] // 2
    width = normed.shape[1]

    @pl.when(step == 0)
    def _():
        for index, (seq_jump, dp_jump) in enumerate(found):
            pair[place[0] ^ seq_jump, place[1] ^ dp_jump] = own_pair[index]
            pair[place[0] ^ (seq_jump ^ 1), place[1] ^ dp_jump] = their_pair[index]

    own = normed[...]
    grads = target[...]
    own_turned = own.T
    grads_turned = grads.T

    @pl.when(step == 0)
    def _():
        first_sum[...] = jnp.zeros_like(first_sum)
        second_sum[...] = jnp.zeros_like(second_sum)
        norm_grad[...] = jnp.zeros_like(norm_grad)

    result = jnp.zeros(own.shape, F32)
    grad_normed = jnp.zeros(own.shape, F32)
    for group in range(groups):
        first = pair[group, :, :, :half].reshape(width, half)
        second = pair[group, :, :, half:].reshape(width, half)
        active, slope = gelu_pair(dot_nn(own, first))
        active = active.astype(LOW)
        result = result + dot_nt(active, second)
        grad_hidden = (dot_nn(grads, second) * slope).astype(LOW)
        grad_normed = grad_normed + dot_nt(grad_hidden, first)
        first_sum[group] += dot_nn(own_turned, grad_hidden)
        second_sum[group] += dot_nn(grads_turned, active)
    rows = middle[...]
    out[...] = (rows + result).astype(LOW)
    unit, root = norm_parts(rows)
    grad_out[...] = grads.astype(F32) + norm_back(grad_normed, norms[2:3], unit, root)
    norm_grad[0:1] += jnp.sum(grad_normed * unit, axis=0, keepdims=True)
    norm_grad[1:2] += jnp.sum(grad_normed, axis=0, keepdims=True)

    @pl.when(step == pl.num_programs(0) - 1)
    def _():
        mine = core[0]
        count = normed.shape[1] // devices
        for chip in range(groups // 2):
            at = 2 * half * chip
            for side, target_ref in ((mine, stay), (1 - mine, leave)):
                for place in range(devices):
                    spot = place // 2 + (place % 2) * (devices // 2)
                    rows_in = slice(place * count, (place + 1) * count)
                    rows_out = slice(spot * count, (spot + 1) * count)
                    target_ref[rows_out, at : at + half] = first_sum[2 * chip + side, rows_in].astype(LOW)
                    target_ref[rows_out, at + half : at + 2 * half] = second_sum[2 * chip + side, rows_in].astype(LOW)


def through_omega(flow, scaled, omega_low, size):
    back = dot_nn(omega_low, flow)
    return ((back[:size] - scaled.astype(F32) * back[size : size + 1]) * size ** (-0.25))


def outer_kernel(
    heads, size, grad_middle, out_weight, mixed, recip, pq, core, outer_out, own_out, their_out, out_proj, grad_mixed, states
):
    length = grad_middle.shape[1]

    @pl.when(pl.program_id(0) == 0)
    def _():
        out_proj[...] = jnp.zeros_like(out_proj)

    grad_low = grad_middle[0].astype(LOW)
    grad_mixed[...] = dot_nt(out_weight[...], grad_low)
    out_proj[...] += dot_nn(mixed[0], grad_low)
    line = lax.broadcasted_iota(jnp.int32, (SPARE, length), 0)

    def scale(head):
        at = head * size
        outer = grad_mixed[at : at + size] * recip[0, head : head + 1]
        centre = -jnp.sum(outer * mixed[0, at : at + size].astype(F32), axis=0, keepdims=True)
        rest = centre - centre.astype(LOW).astype(F32)
        outer_out[0, head, :size] = outer.astype(LOW)
        outer_out[0, head, size:] = jnp.where(line == 0, centre, jnp.where(line == 1, rest, 0.0)).astype(LOW)

    def local_state(head):
        states[head] = dot_nt(outer_out[0, head], pq[0, head])

    staged(heads, scale, local_state)
    put_states(own_out, their_out, core, heads, size, states, 2)


def back_query_kernel(
    heads,
    size,
    turned,
    omega_low,
    outers,
    value,
    pq,
    pk,
    scores,
    core,
    keep_state,
    come_state,
    uq,
    uk,
    query_out,
    key_out,
    value_out,
    query_weight,
    befores,
    grad_scores,
    flows,
    key_flows,
):
    @pl.when(pl.program_id(0) == 0)
    def _():
        query_weight[...] = jnp.zeros_like(query_weight)

    keep = causal(turned.shape[2])

    def score(head):
        befores[head] = get_state(core, keep_state, come_state, head, heads, size, 2)
        grad_scores[head] = jnp.where(keep, dot_tn(value[0, head], outers[0, head]), 0.0).astype(LOW)

    def feature(head):
        at = head * size
        grad_feat = dot_nn(pk[0, head], grad_scores[head]) + dot_tn(befores[head], outers[0, head])
        flows[head] = (grad_feat * pq[0, head].astype(F32)).astype(LOW)
        grad_key_feat = dot_nt(pq[0, head], grad_scores[head])
        key_flows[head] = (grad_key_feat * pk[0, head].astype(F32)).astype(LOW)
        value_out[0, at : at + size] = dot_nt(outers[0, head], scores[0, head])[:size].astype(LOW)

    def query(head):
        at = head * size
        query_out[0, at : at + size] = through_omega(flows[head], uq[0, at : at + size], omega_low[...], size).astype(
            LOW
        )
        key_out[0, at : at + size] = through_omega(key_flows[head], uk[0, at : at + size], omega_low[...], size).astype(LOW)

    staged(heads, score, feature, query)
    query_weight[...] += dot_nt(turned[0], query_out[0])


def back_key_kernel(
    heads,
    size,
    layout,
    tok,
    norms,
    grad_middle,
    weights,
    omega_low,
    value,
    pk,
    core,
    keep_state,
    come_state,
    uk,
    query_grad,
    key_part,
    value_part,
    query_weight,
    out_proj,
    norm_two,
    turned,
    input_grad,
    leave,
    stay_left,
    stay_right,
    flat,
    laters,
    flows,
    pair_weight,
    norm_grad,
    whole,
):
    width = heads * size

    @pl.when(pl.program_id(0) == 0)
    def _():
        pair_weight[...] = jnp.zeros_like(pair_weight)
        norm_grad[...] = jnp.zeros_like(norm_grad)

    unit, root = norm_parts(tok[0].astype(F32))
    flat[:width] = query_grad[0]

    def later(head):
        laters[head] = get_state(core, keep_state, come_state, head, heads, size, 1)

    def feature(head):
        at = 2 * width + head * size
        grad_feat = dot_tn(laters[head], value[0, head])
        flows[head] = (grad_feat * pk[0, head].astype(F32)).astype(LOW)
        extra = dot_nn(laters[head], pk[0, head])[:size]
        flat[at : at + size] = (
            value_part[0, head * size : (head + 1) * size].astype(F32) + extra
        ).astype(LOW)

    def key(head):
        at = width + head * size
        part = slice(head * size, (head + 1) * size)
        total = key_part[0, part].astype(F32) + through_omega(flows[head], uk[0, part], omega_low[...], size)
        flat[at : at + size] = total.astype(LOW)

    staged(heads, later, feature, key)
    pair_weight[...] += dot_nt(turned[0], flat[width:])
    grad_normed = dot_tn(flat[...], weights[...])
    input_grad[0] = grad_middle[0] + norm_back(grad_normed, norms[0:1], unit, root)
    norm_grad[0:1] += jnp.sum(grad_normed * unit, axis=0, keepdims=True)
    norm_grad[1:2] += jnp.sum(grad_normed, axis=0, keepdims=True)

    @pl.when(pl.program_id(0) == pl.num_programs(0) - 1)
    def _():
        whole[:width] = query_weight[...]
        whole[width : 2 * width] = pair_weight[:, :width]
        whole[2 * width : 3 * width] = pair_weight[:, width:]
        whole[3 * width : 4 * width] = out_proj[...]
        whole[4 * width : 4 * width + 2] = norm_grad[...]
        whole[4 * width + 2 : 4 * width + 4] = norm_two[...]
        starts, rows, owners = layout
        half = width // 2
        first = core[0] == 0
        leave[...] = jnp.zeros_like(leave)
        for part, stay in enumerate((stay_left, stay_right)):
            count = leave.shape[1]
            stay[...] = jnp.zeros_like(stay)
            columns = slice(part * half, (part + 1) * half)
            for spot in range(count):
                low = starts[owners[part][spot]]
                high = starts[owners[part][spot + count]]
                low = whole[low : low + rows, columns]
                high = whole[high : high + rows, columns]
                stay[spot, :rows] = jnp.where(first, low, high)
                leave[part, spot, :rows] = jnp.where(first, high, low).astype(LOW)


def per_seq(shape, offset=0):
    rest = tuple(shape[1:])
    return pl.BlockSpec((1,) + rest, lambda i: (i + offset,) + (0,) * len(rest))


def fixed(shape):
    return pl.BlockSpec(tuple(shape), lambda i: (0,) * len(shape))


def call(kernel, steps, args, in_specs, outs, out_specs, name, flops, scratch=(), aliases=None, after=(), chip=None):
    if chip is not None:
        args = tuple(
            on_chip(a) if i in chip else off_chip(a) if math.prod(a.shape) >= BIG else a for i, a in enumerate(args)
        )
    if after:
        count, body = len(args), kernel
        args = tuple(args) + tuple(after)
        in_specs = list(in_specs) + [pl.BlockSpec(memory_space=pl.ANY)] * len(after)

        def kernel(*refs):
            body(*refs[:count], *refs[count + len(after) :])

    moved = sum(math.prod(a.shape) * jnp.dtype(a.dtype).itemsize for a in list(args) + list(outs))
    return pl.pallas_call(
        kernel,
        grid=(steps,),
        in_specs=in_specs,
        out_specs=out_specs,
        out_shape=outs,
        scratch_shapes=list(scratch),
        name=name,
        input_output_aliases=aliases or {},
        compiler_params=pltpu.CompilerParams(
            dimension_semantics=("arbitrary",), vmem_limit_bytes=LIMITS[name] * 1024 * 1024
        ),
        cost_estimate=pl.CostEstimate(
            flops=flops, bytes_accessed=moved if flops > 1 else 1, transcendentals=0
        ),
    )(*args)


def on_chip(value):
    return pltpu.with_memory_space_constraint(value, pltpu.VMEM)


def off_chip(value):
    return pltpu.with_memory_space_constraint(value, pltpu.HBM)


def array(shape, dtype):
    return pltpu.HBM(tuple(shape), dtype)


def flip(value, axis, bit):
    return lax.ppermute(value, axis, [(i, i ^ (1 << bit)) for i in range(lax.axis_size(axis))])


def bit_of(axis, bit):
    return (lax.axis_index(axis) >> bit) & 1


def send_half(own, their, forward, tie):
    count = lax.axis_size("seq")
    beside = flip(their, "seq", 0)
    mine = (own.astype(F32) + beside.astype(F32)).astype(LOW)
    mine, tie = lax.optimization_barrier((mine, tie))
    far = None
    for step in range(1, count // 2):
        hop = 2 * step if forward else -2 * step
        pairs = [(i, i + hop) for i in range(count) if 0 <= i + hop < count]
        come = lax.ppermute(mine, "seq", pairs)
        far = come if far is None else far + come
    return beside, far, tie


def receive_half(own, beside, far, forward):
    core = bit_of("seq", 0)
    giver = (core == 0) if forward else (core == 1)
    give = (far.astype(F32) + jnp.where(giver, own.astype(F32), 0.0)).astype(LOW)
    keep = (far.astype(F32) + jnp.where(giver, 0.0, beside.astype(F32))).astype(LOW)
    return keep, flip(give, "seq", 0)


def axis_bits(axis):
    return lax.axis_size(axis).bit_length() - 1


def gather_orders():
    high = [("dp", bit) for bit in range(1, axis_bits("dp"))]
    seq_high = [("seq", bit) for bit in range(1, axis_bits("seq"))]
    near = [("dp", 0)]
    return [high + near + seq_high + [("seq", 0)], seq_high + high + near + [("seq", 0)]]


def scatter_orders():
    high = [("dp", bit) for bit in range(axis_bits("dp") - 1, 0, -1)]
    seq_high = [("seq", bit) for bit in range(axis_bits("seq") - 1, 0, -1)]
    near = [("dp", 0)]
    return [[("seq", 0)] + seq_high + near + high, [("seq", 0)] + near + high + seq_high]


def place_in(order, index):
    seq_bits = axis_bits("seq")
    spot = 0
    for axis, bit in order:
        shift = bit if axis == "seq" else bit + seq_bits
        spot = 2 * spot + ((index >> shift) & 1)
    return spot


def gather_more(value, found, axis, jumps):
    size = lax.axis_size(axis)
    come = [lax.ppermute(value, axis, [(i, i ^ jump) for i in range(size)]) for jump in jumps]
    more = list(found)
    for jump in jumps:
        more += [(a ^ jump, b) if axis == "seq" else (a, b ^ jump) for a, b in found]
    return jnp.concatenate([value] + come, axis=0), more


def gather_doubling(value, order, late, prepare=None):
    value = value[None]
    for step, (axis, bit) in enumerate(order):
        if step == len(order) - 2:
            value, late = lax.optimization_barrier((value, late))
        come = flip(value, axis, bit)
        if step == 0 and prepare is not None:
            come, late = lax.optimization_barrier((come, late))
            late = prepare(late)
        low = bit_of(axis, bit) == 0
        value = jnp.concatenate([jnp.where(low, value, come), jnp.where(low, come, value)], axis=0)
    return value, late


def total_of(terms):
    return sum(term.astype(F32) for term in terms)


def scatter_step(terms, axis, bit, late=None):
    mine = bit_of(axis, bit)
    leave = total_of([lax.dynamic_index_in_dim(term, 1 - mine, 0, keepdims=False) for term in terms]).astype(LOW)
    if late is not None:
        leave, late = lax.optimization_barrier((leave, late))
    come = flip(leave, axis, bit)
    stay = total_of([lax.dynamic_index_in_dim(term, mine, 0, keepdims=False) for term in terms])
    return [stay, come], late


def split_rows(terms, axis, bits, low, tie):
    ways = 1 << len(bits)
    terms = [t.reshape(-1, ways, low, t.shape[1]) for t in terms]
    shift = min(bits)
    mine = (lax.axis_index(axis) >> shift) & (ways - 1)

    def part(which):
        total = total_of([lax.dynamic_index_in_dim(t, which, 1, keepdims=False) for t in terms]).astype(LOW)
        return total.reshape(-1, total.shape[-1])

    leaving = [part(mine ^ other) for other in range(1, ways)]
    leaving, tie = lax.optimization_barrier((leaving, tie))
    size = lax.axis_size(axis)
    come = [
        lax.ppermute(leave, axis, [(i, i ^ (other << shift)) for i in range(size)])
        for other, leave in enumerate(leaving, 1)
    ]
    return tie, [part(mine)] + come


def adamw(weight, first, second, grad, rate, decay):
    first_new = BETA_FIRST * first + (1.0 - BETA_FIRST) * grad
    second_new = BETA_SECOND * second + (1.0 - BETA_SECOND) * grad * grad
    first_hat = first_new / (1.0 - BETA_FIRST**STEP)
    second_hat = second_new / (1.0 - BETA_SECOND**STEP)
    weight_new = weight - rate * (first_hat / (jnp.sqrt(second_hat) + ADAM_EPS) + decay * weight)
    return (weight_new, first_new, second_new)


def unpack_kernel(starts, spots, rows, left, right, wide_out, out_weight, norms, whole):
    whole[...] = jnp.zeros_like(whole)
    half = left.shape[2]
    for index, start in enumerate(starts):
        whole[start : start + rows, :half] += left[spots[0][index], :rows].astype(F32)
        whole[start : start + rows, half:] += right[spots[1][index], :rows].astype(F32)
    width = out_weight.shape[0]
    for part in range(3):
        wide_out[part * width : (part + 1) * width] = whole[part * width : (part + 1) * width].astype(LOW).T
    out_weight[...] = whole[3 * width : 4 * width].astype(LOW)
    norms[...] = whole[4 * width : 4 * width + 4]


def shards(
    tokens,
    cotangent,
    masked,
    omega,
    att_weights,
    att_first,
    att_second,
    ffn_in,
    ffn_out,
    ffn_in_first,
    ffn_in_second,
    ffn_out_first,
    ffn_out_second,
):
    seqs, length, width = tokens.shape
    size, count = omega.shape
    heads = width // size
    square = width * width
    groups = lax.axis_size("seq")
    devices = lax.axis_size("dp") * groups
    shard_len = att_weights.shape[0]
    place = lax.axis_index(("dp", "seq"))
    starts = [(i * shard_len) // width for i in range(devices)]
    offsets = [(i * shard_len) % width for i in range(devices)]
    rows = -(-(max(offsets) + shard_len) // width)
    held_rows = -(-rows // 8) * 8
    offset = (place * shard_len) % width

    framed = lax.dynamic_update_slice(
        jnp.zeros((held_rows * width,), LOW), att_weights.astype(LOW), (offset,)
    ).reshape(held_rows, width)
    group_width = ffn_in.shape[1]
    ffn_pair = (ffn_in, ffn_out)
    halves = [framed[:, : width // 2], framed[:, width // 2 :]]
    gathered = []

    def beside(shards):
        return jnp.concatenate([shards[0].astype(LOW), shards[1].astype(LOW).T], axis=1)[None]

    for half, order in zip(halves, gather_orders()):
        whole, ffn_pair = gather_doubling(half, order, ffn_pair, None if gathered else beside)
        gathered.append(whole)
    spots = [[place_in(order[::-1], i) for i in range(devices)] for order in gather_orders()]
    whole_rows = -(-(starts[-1] + rows) // 8) * 8
    group_width = ffn_in.shape[1]
    pair = ffn_pair
    top = lax.axis_size("dp") // 4
    pair, found = gather_more(pair, [(0, 0)], "dp", [top, 2 * top, 3 * top])
    for bit in range(axis_bits("dp") - 3, 0, -1):
        pair, found = gather_more(pair, found, "dp", [1 << bit])
    pair, gathered = lax.optimization_barrier((pair, gathered))


    weights, out_weight, norms = pl.pallas_call(
        functools.partial(unpack_kernel, starts, spots, rows),
        out_shape=[pltpu.VMEM((3 * width, width), LOW), pltpu.VMEM((width, width), LOW), pltpu.VMEM((4, width), F32)],
        scratch_shapes=[pltpu.VMEM((whole_rows, width), F32)],
        name="unpack",
        compiler_params=pltpu.CompilerParams(vmem_limit_bytes=VMEM_LIMIT),
    )(*gathered)

    first_shape = (width, groups * group_width)
    target = (cotangent.astype(F32) * masked.astype(F32)[:, :, None]).astype(LOW)
    omega_high = lax.reduce_precision(omega, 8, 7)
    omega_rest = omega - omega_high
    omega_parts = jnp.concatenate([omega_high, omega_rest, omega_high, omega_rest], axis=0).T.astype(LOW)
    omega_low = jnp.concatenate(
        [omega, jnp.ones((1, count), F32), jnp.zeros((SPARE - 1, count), F32)], axis=0
    ).astype(LOW)

    ext = size + SPARE
    unit = 2 * heads * length * length * length * seqs
    flat = (seqs, width, length)
    feat = (seqs, heads, count, length)
    held = (seqs, heads, ext, length)
    score_shape = (seqs, heads, length, length)
    recip_shape = (seqs, heads, length)
    state_rows = heads // 2 * size + SPARE
    state_shape = (seqs, state_rows, count)
    core = bit_of("seq", 0).astype(jnp.int32).reshape(1)
    place_both = jnp.stack([lax.axis_index("seq"), lax.axis_index("dp")]).astype(jnp.int32)
    in_smem = pl.BlockSpec(memory_space=pltpu.SMEM)

    def spec(value):
        return per_seq(value.shape) if value.shape[0] == seqs else fixed(value.shape)

    def scratch_rows(parts):
        return [
            pltpu.VMEM((parts * width, length), F32),
            pltpu.VMEM((heads, 4 * size, length), LOW),
            pltpu.VMEM((heads, length), F32),
        ]

    pair, omega_parts = lax.optimization_barrier((pair, omega_parts))
    for bit in range(1, axis_bits("seq")):
        pair, found = gather_more(pair, found, "seq", [1 << bit])
    args = (tokens, norms, weights, omega_parts)
    outs = [array(flat, LOW)] * 2 + [array(held, LOW), pltpu.VMEM(feat, LOW)] + [pltpu.VMEM(state_shape, LOW)] * 2
    turned, uk, value, pk, own, their = call(
        functools.partial(keys_kernel, heads, size),
        seqs,
        args + (core,),
        [spec(a) for a in args] + [in_smem],
        outs,
        [spec(a) for a in outs],
        "keys",
        1,
        chip=(),
        scratch=scratch_rows(2) + [pltpu.VMEM((heads, ext, count), F32)],
    )
    their, pair = lax.optimization_barrier((their, pair))
    beside, far, omega_tied = send_half(own, their, True, omega_parts)
    pair, omega_tied, pk = lax.optimization_barrier((pair, omega_tied, pk))
    pair, found = gather_more(pair, found, "dp", [1])
    args = (turned, weights, omega_tied, value, pk)
    outs = [array(flat, LOW), pltpu.VMEM(feat, LOW), array(feat, LOW), array(score_shape, LOW), pltpu.VMEM(held, F32)]
    uq, pq_near, pq, score, num = call(
        functools.partial(queries_kernel, heads, size),
        seqs,
        args,
        [spec(a) for a in args],
        outs,
        [spec(a) for a in outs],
        "queries",
        1,
        scratch_rows(1),
        chip=(4,),
    )
    far, uq, target, pair = lax.optimization_barrier((far, uq, target, pair))
    pair, mix_norms = lax.optimization_barrier((pair, norms))
    pair_beside = flip(pair, "seq", 0)
    keep, come = receive_half(own, beside, far, True)
    states = [per_seq(keep.shape)] * 2
    outs = [array(flat, LOW), array(recip_shape, F32), array(tokens.shape, F32), array(tokens.shape, LOW)]
    mixed, recip, middle, normed_two = call(
        functools.partial(mix_kernel, heads, size),
        seqs,
        (tokens, mix_norms, out_weight, num, core, keep, come, pq_near),
        [spec(tokens), spec(norms), spec(out_weight), spec(num), in_smem, *states, spec(pq_near)],
        outs,
        [spec(a) for a in outs],
        "mix",
        1,
        chip=(3, 7),
    )

    total_rows = seqs * length
    block = 2 * length
    by_block = pl.BlockSpec((block, width), lambda i: (i, 0))
    rows_shape = (total_rows, width)
    block_out, grad_middle, leave, stay, norm_two_grad = call(
        functools.partial(ffn_kernel, groups, lax.axis_size("dp"), found),
        total_rows // block,
        (*[a.reshape(rows_shape) for a in (normed_two, middle, target)], norms, pair, pair_beside, core, place_both),
        [by_block, by_block, by_block, fixed(norms.shape), fixed(pair.shape), fixed(pair.shape), in_smem, in_smem],
        [array(rows_shape, LOW), array(rows_shape, F32)] + [array(first_shape, LOW)] * 2 + [array((2, width), F32)],
        [by_block, by_block, fixed(first_shape), fixed(first_shape), fixed((2, width))],
        "ffn",
        20 * unit,
        chip=(),
        scratch=[pltpu.VMEM((groups, width, group_width), F32)] * 2
        + [pltpu.VMEM((groups, lax.axis_size("dp"), width // lax.axis_size("dp"), 2 * group_width), LOW)],
    )
    block_out = block_out.reshape(tokens.shape)
    grad_middle = grad_middle.reshape(tokens.shape)
    come_pair = flip(leave, "seq", 0)

    args = (grad_middle, out_weight, mixed, recip, pq)
    outs = [pltpu.VMEM(held, LOW)] + [pltpu.VMEM(state_shape, LOW)] * 2
    outs = outs + [array((width, width), F32)]
    outers, own, their, out_proj = call(
        functools.partial(outer_kernel, heads, size),
        seqs,
        args + (core,),
        [spec(a) for a in args] + [in_smem],
        outs,
        [spec(a) for a in outs],
        "outer",
        1,
        chip=(),
        scratch=[pltpu.VMEM((width, length), F32), pltpu.VMEM((heads, ext, count), F32)],
    )
    their, come_pair = lax.optimization_barrier((their, come_pair))
    dp_rows = width // lax.axis_size("dp")
    columns = stay.shape[1]
    near = bit_of("dp", 0)
    sent = total_of(
        [lax.dynamic_index_in_dim(t.reshape(2, width // 2, columns), 1 - near, 0, keepdims=False) for t in (stay, come_pair)]
    ).astype(LOW)
    sent, omega_low = lax.optimization_barrier((sent, omega_low))
    come_near = flip(sent, "dp", 0)
    beside, far, omega_low = send_half(own, their, False, omega_low)
    args = (turned, omega_low, outers, value, pq, pk, score, core, keep, come, uq, uk)
    outs = [pltpu.VMEM(flat, LOW)] * 3
    query_grad, key_part, value_part, query_weight = call(
        functools.partial(back_query_kernel, heads, size),
        seqs,
        args,
        [spec(a) for a in args[:7]] + [in_smem, *states, spec(uq), spec(uk)],
        outs + [array((width, width), F32)],
        [spec(a) for a in outs] + [fixed((width, width))],
        "back_query",
        1,
        chip=(2,),
        scratch=[
            pltpu.VMEM((heads, ext, count), LOW),
            pltpu.VMEM(score_shape[1:], LOW),
            pltpu.VMEM(feat[1:], LOW),
            pltpu.VMEM(feat[1:], LOW),
        ],
    )
    far, query_grad = lax.optimization_barrier((far, query_grad))
    keep, come = receive_half(own, beside, far, False)
    high = list(range(axis_bits("dp") - 1, 0, -1))
    ways = 1 << len(high[:2])
    low = width // 2 // ways
    chosen = (lax.axis_index("dp") >> (high[0] + 1 - len(high[:2]))) & (ways - 1)

    def part(which):
        pieces = [
            lax.dynamic_slice(t.reshape(2, ways, low, columns), (near, which, 0, 0), (1, 1, low, columns))
            for t in (stay, come_pair)
        ]
        pieces.append(lax.dynamic_index_in_dim(come_near.reshape(ways, low, columns), which, 0))
        return total_of([p.reshape(low, columns) for p in pieces]).astype(LOW)

    leaving = [part(chosen ^ other) for other in range(1, ways)]
    leaving, omega_low = lax.optimization_barrier((leaving, omega_low))
    terms = [part(chosen)]
    for other, leave_part in enumerate(leaving, 1):
        jump = other << (high[0] + 1 - len(high[:2]))
        terms.append(lax.ppermute(leave_part, "dp", [(i, i ^ jump) for i in range(lax.axis_size("dp"))]))
    orders = scatter_orders()
    owners = [sorted(range(devices), key=lambda i: place_in(order, i)) for order in orders]
    piece_shape = (2, devices // 2, held_rows, width // 2)
    args = (tokens, norms, grad_middle, weights, omega_low, value, pk, core, keep, come)
    more = (uk, query_grad, key_part, value_part, query_weight, out_proj, norm_two_grad, turned)
    input_grad, leave, *stays = call(
        functools.partial(back_key_kernel, heads, size, (starts, rows, owners)),
        seqs,
        args + more,
        [spec(a) for a in args[:7]] + [in_smem, *states] + [spec(a) for a in more],
        [array(tokens.shape, F32), array(piece_shape, LOW)] + [array(piece_shape[1:], F32)] * 2,
        [per_seq(tokens.shape), fixed(piece_shape)] + [fixed(piece_shape[1:])] * 2,
        "back_key",
        7 * unit,
        chip=(11, 12, 13),
        scratch=[
            pltpu.VMEM((3 * width, length), LOW),
            pltpu.VMEM((heads, ext, count), LOW),
            pltpu.VMEM(feat[1:], LOW),
            pltpu.VMEM((width, 2 * width), F32),
            pltpu.VMEM((2, width), F32),
            pltpu.VMEM((whole_rows, width), F32),
        ],
    )
    leave, terms = lax.optimization_barrier((leave, terms))
    come_pieces = flip(leave, "seq", 0)
    for step, bit in enumerate(high[2:]):
        omega_low, terms = split_rows(terms, "dp", [bit], dp_rows << (len(high) - 3 - step), omega_low)
    sums = []
    for index, (stay, order) in enumerate(zip(stays, orders)):
        part = [stay, come_pieces[index]]
        for step, (axis, bit) in enumerate(order[1:]):
            part = [t.reshape((2, t.shape[0] // 2) + t.shape[1:]) for t in part]
            if index == 0 and step == 1:
                part, terms = scatter_step(part, axis, bit, terms)
            else:
                part, _ = scatter_step(part, axis, bit)
        sums.append(total_of(part)[0])
    terms = [total_of(terms)]
    for bit in range(axis_bits("seq") - 1, 0, -1):
        terms = [t.reshape(t.shape[0], 2, -1) for t in terms]
        side = bit_of("seq", bit)
        sent = total_of([lax.dynamic_index_in_dim(t, 1 - side, 1, keepdims=False) for t in terms]).astype(LOW)
        kept = total_of([lax.dynamic_index_in_dim(t, side, 1, keepdims=False) for t in terms])
        terms = [kept, flip(sent, "seq", bit)]
    own_pair = total_of(terms)
    grad_first = own_pair[:, :group_width]
    grad_second = own_pair[:, group_width:].T
    att_grad = jnp.concatenate(sums, axis=1)
    att_grad = lax.dynamic_slice(att_grad.reshape(-1), (offset,), (shard_len,)).astype(F32)

    position = place * shard_len + jnp.arange(shard_len, dtype=jnp.int32)
    is_matrix = position < 4 * square
    rate = jnp.where(is_matrix, RATE_MATRIX, RATE_NORM)
    decay = jnp.where(is_matrix, WEIGHT_DECAY, 0.0)
    att_new, att_first_new, att_second_new = adamw(
        att_weights, att_first, att_second, att_grad, rate, decay
    )
    ffn_in_new, ffn_in_first_new, ffn_in_second_new = adamw(
        ffn_in, ffn_in_first, ffn_in_second, grad_first, RATE_MATRIX, WEIGHT_DECAY
    )
    ffn_out_new, ffn_out_first_new, ffn_out_second_new = adamw(
        ffn_out, ffn_out_first, ffn_out_second, grad_second, RATE_MATRIX, WEIGHT_DECAY
    )
    return (
        block_out,
        input_grad,
        att_new,
        att_first_new,
        att_second_new,
        att_new.astype(jnp.bfloat16),
        ffn_in_new,
        ffn_in_first_new,
        ffn_in_second_new,
        ffn_in_new.astype(jnp.bfloat16),
        ffn_out_new,
        ffn_out_first_new,
        ffn_out_second_new,
        ffn_out_new.astype(jnp.bfloat16),
    )


def solution(mesh):
    in_specs = (
        P("dp", "seq", None),
        P("dp", "seq", None),
        P("dp", "seq"),
        P(),
        P(("dp", "seq")),
        P(("dp", "seq")),
        P(("dp", "seq")),
        P("dp", "seq"),
        P("seq", "dp"),
        P("dp", "seq"),
        P("dp", "seq"),
        P("seq", "dp"),
        P("seq", "dp"),
    )
    out_specs = (
        P("dp", "seq", None),
        P("dp", "seq", None),
        P(("dp", "seq")),
        P(("dp", "seq")),
        P(("dp", "seq")),
        P(("dp", "seq")),
        P("dp", "seq"),
        P("dp", "seq"),
        P("dp", "seq"),
        P("dp", "seq"),
        P("seq", "dp"),
        P("seq", "dp"),
        P("seq", "dp"),
        P("seq", "dp"),
    )
    return jax.shard_map(shards, mesh=mesh, in_specs=in_specs, out_specs=out_specs, check_vma=False)
```

```python
import functools
import math

import jax
import jax.numpy as jnp
from jax import lax
from jax.experimental import pallas as pl
from jax.experimental.pallas import tpu as pltpu
from jax.sharding import PartitionSpec as P

CH = 256
STEP = 10
BETA_FIRST = 0.9
BETA_SECOND = 0.999
ADAM_EPS = 1e-08
WEIGHT_DECAY = 0.1
RATE_MATRIX = 0.02
RATE_NORM = 0.3
NORM_EPS = 1e-05
SPARE = 16
VMEM_LIMIT = 16 * 1024 * 1024
BIG = 1 << 20
LIMITS = {'keys': 14, 'queries': 16, 'mix': 12, 'ffn': 44, 'outer': 14, 'back_query': 24, 'back_key': 34}
F32 = jnp.float32
LOW = jnp.bfloat16


def dot_nn(left, right):
    return lax.dot_general(left, right, (((1,), (0,)), ((), ())), preferred_element_type=F32)


def dot_nt(left, right):
    return lax.dot_general(left, right, (((1,), (1,)), ((), ())), preferred_element_type=F32)


def dot_tn(left, right):
    return lax.dot_general(left, right, (((0,), (0,)), ((), ())), preferred_element_type=F32)


def norm_parts(inputs):
    centre = inputs - jnp.mean(inputs, axis=-1, keepdims=True)
    root = lax.rsqrt(jnp.mean(centre * centre, axis=-1, keepdims=True) + NORM_EPS)
    return centre * root, root


def norm_back(grad, gain, unit, root):
    inner = grad * gain
    mean_inner = jnp.mean(inner, axis=-1, keepdims=True)
    return root * (inner - mean_inner - unit * jnp.mean(inner * unit, axis=-1, keepdims=True))


def causal(length):
    earlier = lax.broadcasted_iota(jnp.int32, (length, length), 0)
    return earlier <= lax.broadcasted_iota(jnp.int32, (length, length), 1)


def put_states(own_out, their_out, core, heads, size, states, copies):
    half = heads // 2
    base = half * size
    first = core[0] == 0
    own_out[0, base:] = jnp.zeros((SPARE, own_out.shape[2]), LOW)
    their_out[0, base:] = jnp.zeros((SPARE, own_out.shape[2]), LOW)
    for index in range(half):
        low, high = states[index], states[index + half]
        total_low, total_high = [
            sum(s[size + i : size + i + 1] for i in range(copies)) for s in (low, high)
        ]
        at = slice(index * size, (index + 1) * size)
        own_out[0, at] = jnp.where(first, low[:size], high[:size]).astype(LOW)
        their_out[0, at] = jnp.where(first, high[:size], low[:size]).astype(LOW)
        row = slice(base + index, base + index + 1)
        own_out[0, row] = jnp.where(first, total_low, total_high).astype(LOW)
        their_out[0, row] = jnp.where(first, total_high, total_low).astype(LOW)


def get_state(core, keep, come, head, heads, size, copies):
    part, index = divmod(head, heads // 2)
    base = heads // 2 * size
    own = core[0] == part
    total = jnp.where(own, keep[0, base : base + SPARE], come[0, base : base + SPARE]).astype(F32)[index : index + 1]
    line = lax.broadcasted_iota(jnp.int32, (SPARE, total.shape[1]), 0)
    spare = jnp.where(line < copies, total, 0.0).astype(LOW)
    rows = slice(index * size, (index + 1) * size)
    return jnp.concatenate([jnp.where(own, keep[0, rows], come[0, rows]), spare], axis=0)


def split_features(rows, scale, shift, high_out, stack, half):
    size = rows.shape[0]
    scaled = rows * scale
    high = scaled.astype(LOW)
    rest = (scaled - high.astype(F32)).astype(LOW)
    high_out[...] = high
    for part, piece in enumerate((high, high, rest, rest)):
        stack[part * size : (part + 1) * size] = piece
    half[...] = 0.5 * jnp.sum(scaled * scaled, axis=0, keepdims=True) + shift


def staged(count, *stages):
    for stage in stages:
        for item in range(count):
            stage(item)


def keys_kernel(
    heads,
    size,
    tok,
    norms,
    weights,
    omega,
    core,
    turned_out,
    uk_out,
    value_out,
    pk_out,
    own_out,
    their_out,
    rows,
    stacks,
    halves,
    states,
):
    width = heads * size
    length = tok.shape[1]
    unit, _ = norm_parts(tok[0].astype(F32))
    turned_out[0] = (unit * norms[0:1] + norms[1:2]).astype(LOW).T
    rows[...] = dot_nn(weights[width:], turned_out[0])
    spare = (lax.broadcasted_iota(jnp.int32, (SPARE, length), 0) < 2).astype(F32).astype(LOW)
    shift = 0.5 * math.log(omega.shape[0])

    def split(head):
        at = slice(head * size, (head + 1) * size)
        split_features(
            rows[at], size ** (-0.25), shift, uk_out.at[0, at], stacks.at[head], halves.at[head : head + 1]
        )
        value_out[0, head, :size] = rows[width + head * size : width + (head + 1) * size].astype(LOW)
        value_out[0, head, size:] = spare

    def feature(head):
        projected = dot_nn(omega[...], stacks[head])
        pk_out[0, head] = jnp.exp(projected - halves[head : head + 1]).astype(LOW)

    def local_state(head):
        states[head] = dot_nt(value_out[0, head], pk_out[0, head])

    staged(heads, split, feature, local_state)
    put_states(own_out, their_out, core, heads, size, states, 1)


def queries_kernel(heads, size, turned, weights, omega, value, pk, uq_out, pq_out, pq_copy, score_out, num_out, rows, stacks, halves):
    width = heads * size
    length = turned.shape[2]
    rows[...] = dot_nn(weights[:width], turned[0])
    shift = 0.5 * math.log(omega.shape[0])
    keep = causal(length)

    def split(head):
        at = slice(head * size, (head + 1) * size)
        split_features(
            rows[at], size ** (-0.25), shift, uq_out.at[0, at], stacks.at[head], halves.at[head : head + 1]
        )

    def feature(head):
        projected = dot_nn(omega[...], stacks[head])
        feat = jnp.exp(projected - halves[head : head + 1]).astype(LOW)
        pq_out[0, head] = feat
        pq_copy[0, head] = feat

    def score(head):
        score_out[0, head] = jnp.where(keep, dot_tn(pk[0, head], pq_out[0, head]), 0.0).astype(LOW)

    def numerator(head):
        num_out[0, head] = dot_nn(value[0, head], score_out[0, head])

    staged(heads, split, feature, score, numerator)


def mix_kernel(heads, size, tok, norms, out_weight, num, core, keep, come, pq, mixed_out, recip_out, middle_out, normed_out):
    state = (core, keep, come)
    for head in range(heads):
        at = head * size
        total = num[0, head] + dot_nn(get_state(*state, head, heads, size, 2), pq[0, head])
        recip = 1.0 / total[size : size + 1]
        mixed_out[0, at : at + size] = (total[:size] * recip).astype(LOW)
        recip_out[0, head : head + 1] = recip
    mixed = mixed_out[0]
    middle = tok[0].astype(F32) + dot_tn(mixed, out_weight[...])
    middle_out[0] = middle
    unit, _ = norm_parts(middle)
    normed_out[0] = (unit * norms[2:3] + norms[3:4]).astype(LOW)


def gelu_pair(hidden):
    slope = math.sqrt(2.0 / math.pi)
    square = hidden * hidden
    tanh = jnp.tanh(hidden * (slope + (slope * 0.044715) * square))
    upper = 0.5 + 0.5 * tanh
    inner = (0.5 * slope) + (1.5 * slope * 0.044715) * square
    return hidden * upper, upper + hidden * (1.0 - tanh * tanh) * inner


def ffn_kernel(
    groups,
    devices,
    found,
    normed,
    middle,
    target,
    norms,
    own_pair,
    their_pair,
    core,
    place,
    out,
    grad_out,
    leave,
    stay,
    norm_grad,
    first_sum,
    second_sum,
    pair,
):
    step = pl.program_id(0)
    half = pair.shape[3] // 2
    width = normed.shape[1]

    @pl.when(step == 0)
    def _():
        for index, (seq_jump, dp_jump) in enumerate(found):
            pair[place[0] ^ seq_jump, place[1] ^ dp_jump] = own_pair[index]
            pair[place[0] ^ (seq_jump ^ 1), place[1] ^ dp_jump] = their_pair[index]

    own = normed[...]
    grads = target[...]
    own_turned = own.T
    grads_turned = grads.T

    @pl.when(step == 0)
    def _():
        first_sum[...] = jnp.zeros_like(first_sum)
        second_sum[...] = jnp.zeros_like(second_sum)
        norm_grad[...] = jnp.zeros_like(norm_grad)

    result = jnp.zeros(own.shape, F32)
    grad_normed = jnp.zeros(own.shape, F32)
    for group in range(groups):
        first = pair[group, :, :, :half].reshape(width, half)
        second = pair[group, :, :, half:].reshape(width, half)
        active, slope = gelu_pair(dot_nn(own, first))
        active = active.astype(LOW)
        result = result + dot_nt(active, second)
        grad_hidden = (dot_nn(grads, second) * slope).astype(LOW)
        grad_normed = grad_normed + dot_nt(grad_hidden, first)
        first_sum[group] += dot_nn(own_turned, grad_hidden)
        second_sum[group] += dot_nn(grads_turned, active)
    rows = middle[...]
    out[...] = (rows + result).astype(LOW)
    unit, root = norm_parts(rows)
    grad_out[...] = grads.astype(F32) + norm_back(grad_normed, norms[2:3], unit, root)
    norm_grad[0:1] += jnp.sum(grad_normed * unit, axis=0, keepdims=True)
    norm_grad[1:2] += jnp.sum(grad_normed, axis=0, keepdims=True)

    @pl.when(step == pl.num_programs(0) - 1)
    def _():
        mine = core[0]
        count = normed.shape[1] // devices
        for chip in range(groups // 2):
            at = 2 * half * chip
            for side, target_ref in ((mine, stay), (1 - mine, leave)):
                for place in range(devices):
                    spot = place // 2 + (place % 2) * (devices // 2)
                    rows_in = slice(place * count, (place + 1) * count)
                    rows_out = slice(spot * count, (spot + 1) * count)
                    target_ref[rows_out, at : at + half] = first_sum[2 * chip + side, rows_in].astype(LOW)
                    target_ref[rows_out, at + half : at + 2 * half] = second_sum[2 * chip + side, rows_in].astype(LOW)


def through_omega(flow, scaled, omega_low, size):
    back = dot_nn(omega_low, flow)
    return ((back[:size] - scaled.astype(F32) * back[size : size + 1]) * size ** (-0.25))


def outer_kernel(
    heads, size, grad_middle, out_weight, mixed, recip, pq, core, outer_out, own_out, their_out, out_proj, grad_mixed, states
):
    length = grad_middle.shape[1]

    @pl.when(pl.program_id(0) == 0)
    def _():
        out_proj[...] = jnp.zeros_like(out_proj)

    grad_low = grad_middle[0].astype(LOW)
    grad_mixed[...] = dot_nt(out_weight[...], grad_low)
    out_proj[...] += dot_nn(mixed[0], grad_low)
    line = lax.broadcasted_iota(jnp.int32, (SPARE, length), 0)

    def scale(head):
        at = head * size
        outer = grad_mixed[at : at + size] * recip[0, head : head + 1]
        centre = -jnp.sum(outer * mixed[0, at : at + size].astype(F32), axis=0, keepdims=True)
        rest = centre - centre.astype(LOW).astype(F32)
        outer_out[0, head, :size] = outer.astype(LOW)
        outer_out[0, head, size:] = jnp.where(line == 0, centre, jnp.where(line == 1, rest, 0.0)).astype(LOW)

    def local_state(head):
        states[head] = dot_nt(outer_out[0, head], pq[0, head])

    staged(heads, scale, local_state)
    put_states(own_out, their_out, core, heads, size, states, 2)


def back_query_kernel(
    heads,
    size,
    turned,
    omega_low,
    outers,
    value,
    pq,
    pk,
    scores,
    core,
    keep_state,
    come_state,
    uq,
    uk,
    query_out,
    key_out,
    value_out,
    query_weight,
    befores,
    grad_scores,
    flows,
    key_flows,
):
    @pl.when(pl.program_id(0) == 0)
    def _():
        query_weight[...] = jnp.zeros_like(query_weight)

    keep = causal(turned.shape[2])

    def score(head):
        befores[head] = get_state(core, keep_state, come_state, head, heads, size, 2)
        grad_scores[head] = jnp.where(keep, dot_tn(value[0, head], outers[0, head]), 0.0).astype(LOW)

    def feature(head):
        at = head * size
        grad_feat = dot_nn(pk[0, head], grad_scores[head]) + dot_tn(befores[head], outers[0, head])
        flows[head] = (grad_feat * pq[0, head].astype(F32)).astype(LOW)
        grad_key_feat = dot_nt(pq[0, head], grad_scores[head])
        key_flows[head] = (grad_key_feat * pk[0, head].astype(F32)).astype(LOW)
        value_out[0, at : at + size] = dot_nt(outers[0, head], scores[0, head])[:size].astype(LOW)

    def query(head):
        at = head * size
        query_out[0, at : at + size] = through_omega(flows[head], uq[0, at : at + size], omega_low[...], size).astype(
            LOW
        )
        key_out[0, at : at + size] = through_omega(key_flows[head], uk[0, at : at + size], omega_low[...], size).astype(LOW)

    staged(heads, score, feature, query)
    query_weight[...] += dot_nt(turned[0], query_out[0])


def back_key_kernel(
    heads,
    size,
    layout,
    tok,
    norms,
    grad_middle,
    weights,
    omega_low,
    value,
    pk,
    core,
    keep_state,
    come_state,
    uk,
    query_grad,
    key_part,
    value_part,
    query_weight,
    out_proj,
    norm_two,
    turned,
    input_grad,
    leave,
    stay_left,
    stay_right,
    flat,
    laters,
    flows,
    pair_weight,
    norm_grad,
    whole,
):
    width = heads * size

    @pl.when(pl.program_id(0) == 0)
    def _():
        pair_weight[...] = jnp.zeros_like(pair_weight)
        norm_grad[...] = jnp.zeros_like(norm_grad)

    unit, root = norm_parts(tok[0].astype(F32))
    flat[:width] = query_grad[0]

    def later(head):
        laters[head] = get_state(core, keep_state, come_state, head, heads, size, 1)

    def feature(head):
        at = 2 * width + head * size
        grad_feat = dot_tn(laters[head], value[0, head])
        flows[head] = (grad_feat * pk[0, head].astype(F32)).astype(LOW)
        extra = dot_nn(laters[head], pk[0, head])[:size]
        flat[at : at + size] = (
            value_part[0, head * size : (head + 1) * size].astype(F32) + extra
        ).astype(LOW)

    def key(head):
        at = width + head * size
        part = slice(head * size, (head + 1) * size)
        total = key_part[0, part].astype(F32) + through_omega(flows[head], uk[0, part], omega_low[...], size)
        flat[at : at + size] = total.astype(LOW)

    staged(heads, later, feature, key)
    pair_weight[...] += dot_nt(turned[0], flat[width:])
    grad_normed = dot_tn(flat[...], weights[...])
    input_grad[0] = grad_middle[0] + norm_back(grad_normed, norms[0:1], unit, root)
    norm_grad[0:1] += jnp.sum(grad_normed * unit, axis=0, keepdims=True)
    norm_grad[1:2] += jnp.sum(grad_normed, axis=0, keepdims=True)

    @pl.when(pl.program_id(0) == pl.num_programs(0) - 1)
    def _():
        whole[:width] = query_weight[...]
        whole[width : 2 * width] = pair_weight[:, :width]
        whole[2 * width : 3 * width] = pair_weight[:, width:]
        whole[3 * width : 4 * width] = out_proj[...]
        whole[4 * width : 4 * width + 2] = norm_grad[...]
        whole[4 * width + 2 : 4 * width + 4] = norm_two[...]
        starts, rows, owners = layout
        half = width // 2
        first = core[0] == 0
        leave[...] = jnp.zeros_like(leave)
        for part, stay in enumerate((stay_left, stay_right)):
            count = leave.shape[1]
            stay[...] = jnp.zeros_like(stay)
            columns = slice(part * half, (part + 1) * half)
            for spot in range(count):
                low = starts[owners[part][spot]]
                high = starts[owners[part][spot + count]]
                low = whole[low : low + rows, columns]
                high = whole[high : high + rows, columns]
                stay[spot, :rows] = jnp.where(first, low, high)
                leave[part, spot, :rows] = jnp.where(first, high, low).astype(LOW)


def per_seq(shape, offset=0):
    rest = tuple(shape[1:])
    return pl.BlockSpec((1,) + rest, lambda i: (i + offset,) + (0,) * len(rest))


def fixed(shape):
    return pl.BlockSpec(tuple(shape), lambda i: (0,) * len(shape))


def call(kernel, steps, args, in_specs, outs, out_specs, name, flops, scratch=(), aliases=None, after=(), chip=None):
    if chip is not None:
        args = tuple(
            on_chip(a) if i in chip else off_chip(a) if math.prod(a.shape) >= BIG else a for i, a in enumerate(args)
        )
    if after:
        count, body = len(args), kernel
        args = tuple(args) + tuple(after)
        in_specs = list(in_specs) + [pl.BlockSpec(memory_space=pl.ANY)] * len(after)

        def kernel(*refs):
            body(*refs[:count], *refs[count + len(after) :])

    moved = sum(math.prod(a.shape) * jnp.dtype(a.dtype).itemsize for a in list(args) + list(outs))
    return pl.pallas_call(
        kernel,
        grid=(steps,),
        in_specs=in_specs,
        out_specs=out_specs,
        out_shape=outs,
        scratch_shapes=list(scratch),
        name=name,
        input_output_aliases=aliases or {},
        compiler_params=pltpu.CompilerParams(
            dimension_semantics=("arbitrary",), vmem_limit_bytes=LIMITS[name] * 1024 * 1024
        ),
        cost_estimate=pl.CostEstimate(
            flops=flops, bytes_accessed=moved if flops > 1 else 1, transcendentals=0
        ),
    )(*args)


def on_chip(value):
    return pltpu.with_memory_space_constraint(value, pltpu.VMEM)


def off_chip(value):
    return pltpu.with_memory_space_constraint(value, pltpu.HBM)


def array(shape, dtype):
    return pltpu.HBM(tuple(shape), dtype)


def flip(value, axis, bit):
    return lax.ppermute(value, axis, [(i, i ^ (1 << bit)) for i in range(lax.axis_size(axis))])


def bit_of(axis, bit):
    return (lax.axis_index(axis) >> bit) & 1


def send_half(own, their, forward, tie):
    count = lax.axis_size("seq")
    beside = flip(their, "seq", 0)
    mine = (own.astype(F32) + beside.astype(F32)).astype(LOW)
    mine, tie = lax.optimization_barrier((mine, tie))
    far = None
    for step in range(1, count // 2):
        hop = 2 * step if forward else -2 * step
        pairs = [(i, i + hop) for i in range(count) if 0 <= i + hop < count]
        come = lax.ppermute(mine, "seq", pairs)
        far = come if far is None else far + come
    return beside, far, tie


def receive_half(own, beside, far, forward):
    core = bit_of("seq", 0)
    giver = (core == 0) if forward else (core == 1)
    give = (far.astype(F32) + jnp.where(giver, own.astype(F32), 0.0)).astype(LOW)
    keep = (far.astype(F32) + jnp.where(giver, 0.0, beside.astype(F32))).astype(LOW)
    return keep, flip(give, "seq", 0)


def axis_bits(axis):
    return lax.axis_size(axis).bit_length() - 1


def gather_orders():
    high = [("dp", bit) for bit in range(1, axis_bits("dp"))]
    seq_high = [("seq", bit) for bit in range(1, axis_bits("seq"))]
    near = [("dp", 0)]
    return [high + near + seq_high + [("seq", 0)], seq_high + high + near + [("seq", 0)]]


def scatter_orders():
    high = [("dp", bit) for bit in range(axis_bits("dp") - 1, 0, -1)]
    seq_high = [("seq", bit) for bit in range(axis_bits("seq") - 1, 0, -1)]
    near = [("dp", 0)]
    return [[("seq", 0)] + seq_high + near + high, [("seq", 0)] + near + high + seq_high]


def place_in(order, index):
    seq_bits = axis_bits("seq")
    spot = 0
    for axis, bit in order:
        shift = bit if axis == "seq" else bit + seq_bits
        spot = 2 * spot + ((index >> shift) & 1)
    return spot


def gather_more(value, found, axis, jumps):
    size = lax.axis_size(axis)
    come = [lax.ppermute(value, axis, [(i, i ^ jump) for i in range(size)]) for jump in jumps]
    more = list(found)
    for jump in jumps:
        more += [(a ^ jump, b) if axis == "seq" else (a, b ^ jump) for a, b in found]
    return jnp.concatenate([value] + come, axis=0), more


def gather_doubling(value, order, late, prepare=None):
    value = value[None]
    for step, (axis, bit) in enumerate(order):
        if step == len(order) - 2:
            value, late = lax.optimization_barrier((value, late))
        come = flip(value, axis, bit)
        if step == 0 and prepare is not None:
            come, late = lax.optimization_barrier((come, late))
            late = prepare(late)
        low = bit_of(axis, bit) == 0
        value = jnp.concatenate([jnp.where(low, value, come), jnp.where(low, come, value)], axis=0)
    return value, late


def total_of(terms):
    return sum(term.astype(F32) for term in terms)


def scatter_step(terms, axis, bit, late=None):
    mine = bit_of(axis, bit)
    leave = total_of([lax.dynamic_index_in_dim(term, 1 - mine, 0, keepdims=False) for term in terms]).astype(LOW)
    if late is not None:
        leave, late = lax.optimization_barrier((leave, late))
    come = flip(leave, axis, bit)
    stay = total_of([lax.dynamic_index_in_dim(term, mine, 0, keepdims=False) for term in terms])
    return [stay, come], late


def split_rows(terms, axis, bits, low, tie):
    ways = 1 << len(bits)
    terms = [t.reshape(-1, ways, low, t.shape[1]) for t in terms]
    shift = min(bits)
    mine = (lax.axis_index(axis) >> shift) & (ways - 1)

    def part(which):
        total = total_of([lax.dynamic_index_in_dim(t, which, 1, keepdims=False) for t in terms]).astype(LOW)
        return total.reshape(-1, total.shape[-1])

    leaving = [part(mine ^ other) for other in range(1, ways)]
    leaving, tie = lax.optimization_barrier((leaving, tie))
    size = lax.axis_size(axis)
    come = [
        lax.ppermute(leave, axis, [(i, i ^ (other << shift)) for i in range(size)])
        for other, leave in enumerate(leaving, 1)
    ]
    return tie, [part(mine)] + come


def adamw(weight, first, second, grad, rate, decay):
    first_new = BETA_FIRST * first + (1.0 - BETA_FIRST) * grad
    second_new = BETA_SECOND * second + (1.0 - BETA_SECOND) * grad * grad
    first_hat = first_new / (1.0 - BETA_FIRST**STEP)
    second_hat = second_new / (1.0 - BETA_SECOND**STEP)
    weight_new = weight - rate * (first_hat / (jnp.sqrt(second_hat) + ADAM_EPS) + decay * weight)
    return (weight_new, first_new, second_new)


def unpack_kernel(starts, spots, rows, left, right, wide_out, out_weight, norms, whole):
    whole[...] = jnp.zeros_like(whole)
    half = left.shape[2]
    for index, start in enumerate(starts):
        whole[start : start + rows, :half] += left[spots[0][index], :rows].astype(F32)
        whole[start : start + rows, half:] += right[spots[1][index], :rows].astype(F32)
    width = out_weight.shape[0]
    for part in range(3):
        wide_out[part * width : (part + 1) * width] = whole[part * width : (part + 1) * width].astype(LOW).T
    out_weight[...] = whole[3 * width : 4 * width].astype(LOW)
    norms[...] = whole[4 * width : 4 * width + 4]


def shards(
    tokens,
    cotangent,
    masked,
    omega,
    att_weights,
    att_first,
    att_second,
    ffn_in,
    ffn_out,
    ffn_in_first,
    ffn_in_second,
    ffn_out_first,
    ffn_out_second,
):
    seqs, length, width = tokens.shape
    size, count = omega.shape
    heads = width // size
    square = width * width
    groups = lax.axis_size("seq")
    devices = lax.axis_size("dp") * groups
    shard_len = att_weights.shape[0]
    place = lax.axis_index(("dp", "seq"))
    starts = [(i * shard_len) // width for i in range(devices)]
    offsets = [(i * shard_len) % width for i in range(devices)]
    rows = -(-(max(offsets) + shard_len) // width)
    held_rows = -(-rows // 8) * 8
    offset = (place * shard_len) % width

    framed = lax.dynamic_update_slice(
        jnp.zeros((held_rows * width,), LOW), att_weights.astype(LOW), (offset,)
    ).reshape(held_rows, width)
    group_width = ffn_in.shape[1]
    ffn_pair = (ffn_in, ffn_out)
    halves = [framed[:, : width // 2], framed[:, width // 2 :]]
    gathered = []

    def beside(shards):
        return jnp.concatenate([shards[0].astype(LOW), shards[1].astype(LOW).T], axis=1)[None]

    for half, order in zip(halves, gather_orders()):
        whole, ffn_pair = gather_doubling(half, order, ffn_pair, None if gathered else beside)
        gathered.append(whole)
    spots = [[place_in(order[::-1], i) for i in range(devices)] for order in gather_orders()]
    whole_rows = -(-(starts[-1] + rows) // 8) * 8
    group_width = ffn_in.shape[1]
    pair = ffn_pair
    top = lax.axis_size("dp") // 4
    pair, found = gather_more(pair, [(0, 0)], "dp", [top, 2 * top, 3 * top])
    for bit in range(axis_bits("dp") - 3, 0, -1):
        pair, found = gather_more(pair, found, "dp", [1 << bit])
    pair, gathered = lax.optimization_barrier((pair, gathered))


    weights, out_weight, norms = pl.pallas_call(
        functools.partial(unpack_kernel, starts, spots, rows),
        out_shape=[pltpu.VMEM((3 * width, width), LOW), pltpu.VMEM((width, width), LOW), pltpu.VMEM((4, width), F32)],
        scratch_shapes=[pltpu.VMEM((whole_rows, width), F32)],
        name="unpack",
        compiler_params=pltpu.CompilerParams(vmem_limit_bytes=VMEM_LIMIT),
    )(*gathered)

    first_shape = (width, groups * group_width)
    target = (cotangent.astype(F32) * masked.astype(F32)[:, :, None]).astype(LOW)
    omega_high = lax.reduce_precision(omega, 8, 7)
    omega_rest = omega - omega_high
    omega_parts = jnp.concatenate([omega_high, omega_rest, omega_high, omega_rest], axis=0).T.astype(LOW)
    omega_low = jnp.concatenate(
        [omega, jnp.ones((1, count), F32), jnp.zeros((SPARE - 1, count), F32)], axis=0
    ).astype(LOW)

    ext = size + SPARE
    unit = 2 * heads * length * length * length * seqs
    flat = (seqs, width, length)
    feat = (seqs, heads, count, length)
    held = (seqs, heads, ext, length)
    score_shape = (seqs, heads, length, length)
    recip_shape = (seqs, heads, length)
    state_rows = heads // 2 * size + SPARE
    state_shape = (seqs, state_rows, count)
    core = bit_of("seq", 0).astype(jnp.int32).reshape(1)
    place_both = jnp.stack([lax.axis_index("seq"), lax.axis_index("dp")]).astype(jnp.int32)
    in_smem = pl.BlockSpec(memory_space=pltpu.SMEM)

    def spec(value):
        return per_seq(value.shape) if value.shape[0] == seqs else fixed(value.shape)

    def scratch_rows(parts):
        return [
            pltpu.VMEM((parts * width, length), F32),
            pltpu.VMEM((heads, 4 * size, length), LOW),
            pltpu.VMEM((heads, length), F32),
        ]

    pair, omega_parts = lax.optimization_barrier((pair, omega_parts))
    for bit in range(1, axis_bits("seq")):
        pair, found = gather_more(pair, found, "seq", [1 << bit])
    args = (tokens, norms, weights, omega_parts)
    outs = [array(flat, LOW)] * 2 + [array(held, LOW), pltpu.VMEM(feat, LOW)] + [pltpu.VMEM(state_shape, LOW)] * 2
    turned, uk, value, pk, own, their = call(
        functools.partial(keys_kernel, heads, size),
        seqs,
        args + (core,),
        [spec(a) for a in args] + [in_smem],
        outs,
        [spec(a) for a in outs],
        "keys",
        1,
        chip=(),
        scratch=scratch_rows(2) + [pltpu.VMEM((heads, ext, count), F32)],
    )
    their, pair = lax.optimization_barrier((their, pair))
    beside, far, omega_tied = send_half(own, their, True, omega_parts)
    pair, omega_tied, pk = lax.optimization_barrier((pair, omega_tied, pk))
    pair, found = gather_more(pair, found, "dp", [1])
    args = (turned, weights, omega_tied, value, pk)
    outs = [array(flat, LOW), pltpu.VMEM(feat, LOW), array(feat, LOW), array(score_shape, LOW), pltpu.VMEM(held, F32)]
    uq, pq_near, pq, score, num = call(
        functools.partial(queries_kernel, heads, size),
        seqs,
        args,
        [spec(a) for a in args],
        outs,
        [spec(a) for a in outs],
        "queries",
        1,
        scratch_rows(1),
        chip=(4,),
    )
    far, uq, target, pair = lax.optimization_barrier((far, uq, target, pair))
    pair, mix_norms = lax.optimization_barrier((pair, norms))
    pair_beside = flip(pair, "seq", 0)
    keep, come = receive_half(own, beside, far, True)
    states = [per_seq(keep.shape)] * 2
    outs = [array(flat, LOW), array(recip_shape, F32), array(tokens.shape, F32), array(tokens.shape, LOW)]
    mixed, recip, middle, normed_two = call(
        functools.partial(mix_kernel, heads, size),
        seqs,
        (tokens, mix_norms, out_weight, num, core, keep, come, pq_near),
        [spec(tokens), spec(norms), spec(out_weight), spec(num), in_smem, *states, spec(pq_near)],
        outs,
        [spec(a) for a in outs],
        "mix",
        1,
        chip=(3, 7),
    )

    total_rows = seqs * length
    block = 2 * length
    by_block = pl.BlockSpec((block, width), lambda i: (i, 0))
    rows_shape = (total_rows, width)
    block_out, grad_middle, leave, stay, norm_two_grad = call(
        functools.partial(ffn_kernel, groups, lax.axis_size("dp"), found),
        total_rows // block,
        (*[a.reshape(rows_shape) for a in (normed_two, middle, target)], norms, pair, pair_beside, core, place_both),
        [by_block, by_block, by_block, fixed(norms.shape), fixed(pair.shape), fixed(pair.shape), in_smem, in_smem],
        [array(rows_shape, LOW), array(rows_shape, F32)] + [array(first_shape, LOW)] * 2 + [array((2, width), F32)],
        [by_block, by_block, fixed(first_shape), fixed(first_shape), fixed((2, width))],
        "ffn",
        20 * unit,
        chip=(),
        scratch=[pltpu.VMEM((groups, width, group_width), F32)] * 2
        + [pltpu.VMEM((groups, lax.axis_size("dp"), width // lax.axis_size("dp"), 2 * group_width), LOW)],
    )
    block_out = block_out.reshape(tokens.shape)
    grad_middle = grad_middle.reshape(tokens.shape)
    come_pair = flip(leave, "seq", 0)

    args = (grad_middle, out_weight, mixed, recip, pq)
    outs = [array(held, LOW)] + [pltpu.VMEM(state_shape, LOW)] * 2
    outs = outs + [array((width, width), F32)]
    outers, own, their, out_proj = call(
        functools.partial(outer_kernel, heads, size),
        seqs,
        args + (core,),
        [spec(a) for a in args] + [in_smem],
        outs,
        [spec(a) for a in outs],
        "outer",
        1,
        chip=(),
        scratch=[pltpu.VMEM((width, length), F32), pltpu.VMEM((heads, ext, count), F32)],
    )
    their, come_pair = lax.optimization_barrier((their, come_pair))
    dp_rows = width // lax.axis_size("dp")
    columns = stay.shape[1]
    near = bit_of("dp", 0)
    sent = total_of(
        [lax.dynamic_index_in_dim(t.reshape(2, width // 2, columns), 1 - near, 0, keepdims=False) for t in (stay, come_pair)]
    ).astype(LOW)
    sent, omega_low = lax.optimization_barrier((sent, omega_low))
    come_near = flip(sent, "dp", 0)
    beside, far, omega_low = send_half(own, their, False, omega_low)
    args = (turned, omega_low, outers, value, pq, pk, score, core, keep, come, uq, uk)
    outs = [array(flat, LOW)] * 3
    query_grad, key_part, value_part, query_weight = call(
        functools.partial(back_query_kernel, heads, size),
        seqs,
        args,
        [spec(a) for a in args[:7]] + [in_smem, *states, spec(uq), spec(uk)],
        outs + [array((width, width), F32)],
        [spec(a) for a in outs] + [fixed((width, width))],
        "back_query",
        1,
        chip=(),
        scratch=[
            pltpu.VMEM((heads, ext, count), LOW),
            pltpu.VMEM(score_shape[1:], LOW),
            pltpu.VMEM(feat[1:], LOW),
            pltpu.VMEM(feat[1:], LOW),
        ],
    )
    far, query_grad = lax.optimization_barrier((far, query_grad))
    keep, come = receive_half(own, beside, far, False)
    high = list(range(axis_bits("dp") - 1, 0, -1))
    ways = 1 << len(high[:2])
    low = width // 2 // ways
    chosen = (lax.axis_index("dp") >> (high[0] + 1 - len(high[:2]))) & (ways - 1)

    def part(which):
        pieces = [
            lax.dynamic_slice(t.reshape(2, ways, low, columns), (near, which, 0, 0), (1, 1, low, columns))
            for t in (stay, come_pair)
        ]
        pieces.append(lax.dynamic_index_in_dim(come_near.reshape(ways, low, columns), which, 0))
        return total_of([p.reshape(low, columns) for p in pieces]).astype(LOW)

    leaving = [part(chosen ^ other) for other in range(1, ways)]
    leaving, omega_low = lax.optimization_barrier((leaving, omega_low))
    terms = [part(chosen)]
    for other, leave_part in enumerate(leaving, 1):
        jump = other << (high[0] + 1 - len(high[:2]))
        terms.append(lax.ppermute(leave_part, "dp", [(i, i ^ jump) for i in range(lax.axis_size("dp"))]))
    orders = scatter_orders()
    owners = [sorted(range(devices), key=lambda i: place_in(order, i)) for order in orders]
    piece_shape = (2, devices // 2, held_rows, width // 2)
    args = (tokens, norms, grad_middle, weights, omega_low, value, pk, core, keep, come)
    more = (uk, query_grad, key_part, value_part, query_weight, out_proj, norm_two_grad, turned)
    input_grad, leave, *stays = call(
        functools.partial(back_key_kernel, heads, size, (starts, rows, owners)),
        seqs,
        args + more,
        [spec(a) for a in args[:7]] + [in_smem, *states] + [spec(a) for a in more],
        [array(tokens.shape, F32), array(piece_shape, LOW)] + [array(piece_shape[1:], F32)] * 2,
        [per_seq(tokens.shape), fixed(piece_shape)] + [fixed(piece_shape[1:])] * 2,
        "back_key",
        7 * unit,
        chip=(),
        scratch=[
            pltpu.VMEM((3 * width, length), LOW),
            pltpu.VMEM((heads, ext, count), LOW),
            pltpu.VMEM(feat[1:], LOW),
            pltpu.VMEM((width, 2 * width), F32),
            pltpu.VMEM((2, width), F32),
            pltpu.VMEM((whole_rows, width), F32),
        ],
    )
    leave, terms = lax.optimization_barrier((leave, terms))
    come_pieces = flip(leave, "seq", 0)
    for step, bit in enumerate(high[2:]):
        omega_low, terms = split_rows(terms, "dp", [bit], dp_rows << (len(high) - 3 - step), omega_low)
    terms = [total_of(terms)]
    for bit in range(axis_bits("seq") - 1, 0, -1):
        terms = [t.reshape(t.shape[0], 2, -1) for t in terms]
        side = bit_of("seq", bit)
        sent = total_of([lax.dynamic_index_in_dim(t, 1 - side, 1, keepdims=False) for t in terms]).astype(LOW)
        kept = total_of([lax.dynamic_index_in_dim(t, side, 1, keepdims=False) for t in terms])
        terms = [kept, flip(sent, "seq", bit)]
    sums = []
    for index, (stay, order) in enumerate(zip(stays, orders)):
        part = [stay, come_pieces[index]]
        for step, (axis, bit) in enumerate(order[1:]):
            part = [t.reshape((2, t.shape[0] // 2) + t.shape[1:]) for t in part]
            if index == 0 and step == 2:
                part, terms = scatter_step(part, axis, bit, terms)
            else:
                part, _ = scatter_step(part, axis, bit)
        sums.append(total_of(part)[0])
    own_pair = total_of(terms)
    grad_first = own_pair[:, :group_width]
    grad_second = own_pair[:, group_width:].T
    att_grad = jnp.concatenate(sums, axis=1)
    att_grad = lax.dynamic_slice(att_grad.reshape(-1), (offset,), (shard_len,)).astype(F32)

    position = place * shard_len + jnp.arange(shard_len, dtype=jnp.int32)
    is_matrix = position < 4 * square
    rate = jnp.where(is_matrix, RATE_MATRIX, RATE_NORM)
    decay = jnp.where(is_matrix, WEIGHT_DECAY, 0.0)
    att_new, att_first_new, att_second_new = adamw(
        att_weights, att_first, att_second, att_grad, rate, decay
    )
    ffn_in_new, ffn_in_first_new, ffn_in_second_new = adamw(
        ffn_in, ffn_in_first, ffn_in_second, grad_first, RATE_MATRIX, WEIGHT_DECAY
    )
    ffn_out_new, ffn_out_first_new, ffn_out_second_new = adamw(
        ffn_out, ffn_out_first, ffn_out_second, grad_second, RATE_MATRIX, WEIGHT_DECAY
    )
    return (
        block_out,
        input_grad,
        att_new,
        att_first_new,
        att_second_new,
        att_new.astype(jnp.bfloat16),
        ffn_in_new,
        ffn_in_first_new,
        ffn_in_second_new,
        ffn_in_new.astype(jnp.bfloat16),
        ffn_out_new,
        ffn_out_first_new,
        ffn_out_second_new,
        ffn_out_new.astype(jnp.bfloat16),
    )


def solution(mesh):
    in_specs = (
        P("dp", "seq", None),
        P("dp", "seq", None),
        P("dp", "seq"),
        P(),
        P(("dp", "seq")),
        P(("dp", "seq")),
        P(("dp", "seq")),
        P("dp", "seq"),
        P("seq", "dp"),
        P("dp", "seq"),
        P("dp", "seq"),
        P("seq", "dp"),
        P("seq", "dp"),
    )
    out_specs = (
        P("dp", "seq", None),
        P("dp", "seq", None),
        P(("dp", "seq")),
        P(("dp", "seq")),
        P(("dp", "seq")),
        P(("dp", "seq")),
        P("dp", "seq"),
        P("dp", "seq"),
        P("dp", "seq"),
        P("dp", "seq"),
        P("seq", "dp"),
        P("seq", "dp"),
        P("seq", "dp"),
        P("seq", "dp"),
    )
    return jax.shard_map(shards, mesh=mesh, in_specs=in_specs, out_specs=out_specs, check_vma=False)
```

```python
import functools
import math

import jax
import jax.numpy as jnp
from jax import lax
from jax.experimental import pallas as pl
from jax.experimental.pallas import tpu as pltpu
from jax.sharding import PartitionSpec as P

CH = 256
STEP = 10
BETA_FIRST = 0.9
BETA_SECOND = 0.999
ADAM_EPS = 1e-08
WEIGHT_DECAY = 0.1
RATE_MATRIX = 0.02
RATE_NORM = 0.3
NORM_EPS = 1e-05
SPARE = 16
VMEM_LIMIT = 16 * 1024 * 1024
BIG = 1 << 20
LIMITS = {'keys': 14, 'queries': 16, 'mix': 12, 'ffn': 44, 'outer': 14, 'back_query': 24, 'back_key': 34}
F32 = jnp.float32
LOW = jnp.bfloat16


def dot_nn(left, right):
    return lax.dot_general(left, right, (((1,), (0,)), ((), ())), preferred_element_type=F32)


def dot_nt(left, right):
    return lax.dot_general(left, right, (((1,), (1,)), ((), ())), preferred_element_type=F32)


def dot_tn(left, right):
    return lax.dot_general(left, right, (((0,), (0,)), ((), ())), preferred_element_type=F32)


def norm_parts(inputs):
    centre = inputs - jnp.mean(inputs, axis=-1, keepdims=True)
    root = lax.rsqrt(jnp.mean(centre * centre, axis=-1, keepdims=True) + NORM_EPS)
    return centre * root, root


def norm_back(grad, gain, unit, root):
    inner = grad * gain
    mean_inner = jnp.mean(inner, axis=-1, keepdims=True)
    return root * (inner - mean_inner - unit * jnp.mean(inner * unit, axis=-1, keepdims=True))


def causal(length):
    earlier = lax.broadcasted_iota(jnp.int32, (length, length), 0)
    return earlier <= lax.broadcasted_iota(jnp.int32, (length, length), 1)


def put_states(own_out, their_out, core, heads, size, states, copies):
    half = heads // 2
    base = half * size
    first = core[0] == 0
    own_out[0, base:] = jnp.zeros((SPARE, own_out.shape[2]), LOW)
    their_out[0, base:] = jnp.zeros((SPARE, own_out.shape[2]), LOW)
    for index in range(half):
        low, high = states[index], states[index + half]
        total_low, total_high = [
            sum(s[size + i : size + i + 1] for i in range(copies)) for s in (low, high)
        ]
        at = slice(index * size, (index + 1) * size)
        own_out[0, at] = jnp.where(first, low[:size], high[:size]).astype(LOW)
        their_out[0, at] = jnp.where(first, high[:size], low[:size]).astype(LOW)
        row = slice(base + index, base + index + 1)
        own_out[0, row] = jnp.where(first, total_low, total_high).astype(LOW)
        their_out[0, row] = jnp.where(first, total_high, total_low).astype(LOW)


def get_state(core, keep, come, head, heads, size, copies):
    part, index = divmod(head, heads // 2)
    base = heads // 2 * size
    own = core[0] == part
    total = jnp.where(own, keep[0, base : base + SPARE], come[0, base : base + SPARE]).astype(F32)[index : index + 1]
    line = lax.broadcasted_iota(jnp.int32, (SPARE, total.shape[1]), 0)
    spare = jnp.where(line < copies, total, 0.0).astype(LOW)
    rows = slice(index * size, (index + 1) * size)
    return jnp.concatenate([jnp.where(own, keep[0, rows], come[0, rows]), spare], axis=0)


def split_features(rows, scale, shift, high_out, stack, half):
    size = rows.shape[0]
    scaled = rows * scale
    high = scaled.astype(LOW)
    rest = (scaled - high.astype(F32)).astype(LOW)
    high_out[...] = high
    for part, piece in enumerate((high, high, rest, rest)):
        stack[part * size : (part + 1) * size] = piece
    half[...] = 0.5 * jnp.sum(scaled * scaled, axis=0, keepdims=True) + shift


def staged(count, *stages):
    for stage in stages:
        for item in range(count):
            stage(item)


def keys_kernel(
    heads,
    size,
    tok,
    norms,
    weights,
    omega,
    core,
    turned_out,
    uk_out,
    value_out,
    pk_out,
    own_out,
    their_out,
    rows,
    stacks,
    halves,
    states,
):
    width = heads * size
    length = tok.shape[1]
    unit, _ = norm_parts(tok[0].astype(F32))
    turned_out[0] = (unit * norms[0:1] + norms[1:2]).astype(LOW).T
    rows[...] = dot_nn(weights[width:], turned_out[0])
    spare = (lax.broadcasted_iota(jnp.int32, (SPARE, length), 0) < 2).astype(F32).astype(LOW)
    shift = 0.5 * math.log(omega.shape[0])

    def split(head):
        at = slice(head * size, (head + 1) * size)
        split_features(
            rows[at], size ** (-0.25), shift, uk_out.at[0, at], stacks.at[head], halves.at[head : head + 1]
        )
        value_out[0, head, :size] = rows[width + head * size : width + (head + 1) * size].astype(LOW)
        value_out[0, head, size:] = spare

    def feature(head):
        projected = dot_nn(omega[...], stacks[head])
        pk_out[0, head] = jnp.exp(projected - halves[head : head + 1]).astype(LOW)

    def local_state(head):
        states[head] = dot_nt(value_out[0, head], pk_out[0, head])

    staged(heads, split, feature, local_state)
    put_states(own_out, their_out, core, heads, size, states, 1)


def queries_kernel(heads, size, turned, weights, omega, value, pk, uq_out, pq_out, pq_copy, score_out, num_out, rows, stacks, halves):
    width = heads * size
    length = turned.shape[2]
    rows[...] = dot_nn(weights[:width], turned[0])
    shift = 0.5 * math.log(omega.shape[0])
    keep = causal(length)

    def split(head):
        at = slice(head * size, (head + 1) * size)
        split_features(
            rows[at], size ** (-0.25), shift, uq_out.at[0, at], stacks.at[head], halves.at[head : head + 1]
        )

    def feature(head):
        projected = dot_nn(omega[...], stacks[head])
        feat = jnp.exp(projected - halves[head : head + 1]).astype(LOW)
        pq_out[0, head] = feat
        pq_copy[0, head] = feat

    def score(head):
        score_out[0, head] = jnp.where(keep, dot_tn(pk[0, head], pq_out[0, head]), 0.0).astype(LOW)

    def numerator(head):
        num_out[0, head] = dot_nn(value[0, head], score_out[0, head])

    staged(heads, split, feature, score, numerator)


def mix_kernel(heads, size, tok, norms, out_weight, num, core, keep, come, pq, mixed_out, recip_out, middle_out, normed_out):
    state = (core, keep, come)
    for head in range(heads):
        at = head * size
        total = num[0, head] + dot_nn(get_state(*state, head, heads, size, 2), pq[0, head])
        recip = 1.0 / total[size : size + 1]
        mixed_out[0, at : at + size] = (total[:size] * recip).astype(LOW)
        recip_out[0, head : head + 1] = recip
    mixed = mixed_out[0]
    middle = tok[0].astype(F32) + dot_tn(mixed, out_weight[...])
    middle_out[0] = middle
    unit, _ = norm_parts(middle)
    normed_out[0] = (unit * norms[2:3] + norms[3:4]).astype(LOW)


def gelu_pair(hidden):
    slope = math.sqrt(2.0 / math.pi)
    square = hidden * hidden
    tanh = jnp.tanh(hidden * (slope + (slope * 0.044715) * square))
    upper = 0.5 + 0.5 * tanh
    inner = (0.5 * slope) + (1.5 * slope * 0.044715) * square
    return hidden * upper, upper + hidden * (1.0 - tanh * tanh) * inner


def ffn_kernel(
    groups,
    devices,
    found,
    normed,
    middle,
    target,
    norms,
    own_pair,
    their_pair,
    core,
    place,
    out,
    grad_out,
    leave,
    stay,
    norm_grad,
    first_sum,
    second_sum,
    pair,
):
    step = pl.program_id(0)
    half = pair.shape[3] // 2
    width = normed.shape[1]

    @pl.when(step == 0)
    def _():
        for index, (seq_jump, dp_jump) in enumerate(found):
            pair[place[0] ^ seq_jump, place[1] ^ dp_jump] = own_pair[index]
            pair[place[0] ^ (seq_jump ^ 1), place[1] ^ dp_jump] = their_pair[index]

    own = normed[...]
    grads = target[...]
    own_turned = own.T
    grads_turned = grads.T

    @pl.when(step == 0)
    def _():
        first_sum[...] = jnp.zeros_like(first_sum)
        second_sum[...] = jnp.zeros_like(second_sum)
        norm_grad[...] = jnp.zeros_like(norm_grad)

    result = jnp.zeros(own.shape, F32)
    grad_normed = jnp.zeros(own.shape, F32)
    for group in range(groups):
        first = pair[group, :, :, :half].reshape(width, half)
        second = pair[group, :, :, half:].reshape(width, half)
        active, slope = gelu_pair(dot_nn(own, first))
        active = active.astype(LOW)
        result = result + dot_nt(active, second)
        grad_hidden = (dot_nn(grads, second) * slope).astype(LOW)
        grad_normed = grad_normed + dot_nt(grad_hidden, first)
        first_sum[group] += dot_nn(own_turned, grad_hidden)
        second_sum[group] += dot_nn(grads_turned, active)
    rows = middle[...]
    out[...] = (rows + result).astype(LOW)
    unit, root = norm_parts(rows)
    grad_out[...] = grads.astype(F32) + norm_back(grad_normed, norms[2:3], unit, root)
    norm_grad[0:1] += jnp.sum(grad_normed * unit, axis=0, keepdims=True)
    norm_grad[1:2] += jnp.sum(grad_normed, axis=0, keepdims=True)

    @pl.when(step == pl.num_programs(0) - 1)
    def _():
        mine = core[0]
        count = normed.shape[1] // devices
        for chip in range(groups // 2):
            at = 2 * half * chip
            for side, target_ref in ((mine, stay), (1 - mine, leave)):
                for place in range(devices):
                    spot = place // 2 + (place % 2) * (devices // 2)
                    rows_in = slice(place * count, (place + 1) * count)
                    rows_out = slice(spot * count, (spot + 1) * count)
                    target_ref[rows_out, at : at + half] = first_sum[2 * chip + side, rows_in].astype(LOW)
                    target_ref[rows_out, at + half : at + 2 * half] = second_sum[2 * chip + side, rows_in].astype(LOW)


def through_omega(flow, scaled, omega_low, size):
    back = dot_nn(omega_low, flow)
    return ((back[:size] - scaled.astype(F32) * back[size : size + 1]) * size ** (-0.25))


def outer_kernel(
    heads, size, grad_middle, out_weight, mixed, recip, pq, core, outer_out, own_out, their_out, out_proj, grad_mixed, states
):
    length = grad_middle.shape[1]

    @pl.when(pl.program_id(0) == 0)
    def _():
        out_proj[...] = jnp.zeros_like(out_proj)

    grad_low = grad_middle[0].astype(LOW)
    grad_mixed[...] = dot_nt(out_weight[...], grad_low)
    out_proj[...] += dot_nn(mixed[0], grad_low)
    line = lax.broadcasted_iota(jnp.int32, (SPARE, length), 0)

    def scale(head):
        at = head * size
        outer = grad_mixed[at : at + size] * recip[0, head : head + 1]
        centre = -jnp.sum(outer * mixed[0, at : at + size].astype(F32), axis=0, keepdims=True)
        rest = centre - centre.astype(LOW).astype(F32)
        outer_out[0, head, :size] = outer.astype(LOW)
        outer_out[0, head, size:] = jnp.where(line == 0, centre, jnp.where(line == 1, rest, 0.0)).astype(LOW)

    def local_state(head):
        states[head] = dot_nt(outer_out[0, head], pq[0, head])

    staged(heads, scale, local_state)
    put_states(own_out, their_out, core, heads, size, states, 2)


def back_query_kernel(
    heads,
    size,
    turned,
    omega_low,
    outers,
    value,
    pq,
    pk,
    scores,
    core,
    keep_state,
    come_state,
    uq,
    uk,
    query_out,
    key_out,
    value_out,
    query_weight,
    befores,
    grad_scores,
    flows,
    key_flows,
):
    @pl.when(pl.program_id(0) == 0)
    def _():
        query_weight[...] = jnp.zeros_like(query_weight)

    keep = causal(turned.shape[2])

    def score(head):
        befores[head] = get_state(core, keep_state, come_state, head, heads, size, 2)
        grad_scores[head] = jnp.where(keep, dot_tn(value[0, head], outers[0, head]), 0.0).astype(LOW)

    def feature(head):
        at = head * size
        grad_feat = dot_nn(pk[0, head], grad_scores[head]) + dot_tn(befores[head], outers[0, head])
        flows[head] = (grad_feat * pq[0, head].astype(F32)).astype(LOW)
        grad_key_feat = dot_nt(pq[0, head], grad_scores[head])
        key_flows[head] = (grad_key_feat * pk[0, head].astype(F32)).astype(LOW)
        value_out[0, at : at + size] = dot_nt(outers[0, head], scores[0, head])[:size].astype(LOW)

    def query(head):
        at = head * size
        query_out[0, at : at + size] = through_omega(flows[head], uq[0, at : at + size], omega_low[...], size).astype(
            LOW
        )
        key_out[0, at : at + size] = through_omega(key_flows[head], uk[0, at : at + size], omega_low[...], size).astype(LOW)

    staged(heads, score, feature, query)
    query_weight[...] += dot_nt(turned[0], query_out[0])


def back_key_kernel(
    heads,
    size,
    layout,
    tok,
    norms,
    grad_middle,
    weights,
    omega_low,
    value,
    pk,
    core,
    keep_state,
    come_state,
    uk,
    query_grad,
    key_part,
    value_part,
    query_weight,
    out_proj,
    norm_two,
    turned,
    input_grad,
    leave,
    stay_left,
    stay_right,
    flat,
    laters,
    flows,
    pair_weight,
    norm_grad,
    whole,
):
    width = heads * size

    @pl.when(pl.program_id(0) == 0)
    def _():
        pair_weight[...] = jnp.zeros_like(pair_weight)
        norm_grad[...] = jnp.zeros_like(norm_grad)

    unit, root = norm_parts(tok[0].astype(F32))
    flat[:width] = query_grad[0]

    def later(head):
        laters[head] = get_state(core, keep_state, come_state, head, heads, size, 1)

    def feature(head):
        at = 2 * width + head * size
        grad_feat = dot_tn(laters[head], value[0, head])
        flows[head] = (grad_feat * pk[0, head].astype(F32)).astype(LOW)
        extra = dot_nn(laters[head], pk[0, head])[:size]
        flat[at : at + size] = (
            value_part[0, head * size : (head + 1) * size].astype(F32) + extra
        ).astype(LOW)

    def key(head):
        at = width + head * size
        part = slice(head * size, (head + 1) * size)
        total = key_part[0, part].astype(F32) + through_omega(flows[head], uk[0, part], omega_low[...], size)
        flat[at : at + size] = total.astype(LOW)

    staged(heads, later, feature, key)
    pair_weight[...] += dot_nt(turned[0], flat[width:])
    grad_normed = dot_tn(flat[...], weights[...])
    input_grad[0] = grad_middle[0] + norm_back(grad_normed, norms[0:1], unit, root)
    norm_grad[0:1] += jnp.sum(grad_normed * unit, axis=0, keepdims=True)
    norm_grad[1:2] += jnp.sum(grad_normed, axis=0, keepdims=True)

    @pl.when(pl.program_id(0) == pl.num_programs(0) - 1)
    def _():
        whole[:width] = query_weight[...]
        whole[width : 2 * width] = pair_weight[:, :width]
        whole[2 * width : 3 * width] = pair_weight[:, width:]
        whole[3 * width : 4 * width] = out_proj[...]
        whole[4 * width : 4 * width + 2] = norm_grad[...]
        whole[4 * width + 2 : 4 * width + 4] = norm_two[...]
        starts, rows, owners = layout
        half = width // 2
        first = core[0] == 0
        leave[...] = jnp.zeros_like(leave)
        for part, stay in enumerate((stay_left, stay_right)):
            count = leave.shape[1]
            stay[...] = jnp.zeros_like(stay)
            columns = slice(part * half, (part + 1) * half)
            for spot in range(count):
                low = starts[owners[part][spot]]
                high = starts[owners[part][spot + count]]
                low = whole[low : low + rows, columns]
                high = whole[high : high + rows, columns]
                stay[spot, :rows] = jnp.where(first, low, high)
                leave[part, spot, :rows] = jnp.where(first, high, low).astype(LOW)


def per_seq(shape, offset=0):
    rest = tuple(shape[1:])
    return pl.BlockSpec((1,) + rest, lambda i: (i + offset,) + (0,) * len(rest))


def fixed(shape):
    return pl.BlockSpec(tuple(shape), lambda i: (0,) * len(shape))


def call(kernel, steps, args, in_specs, outs, out_specs, name, flops, scratch=(), aliases=None, after=(), chip=None):
    if chip is not None:
        args = tuple(
            on_chip(a) if i in chip else off_chip(a) if math.prod(a.shape) >= BIG else a for i, a in enumerate(args)
        )
    if after:
        count, body = len(args), kernel
        args = tuple(args) + tuple(after)
        in_specs = list(in_specs) + [pl.BlockSpec(memory_space=pl.ANY)] * len(after)

        def kernel(*refs):
            body(*refs[:count], *refs[count + len(after) :])

    moved = sum(math.prod(a.shape) * jnp.dtype(a.dtype).itemsize for a in list(args) + list(outs))
    return pl.pallas_call(
        kernel,
        grid=(steps,),
        in_specs=in_specs,
        out_specs=out_specs,
        out_shape=outs,
        scratch_shapes=list(scratch),
        name=name,
        input_output_aliases=aliases or {},
        compiler_params=pltpu.CompilerParams(
            dimension_semantics=("arbitrary",), vmem_limit_bytes=LIMITS[name] * 1024 * 1024
        ),
        cost_estimate=pl.CostEstimate(
            flops=flops, bytes_accessed=moved if flops > 1 else 1, transcendentals=0
        ),
    )(*args)


def on_chip(value):
    return pltpu.with_memory_space_constraint(value, pltpu.VMEM)


def off_chip(value):
    return pltpu.with_memory_space_constraint(value, pltpu.HBM)


def array(shape, dtype):
    return pltpu.HBM(tuple(shape), dtype)


def flip(value, axis, bit):
    return lax.ppermute(value, axis, [(i, i ^ (1 << bit)) for i in range(lax.axis_size(axis))])


def bit_of(axis, bit):
    return (lax.axis_index(axis) >> bit) & 1


def send_half(own, their, forward, tie):
    count = lax.axis_size("seq")
    beside = flip(their, "seq", 0)
    mine = (own.astype(F32) + beside.astype(F32)).astype(LOW)
    mine, tie = lax.optimization_barrier((mine, tie))
    far = None
    for step in range(1, count // 2):
        hop = 2 * step if forward else -2 * step
        pairs = [(i, i + hop) for i in range(count) if 0 <= i + hop < count]
        come = lax.ppermute(mine, "seq", pairs)
        far = come if far is None else far + come
    return beside, far, tie


def receive_half(own, beside, far, forward):
    core = bit_of("seq", 0)
    giver = (core == 0) if forward else (core == 1)
    give = (far.astype(F32) + jnp.where(giver, own.astype(F32), 0.0)).astype(LOW)
    keep = (far.astype(F32) + jnp.where(giver, 0.0, beside.astype(F32))).astype(LOW)
    return keep, flip(give, "seq", 0)


def axis_bits(axis):
    return lax.axis_size(axis).bit_length() - 1


def gather_orders():
    high = [("dp", bit) for bit in range(1, axis_bits("dp"))]
    seq_high = [("seq", bit) for bit in range(1, axis_bits("seq"))]
    near = [("dp", 0)]
    return [high + near + seq_high + [("seq", 0)], seq_high + high + near + [("seq", 0)]]


def scatter_orders():
    high = [("dp", bit) for bit in range(axis_bits("dp") - 1, 0, -1)]
    seq_high = [("seq", bit) for bit in range(axis_bits("seq") - 1, 0, -1)]
    near = [("dp", 0)]
    return [[("seq", 0)] + seq_high + near + high, [("seq", 0)] + near + high + seq_high]


def place_in(order, index):
    seq_bits = axis_bits("seq")
    spot = 0
    for axis, bit in order:
        shift = bit if axis == "seq" else bit + seq_bits
        spot = 2 * spot + ((index >> shift) & 1)
    return spot


def gather_more(value, found, axis, jumps):
    size = lax.axis_size(axis)
    come = [lax.ppermute(value, axis, [(i, i ^ jump) for i in range(size)]) for jump in jumps]
    more = list(found)
    for jump in jumps:
        more += [(a ^ jump, b) if axis == "seq" else (a, b ^ jump) for a, b in found]
    return jnp.concatenate([value] + come, axis=0), more


def gather_doubling(value, order, late, prepare=None):
    value = value[None]
    for step, (axis, bit) in enumerate(order):
        if step == len(order) - 2:
            value, late = lax.optimization_barrier((value, late))
        come = flip(value, axis, bit)
        if step == 0 and prepare is not None:
            come, late = lax.optimization_barrier((come, late))
            late = prepare(late)
        low = bit_of(axis, bit) == 0
        value = jnp.concatenate([jnp.where(low, value, come), jnp.where(low, come, value)], axis=0)
    return value, late


def total_of(terms):
    return sum(term.astype(F32) for term in terms)


def scatter_step(terms, axis, bit, late=None):
    mine = bit_of(axis, bit)
    leave = total_of([lax.dynamic_index_in_dim(term, 1 - mine, 0, keepdims=False) for term in terms]).astype(LOW)
    if late is not None:
        leave, late = lax.optimization_barrier((leave, late))
    come = flip(leave, axis, bit)
    stay = total_of([lax.dynamic_index_in_dim(term, mine, 0, keepdims=False) for term in terms])
    return [stay, come], late


def split_rows(terms, axis, bits, low, tie):
    ways = 1 << len(bits)
    terms = [t.reshape(-1, ways, low, t.shape[1]) for t in terms]
    shift = min(bits)
    mine = (lax.axis_index(axis) >> shift) & (ways - 1)

    def part(which):
        total = total_of([lax.dynamic_index_in_dim(t, which, 1, keepdims=False) for t in terms]).astype(LOW)
        return total.reshape(-1, total.shape[-1])

    leaving = [part(mine ^ other) for other in range(1, ways)]
    leaving, tie = lax.optimization_barrier((leaving, tie))
    size = lax.axis_size(axis)
    come = [
        lax.ppermute(leave, axis, [(i, i ^ (other << shift)) for i in range(size)])
        for other, leave in enumerate(leaving, 1)
    ]
    return tie, [part(mine)] + come


def adamw(weight, first, second, grad, rate, decay):
    first_new = BETA_FIRST * first + (1.0 - BETA_FIRST) * grad
    second_new = BETA_SECOND * second + (1.0 - BETA_SECOND) * grad * grad
    first_hat = first_new / (1.0 - BETA_FIRST**STEP)
    second_hat = second_new / (1.0 - BETA_SECOND**STEP)
    weight_new = weight - rate * (first_hat / (jnp.sqrt(second_hat) + ADAM_EPS) + decay * weight)
    return (weight_new, first_new, second_new)


def unpack_kernel(starts, spots, rows, left, right, wide_out, out_weight, norms, whole):
    whole[...] = jnp.zeros_like(whole)
    half = left.shape[2]
    for index, start in enumerate(starts):
        whole[start : start + rows, :half] += left[spots[0][index], :rows].astype(F32)
        whole[start : start + rows, half:] += right[spots[1][index], :rows].astype(F32)
    width = out_weight.shape[0]
    for part in range(3):
        wide_out[part * width : (part + 1) * width] = whole[part * width : (part + 1) * width].astype(LOW).T
    out_weight[...] = whole[3 * width : 4 * width].astype(LOW)
    norms[...] = whole[4 * width : 4 * width + 4]


def shards(
    tokens,
    cotangent,
    masked,
    omega,
    att_weights,
    att_first,
    att_second,
    ffn_in,
    ffn_out,
    ffn_in_first,
    ffn_in_second,
    ffn_out_first,
    ffn_out_second,
):
    seqs, length, width = tokens.shape
    size, count = omega.shape
    heads = width // size
    square = width * width
    groups = lax.axis_size("seq")
    devices = lax.axis_size("dp") * groups
    shard_len = att_weights.shape[0]
    place = lax.axis_index(("dp", "seq"))
    starts = [(i * shard_len) // width for i in range(devices)]
    offsets = [(i * shard_len) % width for i in range(devices)]
    rows = -(-(max(offsets) + shard_len) // width)
    held_rows = -(-rows // 8) * 8
    offset = (place * shard_len) % width

    framed = lax.dynamic_update_slice(
        jnp.zeros((held_rows * width,), LOW), att_weights.astype(LOW), (offset,)
    ).reshape(held_rows, width)
    group_width = ffn_in.shape[1]
    ffn_pair = (ffn_in, ffn_out)
    halves = [framed[:, : width // 2], framed[:, width // 2 :]]
    gathered = []

    def beside(shards):
        return jnp.concatenate([shards[0].astype(LOW), shards[1].astype(LOW).T], axis=1)[None]

    for half, order in zip(halves, gather_orders()):
        whole, ffn_pair = gather_doubling(half, order, ffn_pair, None if gathered else beside)
        gathered.append(whole)
    spots = [[place_in(order[::-1], i) for i in range(devices)] for order in gather_orders()]
    whole_rows = -(-(starts[-1] + rows) // 8) * 8
    group_width = ffn_in.shape[1]
    pair = ffn_pair
    top = lax.axis_size("dp") // 4
    pair, found = gather_more(pair, [(0, 0)], "dp", [top, 2 * top, 3 * top])
    for bit in range(axis_bits("dp") - 3, 0, -1):
        pair, found = gather_more(pair, found, "dp", [1 << bit])
    pair, gathered = lax.optimization_barrier((pair, gathered))


    weights, out_weight, norms = pl.pallas_call(
        functools.partial(unpack_kernel, starts, spots, rows),
        out_shape=[pltpu.VMEM((3 * width, width), LOW), pltpu.VMEM((width, width), LOW), pltpu.VMEM((4, width), F32)],
        scratch_shapes=[pltpu.VMEM((whole_rows, width), F32)],
        name="unpack",
        compiler_params=pltpu.CompilerParams(vmem_limit_bytes=VMEM_LIMIT),
    )(*gathered)

    first_shape = (width, groups * group_width)
    target = (cotangent.astype(F32) * masked.astype(F32)[:, :, None]).astype(LOW)
    omega_high = lax.reduce_precision(omega, 8, 7)
    omega_rest = omega - omega_high
    omega_parts = jnp.concatenate([omega_high, omega_rest, omega_high, omega_rest], axis=0).T.astype(LOW)
    omega_low = jnp.concatenate(
        [omega, jnp.ones((1, count), F32), jnp.zeros((SPARE - 1, count), F32)], axis=0
    ).astype(LOW)

    ext = size + SPARE
    unit = 2 * heads * length * length * length * seqs
    flat = (seqs, width, length)
    feat = (seqs, heads, count, length)
    held = (seqs, heads, ext, length)
    score_shape = (seqs, heads, length, length)
    recip_shape = (seqs, heads, length)
    state_rows = heads // 2 * size + SPARE
    state_shape = (seqs, state_rows, count)
    core = bit_of("seq", 0).astype(jnp.int32).reshape(1)
    place_both = jnp.stack([lax.axis_index("seq"), lax.axis_index("dp")]).astype(jnp.int32)
    in_smem = pl.BlockSpec(memory_space=pltpu.SMEM)

    def spec(value):
        return per_seq(value.shape) if value.shape[0] == seqs else fixed(value.shape)

    def scratch_rows(parts):
        return [
            pltpu.VMEM((parts * width, length), F32),
            pltpu.VMEM((heads, 4 * size, length), LOW),
            pltpu.VMEM((heads, length), F32),
        ]

    pair, omega_parts = lax.optimization_barrier((pair, omega_parts))
    for bit in range(1, axis_bits("seq")):
        pair, found = gather_more(pair, found, "seq", [1 << bit])
    args = (tokens, norms, weights, omega_parts)
    outs = [array(flat, LOW)] * 2 + [array(held, LOW), pltpu.VMEM(feat, LOW)] + [pltpu.VMEM(state_shape, LOW)] * 2
    turned, uk, value, pk, own, their = call(
        functools.partial(keys_kernel, heads, size),
        seqs,
        args + (core,),
        [spec(a) for a in args] + [in_smem],
        outs,
        [spec(a) for a in outs],
        "keys",
        1,
        chip=(),
        scratch=scratch_rows(2) + [pltpu.VMEM((heads, ext, count), F32)],
    )
    their, pair = lax.optimization_barrier((their, pair))
    beside, far, omega_tied = send_half(own, their, True, omega_parts)
    pair, omega_tied, pk = lax.optimization_barrier((pair, omega_tied, pk))
    pair, found = gather_more(pair, found, "dp", [1])
    args = (turned, weights, omega_tied, value, pk)
    outs = [array(flat, LOW), pltpu.VMEM(feat, LOW), array(feat, LOW), array(score_shape, LOW), pltpu.VMEM(held, F32)]
    uq, pq_near, pq, score, num = call(
        functools.partial(queries_kernel, heads, size),
        seqs,
        args,
        [spec(a) for a in args],
        outs,
        [spec(a) for a in outs],
        "queries",
        1,
        scratch_rows(1),
        chip=(4,),
    )
    far, uq, target, pair = lax.optimization_barrier((far, uq, target, pair))
    keep, come = receive_half(own, beside, far, True)
    pair, come, mix_norms = lax.optimization_barrier((pair, come, norms))
    pair_beside = flip(pair, "seq", 0)
    states = [per_seq(keep.shape)] * 2
    outs = [array(flat, LOW), array(recip_shape, F32), array(tokens.shape, F32), array(tokens.shape, LOW)]
    mixed, recip, middle, normed_two = call(
        functools.partial(mix_kernel, heads, size),
        seqs,
        (tokens, mix_norms, out_weight, num, core, keep, come, pq_near),
        [spec(tokens), spec(norms), spec(out_weight), spec(num), in_smem, *states, spec(pq_near)],
        outs,
        [spec(a) for a in outs],
        "mix",
        1,
        chip=(3, 7),
    )

    total_rows = seqs * length
    block = 2 * length
    by_block = pl.BlockSpec((block, width), lambda i: (i, 0))
    rows_shape = (total_rows, width)
    block_out, grad_middle, leave, stay, norm_two_grad = call(
        functools.partial(ffn_kernel, groups, lax.axis_size("dp"), found),
        total_rows // block,
        (*[a.reshape(rows_shape) for a in (normed_two, middle, target)], norms, pair, pair_beside, core, place_both),
        [by_block, by_block, by_block, fixed(norms.shape), fixed(pair.shape), fixed(pair.shape), in_smem, in_smem],
        [array(rows_shape, LOW), array(rows_shape, F32)] + [array(first_shape, LOW)] * 2 + [array((2, width), F32)],
        [by_block, by_block, fixed(first_shape), fixed(first_shape), fixed((2, width))],
        "ffn",
        20 * unit,
        chip=(),
        scratch=[pltpu.VMEM((groups, width, group_width), F32)] * 2
        + [pltpu.VMEM((groups, lax.axis_size("dp"), width // lax.axis_size("dp"), 2 * group_width), LOW)],
    )
    block_out = block_out.reshape(tokens.shape)
    grad_middle = grad_middle.reshape(tokens.shape)
    come_pair = flip(leave, "seq", 0)

    args = (grad_middle, out_weight, mixed, recip, pq)
    outs = [array(held, LOW)] + [array(state_shape, LOW)] * 2
    outs = outs + [array((width, width), F32)]
    outers, own, their, out_proj = call(
        functools.partial(outer_kernel, heads, size),
        seqs,
        args + (core,),
        [spec(a) for a in args] + [in_smem],
        outs,
        [spec(a) for a in outs],
        "outer",
        1,
        chip=(),
        scratch=[pltpu.VMEM((width, length), F32), pltpu.VMEM((heads, ext, count), F32)],
    )
    their, come_pair = lax.optimization_barrier((their, come_pair))
    dp_rows = width // lax.axis_size("dp")
    columns = stay.shape[1]
    near = bit_of("dp", 0)
    sent = total_of(
        [lax.dynamic_index_in_dim(t.reshape(2, width // 2, columns), 1 - near, 0, keepdims=False) for t in (stay, come_pair)]
    ).astype(LOW)
    sent, omega_low = lax.optimization_barrier((sent, omega_low))
    come_near = flip(sent, "dp", 0)
    beside, far, omega_low = send_half(own, their, False, omega_low)
    args = (turned, omega_low, outers, value, pq, pk, score, core, keep, come, uq, uk)
    outs = [array(flat, LOW)] * 3
    query_grad, key_part, value_part, query_weight = call(
        functools.partial(back_query_kernel, heads, size),
        seqs,
        args,
        [spec(a) for a in args[:7]] + [in_smem, *states, spec(uq), spec(uk)],
        outs + [array((width, width), F32)],
        [spec(a) for a in outs] + [fixed((width, width))],
        "back_query",
        1,
        chip=(),
        scratch=[
            pltpu.VMEM((heads, ext, count), LOW),
            pltpu.VMEM(score_shape[1:], LOW),
            pltpu.VMEM(feat[1:], LOW),
            pltpu.VMEM(feat[1:], LOW),
        ],
    )
    far, query_grad = lax.optimization_barrier((far, query_grad))
    keep, come = receive_half(own, beside, far, False)
    high = list(range(axis_bits("dp") - 1, 0, -1))
    ways = 1 << len(high[:2])
    low = width // 2 // ways
    chosen = (lax.axis_index("dp") >> (high[0] + 1 - len(high[:2]))) & (ways - 1)

    def part(which):
        pieces = [
            lax.dynamic_slice(t.reshape(2, ways, low, columns), (near, which, 0, 0), (1, 1, low, columns))
            for t in (stay, come_pair)
        ]
        pieces.append(lax.dynamic_index_in_dim(come_near.reshape(ways, low, columns), which, 0))
        return total_of([p.reshape(low, columns) for p in pieces]).astype(LOW)

    leaving = [part(chosen ^ other) for other in range(1, ways)]
    leaving, omega_low = lax.optimization_barrier((leaving, omega_low))
    terms = [part(chosen)]
    for other, leave_part in enumerate(leaving, 1):
        jump = other << (high[0] + 1 - len(high[:2]))
        terms.append(lax.ppermute(leave_part, "dp", [(i, i ^ jump) for i in range(lax.axis_size("dp"))]))
    orders = scatter_orders()
    owners = [sorted(range(devices), key=lambda i: place_in(order, i)) for order in orders]
    piece_shape = (2, devices // 2, held_rows, width // 2)
    args = (tokens, norms, grad_middle, weights, omega_low, value, pk, core, keep, come)
    more = (uk, query_grad, key_part, value_part, query_weight, out_proj, norm_two_grad, turned)
    input_grad, leave, *stays = call(
        functools.partial(back_key_kernel, heads, size, (starts, rows, owners)),
        seqs,
        args + more,
        [spec(a) for a in args[:7]] + [in_smem, *states] + [spec(a) for a in more],
        [array(tokens.shape, F32), array(piece_shape, LOW)] + [array(piece_shape[1:], F32)] * 2,
        [per_seq(tokens.shape), fixed(piece_shape)] + [fixed(piece_shape[1:])] * 2,
        "back_key",
        7 * unit,
        chip=(),
        scratch=[
            pltpu.VMEM((3 * width, length), LOW),
            pltpu.VMEM((heads, ext, count), LOW),
            pltpu.VMEM(feat[1:], LOW),
            pltpu.VMEM((width, 2 * width), F32),
            pltpu.VMEM((2, width), F32),
            pltpu.VMEM((whole_rows, width), F32),
        ],
    )
    leave, terms = lax.optimization_barrier((leave, terms))
    come_pieces = flip(leave, "seq", 0)
    for step, bit in enumerate(high[2:]):
        omega_low, terms = split_rows(terms, "dp", [bit], dp_rows << (len(high) - 3 - step), omega_low)
    terms = [total_of(terms)]
    for bit in range(axis_bits("seq") - 1, 0, -1):
        terms = [t.reshape(t.shape[0], 2, -1) for t in terms]
        side = bit_of("seq", bit)
        sent = total_of([lax.dynamic_index_in_dim(t, 1 - side, 1, keepdims=False) for t in terms]).astype(LOW)
        kept = total_of([lax.dynamic_index_in_dim(t, side, 1, keepdims=False) for t in terms])
        terms = [kept, flip(sent, "seq", bit)]
    sums = []
    for index, (stay, order) in enumerate(zip(stays, orders)):
        part = [stay, come_pieces[index]]
        for step, (axis, bit) in enumerate(order[1:]):
            part = [t.reshape((2, t.shape[0] // 2) + t.shape[1:]) for t in part]
            if index == 0 and step == 2:
                part, terms = scatter_step(part, axis, bit, terms)
            else:
                part, _ = scatter_step(part, axis, bit)
        sums.append(total_of(part)[0])
    own_pair = total_of(terms)
    grad_first = own_pair[:, :group_width]
    grad_second = own_pair[:, group_width:].T
    att_grad = jnp.concatenate(sums, axis=1)
    att_grad = lax.dynamic_slice(att_grad.reshape(-1), (offset,), (shard_len,)).astype(F32)

    position = place * shard_len + jnp.arange(shard_len, dtype=jnp.int32)
    is_matrix = position < 4 * square
    rate = jnp.where(is_matrix, RATE_MATRIX, RATE_NORM)
    decay = jnp.where(is_matrix, WEIGHT_DECAY, 0.0)
    att_new, att_first_new, att_second_new = adamw(
        att_weights, att_first, att_second, att_grad, rate, decay
    )
    ffn_in_new, ffn_in_first_new, ffn_in_second_new = adamw(
        ffn_in, ffn_in_first, ffn_in_second, grad_first, RATE_MATRIX, WEIGHT_DECAY
    )
    ffn_out_new, ffn_out_first_new, ffn_out_second_new = adamw(
        ffn_out, ffn_out_first, ffn_out_second, grad_second, RATE_MATRIX, WEIGHT_DECAY
    )
    return (
        block_out,
        input_grad,
        att_new,
        att_first_new,
        att_second_new,
        att_new.astype(jnp.bfloat16),
        ffn_in_new,
        ffn_in_first_new,
        ffn_in_second_new,
        ffn_in_new.astype(jnp.bfloat16),
        ffn_out_new,
        ffn_out_first_new,
        ffn_out_second_new,
        ffn_out_new.astype(jnp.bfloat16),
    )


def solution(mesh):
    in_specs = (
        P("dp", "seq", None),
        P("dp", "seq", None),
        P("dp", "seq"),
        P(),
        P(("dp", "seq")),
        P(("dp", "seq")),
        P(("dp", "seq")),
        P("dp", "seq"),
        P("seq", "dp"),
        P("dp", "seq"),
        P("dp", "seq"),
        P("seq", "dp"),
        P("seq", "dp"),
    )
    out_specs = (
        P("dp", "seq", None),
        P("dp", "seq", None),
        P(("dp", "seq")),
        P(("dp", "seq")),
        P(("dp", "seq")),
        P(("dp", "seq")),
        P("dp", "seq"),
        P("dp", "seq"),
        P("dp", "seq"),
        P("dp", "seq"),
        P("seq", "dp"),
        P("seq", "dp"),
        P("seq", "dp"),
        P("seq", "dp"),
    )
    return jax.shard_map(shards, mesh=mesh, in_specs=in_specs, out_specs=out_specs, check_vma=False)
```

```python
import functools
import math

import jax
import jax.numpy as jnp
from jax import lax
from jax.experimental import pallas as pl
from jax.experimental.pallas import tpu as pltpu
from jax.sharding import PartitionSpec as P

CH = 256
STEP = 10
BETA_FIRST = 0.9
BETA_SECOND = 0.999
ADAM_EPS = 1e-08
WEIGHT_DECAY = 0.1
RATE_MATRIX = 0.02
RATE_NORM = 0.3
NORM_EPS = 1e-05
SPARE = 16
VMEM_LIMIT = 16 * 1024 * 1024
BIG = 1 << 20
LIMITS = {'keys': 14, 'queries': 16, 'mix': 12, 'ffn': 40, 'outer': 14, 'back_query': 24, 'back_key': 34}
F32 = jnp.float32
LOW = jnp.bfloat16


def dot_nn(left, right):
    return lax.dot_general(left, right, (((1,), (0,)), ((), ())), preferred_element_type=F32)


def dot_nt(left, right):
    return lax.dot_general(left, right, (((1,), (1,)), ((), ())), preferred_element_type=F32)


def dot_tn(left, right):
    return lax.dot_general(left, right, (((0,), (0,)), ((), ())), preferred_element_type=F32)


def norm_parts(inputs):
    centre = inputs - jnp.mean(inputs, axis=-1, keepdims=True)
    root = lax.rsqrt(jnp.mean(centre * centre, axis=-1, keepdims=True) + NORM_EPS)
    return centre * root, root


def norm_back(grad, gain, unit, root):
    inner = grad * gain
    mean_inner = jnp.mean(inner, axis=-1, keepdims=True)
    return root * (inner - mean_inner - unit * jnp.mean(inner * unit, axis=-1, keepdims=True))


def causal(length):
    earlier = lax.broadcasted_iota(jnp.int32, (length, length), 0)
    return earlier <= lax.broadcasted_iota(jnp.int32, (length, length), 1)


def put_states(own_out, their_out, core, heads, size, states, copies):
    half = heads // 2
    base = half * size
    first = core[0] == 0
    own_out[0, base:] = jnp.zeros((SPARE, own_out.shape[2]), LOW)
    their_out[0, base:] = jnp.zeros((SPARE, own_out.shape[2]), LOW)
    for index in range(half):
        low, high = states[index], states[index + half]
        total_low, total_high = [
            sum(s[size + i : size + i + 1] for i in range(copies)) for s in (low, high)
        ]
        at = slice(index * size, (index + 1) * size)
        own_out[0, at] = jnp.where(first, low[:size], high[:size]).astype(LOW)
        their_out[0, at] = jnp.where(first, high[:size], low[:size]).astype(LOW)
        row = slice(base + index, base + index + 1)
        own_out[0, row] = jnp.where(first, total_low, total_high).astype(LOW)
        their_out[0, row] = jnp.where(first, total_high, total_low).astype(LOW)


def get_state(core, keep, come, head, heads, size, copies):
    part, index = divmod(head, heads // 2)
    base = heads // 2 * size
    own = core[0] == part
    total = jnp.where(own, keep[0, base : base + SPARE], come[0, base : base + SPARE]).astype(F32)[index : index + 1]
    line = lax.broadcasted_iota(jnp.int32, (SPARE, total.shape[1]), 0)
    spare = jnp.where(line < copies, total, 0.0).astype(LOW)
    rows = slice(index * size, (index + 1) * size)
    return jnp.concatenate([jnp.where(own, keep[0, rows], come[0, rows]), spare], axis=0)


def split_features(rows, scale, shift, high_out, stack, half):
    size = rows.shape[0]
    scaled = rows * scale
    high = scaled.astype(LOW)
    rest = (scaled - high.astype(F32)).astype(LOW)
    high_out[...] = high
    for part, piece in enumerate((high, high, rest, rest)):
        stack[part * size : (part + 1) * size] = piece
    half[...] = 0.5 * jnp.sum(scaled * scaled, axis=0, keepdims=True) + shift


def staged(count, *stages):
    for stage in stages:
        for item in range(count):
            stage(item)


def keys_kernel(
    heads,
    size,
    tok,
    norms,
    weights,
    omega,
    core,
    turned_out,
    uk_out,
    value_out,
    pk_out,
    own_out,
    their_out,
    rows,
    stacks,
    halves,
    states,
):
    width = heads * size
    length = tok.shape[1]
    unit, _ = norm_parts(tok[0].astype(F32))
    turned_out[0] = (unit * norms[0:1] + norms[1:2]).astype(LOW).T
    rows[...] = dot_nn(weights[width:], turned_out[0])
    spare = (lax.broadcasted_iota(jnp.int32, (SPARE, length), 0) < 2).astype(F32).astype(LOW)
    shift = 0.5 * math.log(omega.shape[0])

    def split(head):
        at = slice(head * size, (head + 1) * size)
        split_features(
            rows[at], size ** (-0.25), shift, uk_out.at[0, at], stacks.at[head], halves.at[head : head + 1]
        )
        value_out[0, head, :size] = rows[width + head * size : width + (head + 1) * size].astype(LOW)
        value_out[0, head, size:] = spare

    def feature(head):
        projected = dot_nn(omega[...], stacks[head])
        pk_out[0, head] = jnp.exp(projected - halves[head : head + 1]).astype(LOW)

    def local_state(head):
        states[head] = dot_nt(value_out[0, head], pk_out[0, head])

    staged(heads, split, feature, local_state)
    put_states(own_out, their_out, core, heads, size, states, 1)


def queries_kernel(heads, size, turned, weights, omega, value, pk, uq_out, pq_out, pq_copy, score_out, num_out, rows, stacks, halves):
    width = heads * size
    length = turned.shape[2]
    rows[...] = dot_nn(weights[:width], turned[0])
    shift = 0.5 * math.log(omega.shape[0])
    keep = causal(length)

    def split(head):
        at = slice(head * size, (head + 1) * size)
        split_features(
            rows[at], size ** (-0.25), shift, uq_out.at[0, at], stacks.at[head], halves.at[head : head + 1]
        )

    def feature(head):
        projected = dot_nn(omega[...], stacks[head])
        feat = jnp.exp(projected - halves[head : head + 1]).astype(LOW)
        pq_out[0, head] = feat
        pq_copy[0, head] = feat

    def score(head):
        score_out[0, head] = jnp.where(keep, dot_tn(pk[0, head], pq_out[0, head]), 0.0).astype(LOW)

    def numerator(head):
        num_out[0, head] = dot_nn(value[0, head], score_out[0, head])

    staged(heads, split, feature, score, numerator)


def mix_kernel(heads, size, tok, norms, out_weight, num, core, keep, come, pq, mixed_out, recip_out, middle_out, normed_out):
    state = (core, keep, come)
    for head in range(heads):
        at = head * size
        total = num[0, head] + dot_nn(get_state(*state, head, heads, size, 2), pq[0, head])
        recip = 1.0 / total[size : size + 1]
        mixed_out[0, at : at + size] = (total[:size] * recip).astype(LOW)
        recip_out[0, head : head + 1] = recip
    mixed = mixed_out[0]
    middle = tok[0].astype(F32) + dot_tn(mixed, out_weight[...])
    middle_out[0] = middle
    unit, _ = norm_parts(middle)
    normed_out[0] = (unit * norms[2:3] + norms[3:4]).astype(LOW)


def gelu_pair(hidden):
    slope = math.sqrt(2.0 / math.pi)
    square = hidden * hidden
    tanh = jnp.tanh(hidden * (slope + (slope * 0.044715) * square))
    upper = 0.5 + 0.5 * tanh
    inner = (0.5 * slope) + (1.5 * slope * 0.044715) * square
    return hidden * upper, upper + hidden * (1.0 - tanh * tanh) * inner


def ffn_kernel(
    groups,
    devices,
    found,
    normed,
    middle,
    target,
    norms,
    own_pair,
    their_pair,
    core,
    place,
    out,
    grad_out,
    leave,
    stay,
    norm_grad,
    first_sum,
    second_sum,
    pair,
):
    step = pl.program_id(0)
    half = pair.shape[3] // 2
    width = normed.shape[1]

    @pl.when(step == 0)
    def _():
        for index, (seq_jump, dp_jump) in enumerate(found):
            pair[place[0] ^ seq_jump, place[1] ^ dp_jump] = own_pair[index]
            pair[place[0] ^ (seq_jump ^ 1), place[1] ^ dp_jump] = their_pair[index]

    own = normed[...]
    grads = target[...]
    own_turned = own.T
    grads_turned = grads.T

    @pl.when(step == 0)
    def _():
        first_sum[...] = jnp.zeros_like(first_sum)
        second_sum[...] = jnp.zeros_like(second_sum)
        norm_grad[...] = jnp.zeros_like(norm_grad)

    result = jnp.zeros(own.shape, F32)
    grad_normed = jnp.zeros(own.shape, F32)
    for group in range(groups):
        first = pair[group, :, :, :half].reshape(width, half)
        second = pair[group, :, :, half:].reshape(width, half)
        active, slope = gelu_pair(dot_nn(own, first))
        active = active.astype(LOW)
        result = result + dot_nt(active, second)
        grad_hidden = (dot_nn(grads, second) * slope).astype(LOW)
        grad_normed = grad_normed + dot_nt(grad_hidden, first)
        first_sum[group] += dot_nn(own_turned, grad_hidden)
        second_sum[group] += dot_nn(grads_turned, active)
    rows = middle[...]
    out[...] = (rows + result).astype(LOW)
    unit, root = norm_parts(rows)
    grad_out[...] = grads.astype(F32) + norm_back(grad_normed, norms[2:3], unit, root)
    norm_grad[0:1] += jnp.sum(grad_normed * unit, axis=0, keepdims=True)
    norm_grad[1:2] += jnp.sum(grad_normed, axis=0, keepdims=True)

    @pl.when(step == pl.num_programs(0) - 1)
    def _():
        mine = core[0]
        count = normed.shape[1] // devices
        for chip in range(groups // 2):
            at = 2 * half * chip
            for side, target_ref in ((mine, stay), (1 - mine, leave)):
                for place in range(devices):
                    spot = place // 2 + (place % 2) * (devices // 2)
                    rows_in = slice(place * count, (place + 1) * count)
                    rows_out = slice(spot * count, (spot + 1) * count)
                    target_ref[rows_out, at : at + half] = first_sum[2 * chip + side, rows_in].astype(LOW)
                    target_ref[rows_out, at + half : at + 2 * half] = second_sum[2 * chip + side, rows_in].astype(LOW)


def through_omega(flow, scaled, omega_low, size):
    back = dot_nn(omega_low, flow)
    return ((back[:size] - scaled.astype(F32) * back[size : size + 1]) * size ** (-0.25))


def outer_kernel(
    heads, size, grad_middle, out_weight, mixed, recip, pq, core, outer_out, own_out, their_out, out_proj, grad_mixed, states
):
    length = grad_middle.shape[1]

    @pl.when(pl.program_id(0) == 0)
    def _():
        out_proj[...] = jnp.zeros_like(out_proj)

    grad_low = grad_middle[0].astype(LOW)
    grad_mixed[...] = dot_nt(out_weight[...], grad_low)
    out_proj[...] += dot_nn(mixed[0], grad_low)
    line = lax.broadcasted_iota(jnp.int32, (SPARE, length), 0)

    def scale(head):
        at = head * size
        outer = grad_mixed[at : at + size] * recip[0, head : head + 1]
        centre = -jnp.sum(outer * mixed[0, at : at + size].astype(F32), axis=0, keepdims=True)
        rest = centre - centre.astype(LOW).astype(F32)
        outer_out[0, head, :size] = outer.astype(LOW)
        outer_out[0, head, size:] = jnp.where(line == 0, centre, jnp.where(line == 1, rest, 0.0)).astype(LOW)

    def local_state(head):
        states[head] = dot_nt(outer_out[0, head], pq[0, head])

    staged(heads, scale, local_state)
    put_states(own_out, their_out, core, heads, size, states, 2)


def back_query_kernel(
    heads,
    size,
    turned,
    omega_low,
    outers,
    value,
    pq,
    pk,
    scores,
    core,
    keep_state,
    come_state,
    uq,
    uk,
    query_out,
    key_out,
    value_out,
    query_weight,
    befores,
    grad_scores,
    flows,
    key_flows,
):
    @pl.when(pl.program_id(0) == 0)
    def _():
        query_weight[...] = jnp.zeros_like(query_weight)

    keep = causal(turned.shape[2])

    def score(head):
        befores[head] = get_state(core, keep_state, come_state, head, heads, size, 2)
        grad_scores[head] = jnp.where(keep, dot_tn(value[0, head], outers[0, head]), 0.0).astype(LOW)

    def feature(head):
        at = head * size
        grad_feat = dot_nn(pk[0, head], grad_scores[head]) + dot_tn(befores[head], outers[0, head])
        flows[head] = (grad_feat * pq[0, head].astype(F32)).astype(LOW)
        grad_key_feat = dot_nt(pq[0, head], grad_scores[head])
        key_flows[head] = (grad_key_feat * pk[0, head].astype(F32)).astype(LOW)
        value_out[0, at : at + size] = dot_nt(outers[0, head], scores[0, head])[:size].astype(LOW)

    def query(head):
        at = head * size
        query_out[0, at : at + size] = through_omega(flows[head], uq[0, at : at + size], omega_low[...], size).astype(
            LOW
        )
        key_out[0, at : at + size] = through_omega(key_flows[head], uk[0, at : at + size], omega_low[...], size).astype(LOW)

    staged(heads, score, feature, query)
    query_weight[...] += dot_nt(turned[0], query_out[0])


def back_key_kernel(
    heads,
    size,
    layout,
    tok,
    norms,
    grad_middle,
    weights,
    omega_low,
    value,
    pk,
    core,
    keep_state,
    come_state,
    uk,
    query_grad,
    key_part,
    value_part,
    query_weight,
    out_proj,
    norm_two,
    turned,
    input_grad,
    leave,
    stay_left,
    stay_right,
    flat,
    laters,
    flows,
    pair_weight,
    norm_grad,
    whole,
):
    width = heads * size

    @pl.when(pl.program_id(0) == 0)
    def _():
        pair_weight[...] = jnp.zeros_like(pair_weight)
        norm_grad[...] = jnp.zeros_like(norm_grad)

    unit, root = norm_parts(tok[0].astype(F32))
    flat[:width] = query_grad[0]

    def later(head):
        laters[head] = get_state(core, keep_state, come_state, head, heads, size, 1)

    def feature(head):
        at = 2 * width + head * size
        grad_feat = dot_tn(laters[head], value[0, head])
        flows[head] = (grad_feat * pk[0, head].astype(F32)).astype(LOW)
        extra = dot_nn(laters[head], pk[0, head])[:size]
        flat[at : at + size] = (
            value_part[0, head * size : (head + 1) * size].astype(F32) + extra
        ).astype(LOW)

    def key(head):
        at = width + head * size
        part = slice(head * size, (head + 1) * size)
        total = key_part[0, part].astype(F32) + through_omega(flows[head], uk[0, part], omega_low[...], size)
        flat[at : at + size] = total.astype(LOW)

    staged(heads, later, feature, key)
    pair_weight[...] += dot_nt(turned[0], flat[width:])
    grad_normed = dot_tn(flat[...], weights[...])
    input_grad[0] = grad_middle[0] + norm_back(grad_normed, norms[0:1], unit, root)
    norm_grad[0:1] += jnp.sum(grad_normed * unit, axis=0, keepdims=True)
    norm_grad[1:2] += jnp.sum(grad_normed, axis=0, keepdims=True)

    @pl.when(pl.program_id(0) == pl.num_programs(0) - 1)
    def _():
        whole[:width] = query_weight[...]
        whole[width : 2 * width] = pair_weight[:, :width]
        whole[2 * width : 3 * width] = pair_weight[:, width:]
        whole[3 * width : 4 * width] = out_proj[...]
        whole[4 * width : 4 * width + 2] = norm_grad[...]
        whole[4 * width + 2 : 4 * width + 4] = norm_two[...]
        starts, rows, owners = layout
        half = width // 2
        first = core[0] == 0
        leave[...] = jnp.zeros_like(leave)
        for part, stay in enumerate((stay_left, stay_right)):
            count = leave.shape[1]
            stay[...] = jnp.zeros_like(stay)
            columns = slice(part * half, (part + 1) * half)
            for spot in range(count):
                low = starts[owners[part][spot]]
                high = starts[owners[part][spot + count]]
                low = whole[low : low + rows, columns]
                high = whole[high : high + rows, columns]
                stay[spot, :rows] = jnp.where(first, low, high)
                leave[part, spot, :rows] = jnp.where(first, high, low).astype(LOW)


def per_seq(shape, offset=0):
    rest = tuple(shape[1:])
    return pl.BlockSpec((1,) + rest, lambda i: (i + offset,) + (0,) * len(rest))


def fixed(shape):
    return pl.BlockSpec(tuple(shape), lambda i: (0,) * len(shape))


def call(kernel, steps, args, in_specs, outs, out_specs, name, flops, scratch=(), aliases=None, after=(), chip=None):
    if chip is not None:
        args = tuple(
            on_chip(a) if i in chip else off_chip(a) if math.prod(a.shape) >= BIG else a for i, a in enumerate(args)
        )
    if after:
        count, body = len(args), kernel
        args = tuple(args) + tuple(after)
        in_specs = list(in_specs) + [pl.BlockSpec(memory_space=pl.ANY)] * len(after)

        def kernel(*refs):
            body(*refs[:count], *refs[count + len(after) :])

    moved = sum(math.prod(a.shape) * jnp.dtype(a.dtype).itemsize for a in list(args) + list(outs))
    return pl.pallas_call(
        kernel,
        grid=(steps,),
        in_specs=in_specs,
        out_specs=out_specs,
        out_shape=outs,
        scratch_shapes=list(scratch),
        name=name,
        input_output_aliases=aliases or {},
        compiler_params=pltpu.CompilerParams(
            dimension_semantics=("arbitrary",), vmem_limit_bytes=LIMITS[name] * 1024 * 1024
        ),
        cost_estimate=pl.CostEstimate(
            flops=flops, bytes_accessed=moved if flops > 1 else 1, transcendentals=0
        ),
    )(*args)


def on_chip(value):
    return pltpu.with_memory_space_constraint(value, pltpu.VMEM)


def off_chip(value):
    return pltpu.with_memory_space_constraint(value, pltpu.HBM)


def array(shape, dtype):
    return pltpu.HBM(tuple(shape), dtype)


def flip(value, axis, bit):
    return lax.ppermute(value, axis, [(i, i ^ (1 << bit)) for i in range(lax.axis_size(axis))])


def bit_of(axis, bit):
    return (lax.axis_index(axis) >> bit) & 1


def send_half(own, their, forward, tie):
    count = lax.axis_size("seq")
    beside = flip(their, "seq", 0)
    mine = (own.astype(F32) + beside.astype(F32)).astype(LOW)
    mine, tie = lax.optimization_barrier((mine, tie))
    far = None
    for step in range(1, count // 2):
        hop = 2 * step if forward else -2 * step
        pairs = [(i, i + hop) for i in range(count) if 0 <= i + hop < count]
        come = lax.ppermute(mine, "seq", pairs)
        far = come if far is None else far + come
    return beside, far, tie


def receive_half(own, beside, far, forward):
    core = bit_of("seq", 0)
    giver = (core == 0) if forward else (core == 1)
    give = (far.astype(F32) + jnp.where(giver, own.astype(F32), 0.0)).astype(LOW)
    keep = (far.astype(F32) + jnp.where(giver, 0.0, beside.astype(F32))).astype(LOW)
    return keep, flip(give, "seq", 0)


def axis_bits(axis):
    return lax.axis_size(axis).bit_length() - 1


def gather_orders():
    high = [("dp", bit) for bit in range(1, axis_bits("dp"))]
    seq_high = [("seq", bit) for bit in range(1, axis_bits("seq"))]
    near = [("dp", 0)]
    return [high + near + seq_high + [("seq", 0)], seq_high + high + near + [("seq", 0)]]


def scatter_orders():
    high = [("dp", bit) for bit in range(axis_bits("dp") - 1, 0, -1)]
    seq_high = [("seq", bit) for bit in range(axis_bits("seq") - 1, 0, -1)]
    near = [("dp", 0)]
    return [[("seq", 0)] + seq_high + near + high, [("seq", 0)] + near + high + seq_high]


def place_in(order, index):
    seq_bits = axis_bits("seq")
    spot = 0
    for axis, bit in order:
        shift = bit if axis == "seq" else bit + seq_bits
        spot = 2 * spot + ((index >> shift) & 1)
    return spot


def gather_more(value, found, axis, jumps):
    size = lax.axis_size(axis)
    come = [lax.ppermute(value, axis, [(i, i ^ jump) for i in range(size)]) for jump in jumps]
    more = list(found)
    for jump in jumps:
        more += [(a ^ jump, b) if axis == "seq" else (a, b ^ jump) for a, b in found]
    return jnp.concatenate([value] + come, axis=0), more


def gather_doubling(value, order, late, prepare=None):
    value = value[None]
    for step, (axis, bit) in enumerate(order):
        if step == len(order) - 2:
            value, late = lax.optimization_barrier((value, late))
        come = flip(value, axis, bit)
        if step == 0 and prepare is not None:
            come, late = lax.optimization_barrier((come, late))
            late = prepare(late)
        low = bit_of(axis, bit) == 0
        value = jnp.concatenate([jnp.where(low, value, come), jnp.where(low, come, value)], axis=0)
    return value, late


def total_of(terms):
    return sum(term.astype(F32) for term in terms)


def scatter_step(terms, axis, bit, late=None):
    mine = bit_of(axis, bit)
    leave = total_of([lax.dynamic_index_in_dim(term, 1 - mine, 0, keepdims=False) for term in terms]).astype(LOW)
    if late is not None:
        leave, late = lax.optimization_barrier((leave, late))
    come = flip(leave, axis, bit)
    stay = total_of([lax.dynamic_index_in_dim(term, mine, 0, keepdims=False) for term in terms])
    return [stay, come], late


def split_rows(terms, axis, bits, low, tie):
    ways = 1 << len(bits)
    terms = [t.reshape(-1, ways, low, t.shape[1]) for t in terms]
    shift = min(bits)
    mine = (lax.axis_index(axis) >> shift) & (ways - 1)

    def part(which):
        total = total_of([lax.dynamic_index_in_dim(t, which, 1, keepdims=False) for t in terms]).astype(LOW)
        return total.reshape(-1, total.shape[-1])

    leaving = [part(mine ^ other) for other in range(1, ways)]
    leaving, tie = lax.optimization_barrier((leaving, tie))
    size = lax.axis_size(axis)
    come = [
        lax.ppermute(leave, axis, [(i, i ^ (other << shift)) for i in range(size)])
        for other, leave in enumerate(leaving, 1)
    ]
    return tie, [part(mine)] + come


def adamw(weight, first, second, grad, rate, decay):
    first_new = BETA_FIRST * first + (1.0 - BETA_FIRST) * grad
    second_new = BETA_SECOND * second + (1.0 - BETA_SECOND) * grad * grad
    first_hat = first_new / (1.0 - BETA_FIRST**STEP)
    second_hat = second_new / (1.0 - BETA_SECOND**STEP)
    weight_new = weight - rate * (first_hat / (jnp.sqrt(second_hat) + ADAM_EPS) + decay * weight)
    return (weight_new, first_new, second_new)


def unpack_kernel(starts, spots, rows, left, right, wide_out, out_weight, norms, whole):
    whole[...] = jnp.zeros_like(whole)
    half = left.shape[2]
    for index, start in enumerate(starts):
        whole[start : start + rows, :half] += left[spots[0][index], :rows].astype(F32)
        whole[start : start + rows, half:] += right[spots[1][index], :rows].astype(F32)
    width = out_weight.shape[0]
    for part in range(3):
        wide_out[part * width : (part + 1) * width] = whole[part * width : (part + 1) * width].astype(LOW).T
    out_weight[...] = whole[3 * width : 4 * width].astype(LOW)
    norms[...] = whole[4 * width : 4 * width + 4]


def shards(
    tokens,
    cotangent,
    masked,
    omega,
    att_weights,
    att_first,
    att_second,
    ffn_in,
    ffn_out,
    ffn_in_first,
    ffn_in_second,
    ffn_out_first,
    ffn_out_second,
):
    seqs, length, width = tokens.shape
    size, count = omega.shape
    heads = width // size
    square = width * width
    groups = lax.axis_size("seq")
    devices = lax.axis_size("dp") * groups
    shard_len = att_weights.shape[0]
    place = lax.axis_index(("dp", "seq"))
    starts = [(i * shard_len) // width for i in range(devices)]
    offsets = [(i * shard_len) % width for i in range(devices)]
    rows = -(-(max(offsets) + shard_len) // width)
    held_rows = -(-rows // 8) * 8
    offset = (place * shard_len) % width

    framed = lax.dynamic_update_slice(
        jnp.zeros((held_rows * width,), LOW), att_weights.astype(LOW), (offset,)
    ).reshape(held_rows, width)
    group_width = ffn_in.shape[1]
    ffn_pair = (ffn_in, ffn_out)
    halves = [framed[:, : width // 2], framed[:, width // 2 :]]
    gathered = []

    def beside(shards):
        return jnp.concatenate([shards[0].astype(LOW), shards[1].astype(LOW).T], axis=1)[None]

    for half, order in zip(halves, gather_orders()):
        whole, ffn_pair = gather_doubling(half, order, ffn_pair, None if gathered else beside)
        gathered.append(whole)
    spots = [[place_in(order[::-1], i) for i in range(devices)] for order in gather_orders()]
    whole_rows = -(-(starts[-1] + rows) // 8) * 8
    group_width = ffn_in.shape[1]
    pair = ffn_pair
    top = lax.axis_size("dp") // 4
    pair, found = gather_more(pair, [(0, 0)], "dp", [top, 2 * top, 3 * top])
    for bit in range(axis_bits("dp") - 3, 0, -1):
        pair, found = gather_more(pair, found, "dp", [1 << bit])
    pair, gathered = lax.optimization_barrier((pair, gathered))


    weights, out_weight, norms = pl.pallas_call(
        functools.partial(unpack_kernel, starts, spots, rows),
        out_shape=[pltpu.VMEM((3 * width, width), LOW), pltpu.VMEM((width, width), LOW), pltpu.VMEM((4, width), F32)],
        scratch_shapes=[pltpu.VMEM((whole_rows, width), F32)],
        name="unpack",
        compiler_params=pltpu.CompilerParams(vmem_limit_bytes=VMEM_LIMIT),
    )(*gathered)

    first_shape = (width, groups * group_width)
    target = (cotangent.astype(F32) * masked.astype(F32)[:, :, None]).astype(LOW)
    omega_high = lax.reduce_precision(omega, 8, 7)
    omega_rest = omega - omega_high
    omega_parts = jnp.concatenate([omega_high, omega_rest, omega_high, omega_rest], axis=0).T.astype(LOW)
    omega_low = jnp.concatenate(
        [omega, jnp.ones((1, count), F32), jnp.zeros((SPARE - 1, count), F32)], axis=0
    ).astype(LOW)

    ext = size + SPARE
    unit = 2 * heads * length * length * length * seqs
    flat = (seqs, width, length)
    feat = (seqs, heads, count, length)
    held = (seqs, heads, ext, length)
    score_shape = (seqs, heads, length, length)
    recip_shape = (seqs, heads, length)
    state_rows = heads // 2 * size + SPARE
    state_shape = (seqs, state_rows, count)
    core = bit_of("seq", 0).astype(jnp.int32).reshape(1)
    place_both = jnp.stack([lax.axis_index("seq"), lax.axis_index("dp")]).astype(jnp.int32)
    in_smem = pl.BlockSpec(memory_space=pltpu.SMEM)

    def spec(value):
        return per_seq(value.shape) if value.shape[0] == seqs else fixed(value.shape)

    def scratch_rows(parts):
        return [
            pltpu.VMEM((parts * width, length), F32),
            pltpu.VMEM((heads, 4 * size, length), LOW),
            pltpu.VMEM((heads, length), F32),
        ]

    pair, omega_parts = lax.optimization_barrier((pair, omega_parts))
    for bit in range(1, axis_bits("seq")):
        pair, found = gather_more(pair, found, "seq", [1 << bit])
    args = (tokens, norms, weights, omega_parts)
    outs = [array(flat, LOW)] * 2 + [array(held, LOW), pltpu.VMEM(feat, LOW)] + [pltpu.VMEM(state_shape, LOW)] * 2
    turned, uk, value, pk, own, their = call(
        functools.partial(keys_kernel, heads, size),
        seqs,
        args + (core,),
        [spec(a) for a in args] + [in_smem],
        outs,
        [spec(a) for a in outs],
        "keys",
        1,
        chip=(),
        scratch=scratch_rows(2) + [pltpu.VMEM((heads, ext, count), F32)],
    )
    their, pair = lax.optimization_barrier((their, pair))
    beside, far, omega_tied = send_half(own, their, True, omega_parts)
    pair, omega_tied, pk = lax.optimization_barrier((pair, omega_tied, pk))
    pair, found = gather_more(pair, found, "dp", [1])
    args = (turned, weights, omega_tied, value, pk)
    outs = [array(flat, LOW), pltpu.VMEM(feat, LOW), array(feat, LOW), array(score_shape, LOW), pltpu.VMEM(held, F32)]
    uq, pq_near, pq, score, num = call(
        functools.partial(queries_kernel, heads, size),
        seqs,
        args,
        [spec(a) for a in args],
        outs,
        [spec(a) for a in outs],
        "queries",
        1,
        scratch_rows(1),
        chip=(4,),
    )
    far, uq, target, pair = lax.optimization_barrier((far, uq, target, pair))
    keep, come = receive_half(own, beside, far, True)
    pair, come, mix_norms = lax.optimization_barrier((pair, come, norms))
    pair_beside = flip(pair, "seq", 0)
    states = [per_seq(keep.shape)] * 2
    outs = [array(flat, LOW), array(recip_shape, F32), array(tokens.shape, F32), array(tokens.shape, LOW)]
    mixed, recip, middle, normed_two = call(
        functools.partial(mix_kernel, heads, size),
        seqs,
        (tokens, mix_norms, out_weight, num, core, keep, come, pq_near),
        [spec(tokens), spec(norms), spec(out_weight), spec(num), in_smem, *states, spec(pq_near)],
        outs,
        [spec(a) for a in outs],
        "mix",
        1,
        chip=(3, 7),
    )

    total_rows = seqs * length
    block = 2 * length
    by_block = pl.BlockSpec((block, width), lambda i: (i, 0))
    rows_shape = (total_rows, width)
    block_out, grad_middle, leave, stay, norm_two_grad = call(
        functools.partial(ffn_kernel, groups, lax.axis_size("dp"), found),
        total_rows // block,
        (*[a.reshape(rows_shape) for a in (normed_two, middle, target)], norms, pair, pair_beside, core, place_both),
        [by_block, by_block, by_block, fixed(norms.shape), fixed(pair.shape), fixed(pair.shape), in_smem, in_smem],
        [array(rows_shape, LOW), array(rows_shape, F32)] + [array(first_shape, LOW)] * 2 + [array((2, width), F32)],
        [by_block, by_block, fixed(first_shape), fixed(first_shape), fixed((2, width))],
        "ffn",
        20 * unit,
        chip=(4, 5),
        scratch=[pltpu.VMEM((groups, width, group_width), F32)] * 2
        + [pltpu.VMEM((groups, lax.axis_size("dp"), width // lax.axis_size("dp"), 2 * group_width), LOW)],
    )
    block_out = block_out.reshape(tokens.shape)
    grad_middle = grad_middle.reshape(tokens.shape)
    come_pair = flip(leave, "seq", 0)

    args = (grad_middle, out_weight, mixed, recip, pq)
    outs = [array(held, LOW)] + [array(state_shape, LOW)] * 2
    outs = outs + [array((width, width), F32)]
    outers, own, their, out_proj = call(
        functools.partial(outer_kernel, heads, size),
        seqs,
        args + (core,),
        [spec(a) for a in args] + [in_smem],
        outs,
        [spec(a) for a in outs],
        "outer",
        1,
        chip=(),
        scratch=[pltpu.VMEM((width, length), F32), pltpu.VMEM((heads, ext, count), F32)],
    )
    their, come_pair = lax.optimization_barrier((their, come_pair))
    dp_rows = width // lax.axis_size("dp")
    columns = stay.shape[1]
    near = bit_of("dp", 0)
    sent = total_of(
        [lax.dynamic_index_in_dim(t.reshape(2, width // 2, columns), 1 - near, 0, keepdims=False) for t in (stay, come_pair)]
    ).astype(LOW)
    sent, omega_low = lax.optimization_barrier((sent, omega_low))
    come_near = flip(sent, "dp", 0)
    beside, far, omega_low = send_half(own, their, False, omega_low)
    args = (turned, omega_low, outers, value, pq, pk, score, core, keep, come, uq, uk)
    outs = [array(flat, LOW)] * 3
    query_grad, key_part, value_part, query_weight = call(
        functools.partial(back_query_kernel, heads, size),
        seqs,
        args,
        [spec(a) for a in args[:7]] + [in_smem, *states, spec(uq), spec(uk)],
        outs + [array((width, width), F32)],
        [spec(a) for a in outs] + [fixed((width, width))],
        "back_query",
        1,
        chip=(),
        scratch=[
            pltpu.VMEM((heads, ext, count), LOW),
            pltpu.VMEM(score_shape[1:], LOW),
            pltpu.VMEM(feat[1:], LOW),
            pltpu.VMEM(feat[1:], LOW),
        ],
    )
    far, query_grad = lax.optimization_barrier((far, query_grad))
    keep, come = receive_half(own, beside, far, False)
    high = list(range(axis_bits("dp") - 1, 0, -1))
    ways = 1 << len(high[:2])
    low = width // 2 // ways
    chosen = (lax.axis_index("dp") >> (high[0] + 1 - len(high[:2]))) & (ways - 1)

    def part(which):
        pieces = [
            lax.dynamic_slice(t.reshape(2, ways, low, columns), (near, which, 0, 0), (1, 1, low, columns))
            for t in (stay, come_pair)
        ]
        pieces.append(lax.dynamic_index_in_dim(come_near.reshape(ways, low, columns), which, 0))
        return total_of([p.reshape(low, columns) for p in pieces]).astype(LOW)

    leaving = [part(chosen ^ other) for other in range(1, ways)]
    leaving, omega_low = lax.optimization_barrier((leaving, omega_low))
    terms = [part(chosen)]
    for other, leave_part in enumerate(leaving, 1):
        jump = other << (high[0] + 1 - len(high[:2]))
        terms.append(lax.ppermute(leave_part, "dp", [(i, i ^ jump) for i in range(lax.axis_size("dp"))]))
    orders = scatter_orders()
    owners = [sorted(range(devices), key=lambda i: place_in(order, i)) for order in orders]
    piece_shape = (2, devices // 2, held_rows, width // 2)
    args = (tokens, norms, grad_middle, weights, omega_low, value, pk, core, keep, come)
    more = (uk, query_grad, key_part, value_part, query_weight, out_proj, norm_two_grad, turned)
    input_grad, leave, *stays = call(
        functools.partial(back_key_kernel, heads, size, (starts, rows, owners)),
        seqs,
        args + more,
        [spec(a) for a in args[:7]] + [in_smem, *states] + [spec(a) for a in more],
        [array(tokens.shape, F32), array(piece_shape, LOW)] + [array(piece_shape[1:], F32)] * 2,
        [per_seq(tokens.shape), fixed(piece_shape)] + [fixed(piece_shape[1:])] * 2,
        "back_key",
        7 * unit,
        chip=(),
        scratch=[
            pltpu.VMEM((3 * width, length), LOW),
            pltpu.VMEM((heads, ext, count), LOW),
            pltpu.VMEM(feat[1:], LOW),
            pltpu.VMEM((width, 2 * width), F32),
            pltpu.VMEM((2, width), F32),
            pltpu.VMEM((whole_rows, width), F32),
        ],
    )
    leave, terms = lax.optimization_barrier((leave, terms))
    come_pieces = flip(leave, "seq", 0)
    for step, bit in enumerate(high[2:]):
        omega_low, terms = split_rows(terms, "dp", [bit], dp_rows << (len(high) - 3 - step), omega_low)
    terms = [total_of(terms)]
    for bit in range(axis_bits("seq") - 1, 0, -1):
        terms = [t.reshape(t.shape[0], 2, -1) for t in terms]
        side = bit_of("seq", bit)
        sent = total_of([lax.dynamic_index_in_dim(t, 1 - side, 1, keepdims=False) for t in terms]).astype(LOW)
        kept = total_of([lax.dynamic_index_in_dim(t, side, 1, keepdims=False) for t in terms])
        terms = [kept, flip(sent, "seq", bit)]
    sums = []
    for index, (stay, order) in enumerate(zip(stays, orders)):
        part = [stay, come_pieces[index]]
        for step, (axis, bit) in enumerate(order[1:]):
            part = [t.reshape((2, t.shape[0] // 2) + t.shape[1:]) for t in part]
            if index == 0 and step == 2:
                part, terms = scatter_step(part, axis, bit, terms)
            else:
                part, _ = scatter_step(part, axis, bit)
        sums.append(total_of(part)[0])
    own_pair = total_of(terms)
    grad_first = own_pair[:, :group_width]
    grad_second = own_pair[:, group_width:].T
    att_grad = jnp.concatenate(sums, axis=1)
    att_grad = lax.dynamic_slice(att_grad.reshape(-1), (offset,), (shard_len,)).astype(F32)

    position = place * shard_len + jnp.arange(shard_len, dtype=jnp.int32)
    is_matrix = position < 4 * square
    rate = jnp.where(is_matrix, RATE_MATRIX, RATE_NORM)
    decay = jnp.where(is_matrix, WEIGHT_DECAY, 0.0)
    att_new, att_first_new, att_second_new = adamw(
        att_weights, att_first, att_second, att_grad, rate, decay
    )
    ffn_in_new, ffn_in_first_new, ffn_in_second_new = adamw(
        ffn_in, ffn_in_first, ffn_in_second, grad_first, RATE_MATRIX, WEIGHT_DECAY
    )
    ffn_out_new, ffn_out_first_new, ffn_out_second_new = adamw(
        ffn_out, ffn_out_first, ffn_out_second, grad_second, RATE_MATRIX, WEIGHT_DECAY
    )
    return (
        block_out,
        input_grad,
        att_new,
        att_first_new,
        att_second_new,
        att_new.astype(jnp.bfloat16),
        ffn_in_new,
        ffn_in_first_new,
        ffn_in_second_new,
        ffn_in_new.astype(jnp.bfloat16),
        ffn_out_new,
        ffn_out_first_new,
        ffn_out_second_new,
        ffn_out_new.astype(jnp.bfloat16),
    )


def solution(mesh):
    in_specs = (
        P("dp", "seq", None),
        P("dp", "seq", None),
        P("dp", "seq"),
        P(),
        P(("dp", "seq")),
        P(("dp", "seq")),
        P(("dp", "seq")),
        P("dp", "seq"),
        P("seq", "dp"),
        P("dp", "seq"),
        P("dp", "seq"),
        P("seq", "dp"),
        P("seq", "dp"),
    )
    out_specs = (
        P("dp", "seq", None),
        P("dp", "seq", None),
        P(("dp", "seq")),
        P(("dp", "seq")),
        P(("dp", "seq")),
        P(("dp", "seq")),
        P("dp", "seq"),
        P("dp", "seq"),
        P("dp", "seq"),
        P("dp", "seq"),
        P("seq", "dp"),
        P("seq", "dp"),
        P("seq", "dp"),
        P("seq", "dp"),
    )
    return jax.shard_map(shards, mesh=mesh, in_specs=in_specs, out_specs=out_specs, check_vma=False)
```
